128 devices in a mesh: row: 4 (over x_hi, core), col: 32 (over y, z, x_lo).
Axes of the slice: x: 4 (x_hi: 2, x_lo: 2; x = x_hi * 2 + x_lo), y: 4, z: 4, core: 2. Of those that a mesh axis runs over, the one named last changes fastest.
Arguments:
- force: bfloat16 [3, 256, 256, 512], P(None, 'col', 'row'), may hold values from -6 to 6
- mask: int32 [256, 256, 512], P('col', 'row'), may hold values from 0 to 1, as said below
- scalar: bfloat16 [256, 256, 512], P('col', 'row'), may hold values from -9 to 9
Outputs:
- velocity: bfloat16 [3, 256, 256, 512], P(None, 'col', 'row')
- concentration: bfloat16 [256, 256, 512], P('col', 'row')
The draws below stay inside these ranges and needn't reach their ends.
Inputs may be any that keep to these rules, and one draw needn't show every extreme that they name: `mask`: 1 marks a solid cell and 0 a fluid one.
All inputs are finite; a program needn't handle non-finite values.
Results may differ from the reference program's by a relative error of at most 0.029.
Values may be sent and summed in bfloat16 or wider, within the bound.
A program may use at most 64 MiB of HBM per device.

```python
import math
import jax
import jax.numpy as jnp
from jax import lax

NX = 512
NY = 256
NZ = 256
SECTIONS = 5


def draw_mask(key, part):
    key = jax.random.fold_in(key, 11)
    keys = jax.random.split(key, 3)
    period = max(NX // 4, 1)
    amplitude = NZ // 4
    phase = jax.random.randint(keys[0], (), 0, period)
    z_index = jnp.arange(NZ, dtype=jnp.int32)[:, None, None]
    x_index = jnp.arange(NX, dtype=jnp.int32)[None, None, :]
    winding = (x_index + phase) % period
    center = NZ // 2 + jnp.abs(2 * winding - period) * 2 * amplitude // period - amplitude
    widths = NZ // 4 + jax.random.randint(keys[1], (1, NY, NX), -2, 3)
    spacing = jnp.abs(z_index - center)
    spacing = jnp.minimum(spacing, NZ - spacing)
    posts = jax.random.randint(keys[2], (NZ, NY, NX), 0, 16) == 0
    solid_cells = (spacing > widths) | posts
    return solid_cells.astype(jnp.int32)


def levels(own_key, dims, pieces, low, largest):
    loudness, own = 1.0, jax.random.fold_in(own_key, 6)
    for axis_at, blocks in pieces:
        draws = jnp.exp(jax.random.uniform(jax.random.fold_in(own, axis_at), (blocks,), jnp.float32, low / len(pieces), largest / len(pieces)))
        loudness = loudness * jnp.repeat(draws, dims[axis_at] // blocks).reshape([-1 if axis == axis_at else 1 for axis in range(len(dims))])
    return loudness


def scatter_about(stream_key, dims, scale, reach, pieces=(), held_as=jnp.bfloat16):
    entries = scale * jax.random.normal(stream_key, dims, jnp.float32)
    if pieces:
        entries = entries * levels(stream_key, dims, pieces, -0.22, 0.18)
    return jnp.clip(entries, -reach, reach).astype(held_as)


def setup_inputs(seed: int = 0) -> dict:
    splits = jax.random.split(jax.random.key(seed), 4)
    return {
        "force": scatter_about(splits[0], (3, NZ, NY, NX), 1.0, 6.0, ((1, 32), (2, 4))),
        "mask": draw_mask(jax.random.fold_in(splits[3], 71), 0),
        "scalar": scatter_about(splits[2], (NZ, NY, NX), 1.5, 9.0, ((0, 32), (1, 4))),
    }


viscosity = 0.05
damping = 0.5
penalty = 1.0
time_step = 0.25
diffusivity = 0.25

def phases(rows_index, cols_index, length):
    product = rows_index[:, None] * cols_index[None, :] % length
    return product.astype(jnp.float32) * (2.0 * math.pi / length)

def square_tables(length):
    places = jnp.arange(length, dtype=jnp.int32)
    angles = phases(places, places, length)
    scaling = 1.0 / math.sqrt(length)
    return ((jnp.cos(angles) * scaling).astype(jnp.bfloat16), (jnp.sin(angles) * scaling).astype(jnp.bfloat16))

def wavenumber(index, length):
    signed = jnp.where(index < length // 2, index, index - length)
    return (signed.astype(jnp.float32) * (2.0 * math.pi / length), index == length // 2)

def project(vector_field, wave_vector, damping_gain, inverse_sq):
    along_wave = wave_vector[0] * vector_field[0] + wave_vector[1] * vector_field[1] + wave_vector[2] * vector_field[2]
    return damping_gain * (vector_field - wave_vector * (along_wave * inverse_sq))

def flux_term(center, lower_cell, upper_cell, speed):
    return diffusivity * (upper_cell + lower_cell - 2.0 * center) - (jnp.maximum(speed, 0.0) * (center - lower_cell) + jnp.minimum(speed, 0.0) * (upper_cell - center))

def pair_pass(real_part, imag_part, cosine, sine, pattern, orientation):
    highest = lax.Precision.HIGHEST
    real_wide = real_part.astype(jnp.float32)
    imag_wide = imag_part.astype(jnp.float32)
    cos_wide = cosine.astype(jnp.float32)
    sin_wide = sine.astype(jnp.float32)
    new_real = jnp.einsum(pattern, cos_wide, real_wide, precision=highest) + orientation * jnp.einsum(pattern, sin_wide, imag_wide, precision=highest)
    new_imag = jnp.einsum(pattern, cos_wide, imag_wide, precision=highest) - orientation * jnp.einsum(pattern, sin_wide, real_wide, precision=highest)
    return (new_real.astype(jnp.bfloat16), new_imag.astype(jnp.bfloat16))

def reference(force, mask, scalar):
    highest = lax.Precision.HIGHEST
    half_x = NX // 2
    places = jnp.arange(NX, dtype=jnp.int32)
    frequencies = jnp.arange(half_x, dtype=jnp.int32)
    scaling = 1.0 / math.sqrt(NX)
    angles = phases(places, frequencies, NX)
    x_cosine = (jnp.cos(angles) * scaling).astype(jnp.bfloat16).astype(jnp.float32)
    x_sine = (-(jnp.sin(angles) * scaling)).astype(jnp.bfloat16).astype(jnp.float32)
    weight = jnp.where(frequencies == 0, jnp.float32(1.0), jnp.float32(2.0))
    back_angles = phases(frequencies, places, NX)
    back_cosine = (weight[:, None] * jnp.cos(back_angles) * scaling).astype(jnp.bfloat16).astype(jnp.float32)
    back_sine = (-(weight[:, None] * jnp.sin(back_angles) * scaling)).astype(jnp.bfloat16).astype(jnp.float32)
    y_cosine, y_sine = square_tables(NY)
    z_cosine, z_sine = square_tables(NZ)
    wave_x, nyquist_x = wavenumber(frequencies, NX)
    wave_y, nyquist_y = wavenumber(jnp.arange(NY, dtype=jnp.int32), NY)
    wave_z, nyquist_z = wavenumber(jnp.arange(NZ, dtype=jnp.int32), NZ)
    wave_x = wave_x[None, None, :]
    wave_y = wave_y[None, :, None]
    wave_z = wave_z[:, None, None]
    shape_all = (NZ, NY, half_x)
    ksq = wave_x * wave_x + wave_y * wave_y + wave_z * wave_z
    nyquist = nyquist_x[None, None, :] | nyquist_y[None, :, None] | nyquist_z[:, None, None]
    damping_gain = jnp.where(nyquist, 0.0, 1.0 / (viscosity * ksq + damping)).astype(jnp.float32)
    inverse_sq = jnp.where(ksq > 0.0, 1.0 / jnp.where(ksq > 0.0, ksq, 1.0), 0.0).astype(jnp.float32)
    wave_vector = jnp.stack([jnp.broadcast_to(wave_x, shape_all), jnp.broadcast_to(wave_y, shape_all), jnp.broadcast_to(wave_z, shape_all)])

    def forward_one(component):
        values = component.astype(jnp.float32)
        real_part = jnp.dot(values, x_cosine, precision=highest).astype(jnp.bfloat16)
        imag_part = jnp.dot(values, x_sine, precision=highest).astype(jnp.bfloat16)
        real_part, imag_part = pair_pass(real_part, imag_part, y_cosine, y_sine, 'qy,zyk->zqk', 1.0)
        return pair_pass(real_part, imag_part, z_cosine, z_sine, 'qz,zyk->qyk', 1.0)

    def inverse_one(parts):
        real_part, imag_part = pair_pass(parts[0], parts[1], z_cosine, z_sine, 'qz,zyk->qyk', -1.0)
        real_part, imag_part = pair_pass(real_part, imag_part, y_cosine, y_sine, 'qy,zyk->zqk', -1.0)
        values = jnp.dot(real_part.astype(jnp.float32), back_cosine, precision=highest) + jnp.dot(imag_part.astype(jnp.float32), back_sine, precision=highest)
        return values.astype(jnp.bfloat16)
    force_real, force_imag = lax.map(forward_one, force)
    first_real = project(force_real.astype(jnp.float32), wave_vector, damping_gain, inverse_sq).astype(jnp.bfloat16)
    first_imag = project(force_imag.astype(jnp.float32), wave_vector, damping_gain, inverse_sq).astype(jnp.bfloat16)
    first_pass = lax.map(inverse_one, (first_real, first_imag))
    pushed = first_pass * mask.astype(jnp.bfloat16)[None]
    pushed_real, pushed_imag = lax.map(forward_one, pushed)
    second_real = (first_real.astype(jnp.float32) - penalty * project(pushed_real.astype(jnp.float32), wave_vector, damping_gain, inverse_sq)).astype(jnp.bfloat16)
    second_imag = (first_imag.astype(jnp.float32) - penalty * project(pushed_imag.astype(jnp.float32), wave_vector, damping_gain, inverse_sq)).astype(jnp.bfloat16)
    velocity = lax.map(inverse_one, (second_real, second_imag))
    speeds = velocity.astype(jnp.float32)
    fluid_cells = 1.0 - mask.astype(jnp.float32)
    scalar_state = scalar.astype(jnp.float32)
    for section_index in range(SECTIONS):
        summed = flux_term(scalar_state, jnp.roll(scalar_state, 1, 2), jnp.roll(scalar_state, -1, 2), speeds[0])
        summed = summed + flux_term(scalar_state, jnp.roll(scalar_state, 1, 1), jnp.roll(scalar_state, -1, 1), speeds[1])
        summed = summed + flux_term(scalar_state, jnp.roll(scalar_state, 1, 0), jnp.roll(scalar_state, -1, 0), speeds[2])
        scalar_state = scalar_state + time_step * fluid_cells * summed
    return (velocity, scalar_state.astype(jnp.bfloat16))
```

```python
import numpy as np
import jax
import jax.numpy as jnp
import ml_dtypes
from jax import lax
from jax.experimental import pallas as pl
from jax.experimental.pallas import tpu as pltpu
from jax.sharding import PartitionSpec as P

SECTIONS = 5
MESH = pl.DeviceIdType.MESH
BF = jnp.bfloat16
F32 = jnp.float32
TWO_PI = 2.0 * np.pi
PLANE_ORDER = (
    (1, 0), (3, 0), (0, 1), (0, 3), (1, 1), (3, 3), (1, 3), (3, 1),
    (2, 0), (0, 2), (2, 1), (1, 2), (2, 3), (3, 2), (2, 2),
)


def numpy_tables():
    def half(values):
        return values.astype(np.float32).astype(ml_dtypes.bfloat16)

    x = np.arange(512)
    h, ri, d, k = np.meshgrid(np.arange(2), np.arange(2), np.arange(8), np.arange(16), indexing="ij")
    m = (d * 32 + h * 16 + k).reshape(-1)
    ri = ri.reshape(-1)
    angle = (np.outer(x, m) % 512) * (TWO_PI / 512)
    fx = np.where(ri == 0, np.cos(angle), -np.sin(angle)) / np.sqrt(512.0)
    bx = (fx * np.where(m == 0, 1.0, 2.0)).T
    y = np.arange(256)
    angle = (np.outer(y, y) % 256) * (TWO_PI / 256)
    c, s = np.cos(angle) / 16.0, np.sin(angle) / 16.0
    real = np.concatenate([c, s], 1).reshape(16, 1, 16, 512)
    imag = np.concatenate([-s, c], 1).reshape(16, 1, 16, 512)
    ty = np.concatenate([real, imag], 1).reshape(512, 512)
    n = np.arange(16)
    angle = (np.outer(n, n) % 16) * (TWO_PI / 16)
    c, s = np.cos(angle) / 4.0, np.sin(angle) / 4.0
    cs = np.zeros((8, 256, 512))
    csi = np.zeros((8, 256, 512))
    tw = np.zeros((8, 2, 16, 256))
    k = np.arange(16)
    for d in range(8):
        for low in range(2):
            for p in range(8):
                zp = low * 8 + (p - d) % 8
                at = low * 128 + p * 16
                for k2 in range(16):
                    cs[d, at + k, k2 * 16 + k] = c[zp, k2]
                    cs[d, at + k, 256 + k2 * 16 + k] = s[zp, k2]
                    csi[d, k2 * 16 + k, at + k] = c[zp, k2]
                    csi[d, k2 * 16 + k, 256 + at + k] = s[zp, k2]
                tw[d, 0, :, at : at + 16] = np.cos(TWO_PI * zp * n / 256)[:, None] / 4.0
                tw[d, 1, :, at : at + 16] = np.sin(TWO_PI * zp * n / 256)[:, None] / 4.0
    return dict(
        fx=half(fx), bx=half(bx), ty=half(ty), tyi=half(ty.T), cs=half(cs), csi=half(csi),
        tw=tw.astype(np.float32),
    )


TABLES = ("fx", "ty", "tw", "cs", "csi", "tyi", "bx")
ROTATED = ("cs", "tw", "csi")


def radix4(a, sign):
    def add(u, v):
        return u[0] + v[0], u[1] + v[1]

    def sub(u, v):
        return u[0] - v[0], u[1] - v[1]

    t0, t1 = add(a[0], a[2]), sub(a[0], a[2])
    t2, t3 = add(a[1], a[3]), sub(a[1], a[3])
    t3 = (t3[1], -t3[0]) if sign > 0 else (-t3[1], t3[0])
    return add(t0, t2), add(t1, t3), sub(t0, t2), sub(t1, t3)


def turned_by(value, j, sign):
    if j == 0:
        return value
    c, s = float(np.cos(TWO_PI * j / 16)), float(np.sin(TWO_PI * j / 16)) * sign
    re, im = value
    return re * c + im * s, im * c - re * s


def merge(tiles, place):
    for bit in (1, 2, 4):
        take = (place & bit) != 0
        tiles = [jnp.where(take, tiles[(m + bit) % 8], tiles[m]) for m in range(8)]
    return tiles


def dot(a, b):
    return jnp.dot(a, b, preferred_element_type=F32)


def mixer_kernel(*refs):
    force_h, mask_h, scalar_h = refs[:3]
    count = len(TABLES)
    tables_h = dict(zip(TABLES, refs[3 : 3 + count]))
    velocity_h, conc_h = refs[3 + count : 5 + count]
    (field, mask, scalar, *rest) = refs[5 + count :]
    tab = dict(zip(TABLES, rest[:count]))
    (gain, inv, sa, ra, sb, rb, sbi, rbi, sai, rai, spec, first, second, lines, big, mid,
     zsend, zrecv, ysend, yrecv, coef, state, conc,
     in_sem, tab_sem, a_send, a_recv, b_send, b_recv, z_ssem, z_rsem, y_ssem, y_rsem, out_sem) = rest[count:]

    r = lax.axis_index("row")
    col = lax.axis_index("col")
    e = col // 2
    xl = col % 2
    d = xl * 4 + r

    def load(source, target, sem):
        copy = pltpu.make_async_copy(source, target, sem)
        copy.start()
        return copy

    def load_table(name):
        source = tables_h[name]
        sem = tab_sem.at[TABLES.index(name)]
        return load(source.at[d] if name in ROTATED else source, tab[name], sem)

    loads = {0: load(force_h.at[0], field.at[0], in_sem.at[0]), "fx": load_table("fx")}
    for i in (1, 2):
        loads[i] = load(force_h.at[i], field.at[i], in_sem.at[i])
    loads["scalar"] = load(scalar_h, scalar, in_sem.at[4])
    for name in TABLES[1:]:
        loads[name] = load_table(name)
    loads["mask"] = load(mask_h, mask, in_sem.at[3])

    core = r & 1
    x = (r // 2) * 2 + xl
    y_at, z_at = e // 4, e & 3

    def x_peer(step, of_core):
        at = (x + step * (1 + 2 * core)) & 3
        low = at & 1
        row = (at - low) + of_core
        return low * 4 + row, (row, e * 2 + low)

    def plane_peer(dy, dz):
        to = ((y_at + dy + core * (3 * dz - dy)) & 3) * 4 + ((z_at + dz + core * (3 * dy - dz)) & 3)
        return to, (r, to * 2 + xl)

    x_peers = [
        x_peer(step, core if same else 1 - core)
        for step, same in ((1, 1), (3, 1), (1, 0), (3, 0), (2, 1), (2, 0), (0, 0))
    ]
    plane_peers = [plane_peer(dy, dz) for dy, dz in PLANE_ORDER]

    z_up = (r, lax.rem(col + 1, 32))
    z_down = (r, lax.rem(col + 31, 32))
    y_up = (lax.rem(r + 1, 4), col)
    y_down = (lax.rem(r + 3, 4), col)

    barrier = pltpu.get_barrier_semaphore()

    for _, device in x_peers + plane_peers:
        pl.semaphore_signal(barrier, inc=1, device_id=device, device_id_type=MESH)
    across = (r, lax.rem(col + 31 + 2 * xl, 32))
    pl.semaphore_signal(barrier, inc=1, device_id=across, device_id_type=MESH)
    pl.semaphore_wait(barrier, 23)

    def remote(source, target, ssem, rsem, device):
        return pltpu.make_async_remote_copy(
            src_ref=source, dst_ref=target, send_sem=ssem, recv_sem=rsem,
            device_id=device, device_id_type=MESH)

    my_rows = pl.ds(pl.multiple_of(r * 64, 64), 64)
    my_lanes = pl.ds(pl.multiple_of(xl * 128, 128), 128)
    my_slab = pl.ds(pl.multiple_of(e * 32, 32), 32)

    def send_a(t, i):
        target = ra.at[t, i, :, my_rows, my_lanes]
        recv = a_recv.at[2 * t, i]

        for to, device in x_peers:
            remote(sa.at[i, to], target, a_send.at[2 * t, i], recv, device).start()
        pltpu.make_async_copy(sa.at[i, d], target, recv).start()

    def send_ai(t, i):
        target = rai.at[t, i, d]
        recv = a_recv.at[2 * t + 1, i]

        def piece(to):
            rows = pl.ds(pl.multiple_of((to & 3) * 64, 64), 64)
            lanes = pl.ds(pl.multiple_of((to // 4) * 128, 128), 128)
            return sai.at[i, :, rows, lanes]

        for to, device in x_peers:
            remote(piece(to), target, a_send.at[2 * t + 1, i], recv, device).start()
        pltpu.make_async_copy(piece(d), target, recv).start()

    def send_b(source, into, k, t, i):
        target = into.at[t, i, my_slab]
        recv = b_recv.at[k, i]

        for to, device in plane_peers:
            slab = source.at[i, pl.ds(pl.multiple_of(to * 32, 32), 32)]
            remote(slab, target, b_send.at[k, i], recv, device).start()
        pltpu.make_async_copy(source.at[i, my_slab], target, recv).start()

    def arrived(buffer, sem):
        pltpu.make_async_copy(buffer, buffer, sem).wait()

    def sent_a(k, i):
        part = sa.at[i, pl.ds(0, 7)]
        pltpu.make_async_copy(part, part, a_send.at[k, i]).wait()

    def sent_b(k, i):
        part = sb.at[i, pl.ds(0, 480)]
        pltpu.make_async_copy(part, part, b_send.at[k, i]).wait()

    def send_z(s, q):
        rows = pl.ds(16 * q, 16)
        for side, device in ((0, z_down), (1, z_up)):
            remote(zsend.at[s, side, rows], zrecv.at[s, 1 - side, rows],
                   z_ssem.at[s, side], z_rsem.at[s, 1 - side, q], device).start()

    def send_y(s, side):
        remote(ysend.at[s, side], yrecv.at[s, 1 - side], y_ssem.at[s, side], y_rsem.at[s, 1 - side],
               (y_down, y_up)[side]).start()

    place = lax.broadcasted_iota(jnp.int32, (64, 128), 1) // 16

    def x_forward(t, c):
        spread = dot(field[c].reshape(512, 512), tab["fx"][...])
        for j in range(4):
            tiles = []
            for z in range(8):
                tile = spread[z * 64 : z * 64 + 64, j * 128 : j * 128 + 128]
                tiles.append(pltpu.roll(tile, 16 * z, 1) if z else tile)
            tiles = merge(tiles, place)
            for to in range(8):
                sa[3 * (j // 2) + c, to, j % 2] = tiles[-to % 8].astype(BF)
        send_a(t, c)

    def x_inverse(t, c):
        for j in range(4):
            tiles = [rai[t, 3 * (j // 2) + c, source, j % 2].astype(F32) for source in range(8)]
            tiles = merge(tiles, place)
            for z in range(8):
                tile = tiles[-z % 8]
                tile = pltpu.roll(tile, 128 - 16 * z, 1) if z else tile
                lines[z * 64 : z * 64 + 64, j * 128 : j * 128 + 128] = tile.astype(BF)
        values = dot(lines[...], tab["bx"][...]).astype(BF).reshape(8, 64, 512)
        if t == 0:
            values = (values.astype(F32) * mask[...].astype(F32)).astype(BF)
        field[c] = values

    def y_forward(t, i):
        arrived(ra.at[t, i], a_recv.at[2 * t, i])
        sb[i] = dot(tab["ty"][...], ra[t, i].reshape(512, 256)).astype(BF)
        send_b(sb, rb, 2 * t, t, i)

    def y_inverse(t, i):
        arrived(rbi.at[t, i], b_recv.at[2 * t + 1, i])
        sai[i] = dot(tab["tyi"][...], rbi[t, i]).astype(BF).reshape(2, 256, 256)
        send_ai(t, i)

    def z_forward(t, i):
        arrived(rb.at[t, i], b_recv.at[2 * t, i])
        for half in range(2):
            lanes = slice(half * 128, half * 128 + 128)

            def source(e_from, ri):
                return rb[t, i, e_from * 32 + ri * 16 : e_from * 32 + ri * 16 + 16, lanes].astype(F32)

            for low in range(4):
                out = radix4([(source(low + 4 * j, 0), source(low + 4 * j, 1)) for j in range(4)], 1)
                for k, value in enumerate(out):
                    mid[low, k, 0, :, lanes], mid[low, k, 1, :, lanes] = turned_by(value, low * k, 1)
            for k in range(4):
                out = radix4([(mid[low, k, 0, :, lanes], mid[low, k, 1, :, lanes]) for low in range(4)], 1)
                for high, (re, im) in enumerate(out):
                    k1 = k + 4 * high
                    wc, ws = tab["tw"][0, k1 : k1 + 1, lanes], tab["tw"][1, k1 : k1 + 1, lanes]
                    big[k1 * 16 : k1 * 16 + 16, lanes] = (re * wc + im * ws).astype(BF)
                    big[256 + k1 * 16 : 256 + k1 * 16 + 16, lanes] = (im * wc - re * ws).astype(BF)
        both = dot(big[...], tab["cs"][...])
        spec[i, 0] = both[:256, :256] + both[256:, 256:]
        spec[i, 1] = both[256:, :256] - both[:256, 256:]

    def z_inverse(source, t, i):
        both = dot(source[i].reshape(512, 256), tab["csi"][...])
        for half in range(2):
            lanes = slice(half * 128, half * 128 + 128)
            other = slice(256 + half * 128, 256 + half * 128 + 128)

            def value(k1):
                upper, lower = slice(k1 * 16, k1 * 16 + 16), slice(256 + k1 * 16, 256 + k1 * 16 + 16)
                re = both[upper, lanes] - both[lower, other]
                im = both[lower, lanes] + both[upper, other]
                wc, ws = tab["tw"][0, k1 : k1 + 1, lanes], tab["tw"][1, k1 : k1 + 1, lanes]
                return re * wc - im * ws, im * wc + re * ws

            for low in range(4):
                out = radix4([value(low + 4 * j) for j in range(4)], -1)
                for k, turned in enumerate(out):
                    mid[low, k, 0, :, lanes], mid[low, k, 1, :, lanes] = turned_by(turned, low * k, -1)
            for k in range(4):
                out = radix4([(mid[low, k, 0, :, lanes], mid[low, k, 1, :, lanes]) for low in range(4)], -1)
                for high, (re, im) in enumerate(out):
                    to = (k + 4 * high) * 32
                    sbi[i, to : to + 16, lanes] = re.astype(BF)
                    sbi[i, to + 16 : to + 32, lanes] = im.astype(BF)
        send_b(sbi, rbi, 2 * t + 1, t, i)

    lane = lax.broadcasted_iota(jnp.int32, (16, 256), 1)
    unit_long, unit = np.float32(TWO_PI / 512), np.float32(TWO_PI / 256)
    index_y = e * 16 + lax.broadcasted_iota(jnp.int32, (16, 256), 0)
    wave_y = jnp.where(index_y < 128, index_y, index_y - 256).astype(F32) * unit

    def along_x(h):
        return (d * 32 + h * 16 + (lane & 15)).astype(F32) * unit_long

    def along_z(k1):
        index_z = k1 + 16 * (lane // 16)
        return index_z, jnp.where(index_z < 128, index_z, index_z - 256).astype(F32) * unit

    def factors(step, _):
        h, k1 = step // 16, step & 15
        wave_x = along_x(h)
        index_z, wave_z = along_z(k1)
        ksq = wave_x * wave_x + wave_y * wave_y + wave_z * wave_z
        edge = (index_y == 128) | (index_z == 128)
        rows = pl.ds(pl.multiple_of(k1 * 16, 16), 16)
        gain[h, rows] = jnp.where(edge, 0.0, 1.0 / (0.05 * ksq + 0.5))
        inv[h, rows] = jnp.where(ksq > 0.0, 1.0 / jnp.where(ksq > 0.0, ksq, 1.0), 0.0)
        return _

    def project(t, h):
        wave_x = along_x(h)

        def one(k1, _):
            wave_z = along_z(k1)[1]
            rows = pl.ds(pl.multiple_of(k1 * 16, 16), 16)
            g, n = gain[h, rows], inv[h, rows]
            for ri in range(2):
                w = [spec[3 * h + c, ri, rows] for c in range(3)]
                along = (wave_x * w[0] + wave_y * w[1] + wave_z * w[2]) * n
                for c, wave in enumerate((wave_x, wave_y, wave_z)):
                    value = g * (w[c] - wave * along)
                    if t == 0:
                        first[3 * h + c, ri, rows] = value.astype(BF)
                    else:
                        second[3 * h + c, ri, rows] = (first[3 * h + c, ri, rows].astype(F32) - value).astype(BF)
            return _

        lax.fori_loop(0, 16, one, 0)

    def each(count, step):
        def body(i, _):
            step(i)
            return _

        lax.fori_loop(0, count, body, 0)

    def spectral(t, source):
        def step(n):
            @pl.when(n < 6)
            def _():
                y_forward(t, n)

            @pl.when(((n >= 1) & (n <= 3)) | ((n >= 6) & (n <= 8)))
            def _():
                z_forward(t, jnp.where(n <= 3, n - 1, n - 3))

            @pl.when((n == 3) | (n == 8))
            def _():
                project(t, jnp.where(n == 3, 0, 1))

            @pl.when((n == 3) | (n == 5) | (n == 6) | ((n >= 8) & (n <= 10)))
            def _():
                z_inverse(source, t, jnp.where(n == 3, 0, jnp.where(n <= 6, n - 4, n - 5)))

            @pl.when((n == 5) | (n >= 8))
            def _():
                y_inverse(t, jnp.where(n == 5, 0, n - 7))

        each(13, step)

    loads["fx"].wait()
    for i in range(3):
        loads[i].wait()
    each(3, lambda c: x_forward(0, c))
    each(3, lambda c: send_a(0, c + 3))
    lax.fori_loop(0, 32, factors, 0)
    loads["scalar"].wait()
    for z in range(8):
        state[0, z + 1, pl.ds(8, 64), :] = scalar[z].astype(F32)
        ysend[0, 0, pl.ds(z, 1), :] = state[0, z + 1, pl.ds(8, 1), :]
        ysend[0, 1, pl.ds(z, 1), :] = state[0, z + 1, pl.ds(71, 1), :]
    zsend[0, 0] = scalar[0]
    zsend[0, 1] = scalar[7]
    for q in range(4):
        send_z(0, q)
    for side in range(2):
        send_y(0, side)
    for name in TABLES[1:]:
        loads[name].wait()
    loads["mask"].wait()
    spectral(0, first)

    def back_in_x(t, c):
        for i in (c, c + 3):
            arrived(rai.at[t, i], a_recv.at[2 * t + 1, i])
        x_inverse(t, c)

    def sent(t, c):
        for i in (c, c + 3):
            sent_b(2 * t, i)
            sent_b(2 * t + 1, i)
            sent_a(2 * t + 1, i)

    def middle(c):
        back_in_x(0, c)
        for i in (c, c + 3):
            sent_a(0, i)
        x_forward(1, c)
        sent(0, c)

    each(3, middle)
    each(3, lambda c: send_a(1, c + 3))
    spectral(1, second)

    def coefficients(z, c):
        fluid = 0.25 * (1.0 - mask[z].astype(F32))
        u = field[c, z].astype(F32)
        below = fluid * (0.25 + jnp.maximum(u, 0.0))
        above = fluid * (0.25 - jnp.minimum(u, 0.0))
        coef[2 * c, z] = below
        coef[2 * c + 1, z] = above
        start = jnp.where(c == 0, jnp.ones_like(u), coef[6, z])
        coef[6, z] = start - (below + above)
        return c

    def last(c):
        back_in_x(1, c)
        pltpu.make_async_copy(field.at[c], velocity_h.at[c], out_sem.at[c]).start()
        lax.fori_loop(0, 8, coefficients, c)
        for i in (c, c + 3):
            sent_a(2, i)
        sent(1, c)

    each(3, last)

    def section(s, carry):
        now, later = s & 1, (s + 1) & 1

        def block(z, q, below_z, above_z):
            at = 8 + 16 * q
            rows, cells = pl.ds(at, 16), pl.ds(16 * q, 16)
            center = state[now, z, rows]
            new = coef[6, z - 1, cells] * center
            new = new + coef[0, z - 1, cells] * pltpu.roll(center, 1, 1)
            new = new + coef[1, z - 1, cells] * pltpu.roll(center, 511, 1)
            new = new + coef[2, z - 1, cells] * state[now, z, pl.ds(at - 1, 16)]
            new = new + coef[3, z - 1, cells] * state[now, z, pl.ds(at + 1, 16)]
            new = new + coef[4, z - 1, cells] * below_z + coef[5, z - 1, cells] * above_z
            state[later, z, rows] = new
            return new

        for q in (1, 2, 0, 3):
            rows, cells = pl.ds(8 + 16 * q, 16), pl.ds(16 * q, 16)
            if q in (0, 3):
                side = q // 3
                arrived(yrecv.at[s, side], y_rsem.at[s, side])
                for z in range(8):
                    state[now, z + 1, pl.ds(7 + 65 * side, 1), :] = yrecv[s, side, pl.ds(z, 1), :]
            for side in range(2):
                arrived(zrecv.at[s, side, cells], z_rsem.at[s, side, q])
            bottom = block(1, q, zrecv[s, 0, cells].astype(F32), state[now, 2, rows])
            top = block(8, q, state[now, 7, rows], zrecv[s, 1, cells].astype(F32))

            @pl.when(s < SECTIONS - 1)
            def _():
                zsend[s + 1, 0, cells] = bottom.astype(BF)
                zsend[s + 1, 1, cells] = top.astype(BF)
                send_z(s + 1, q)

            def inner(z, _):
                block(z, q, state[now, z - 1, rows], state[now, z + 1, rows])
                return _

            lax.fori_loop(2, 8, inner, 0)
            if q in (0, 3):
                side = q // 3

                @pl.when(s < SECTIONS - 1)
                def _():
                    for z in range(8):
                        ysend[s + 1, side, pl.ds(z, 1), :] = state[later, z + 1, pl.ds(8 + 63 * side, 1), :]
                    send_y(s + 1, side)
        return carry

    lax.fori_loop(0, SECTIONS, section, 0)
    for z in range(8):
        conc[z] = state[SECTIONS % 2, z + 1, pl.ds(8, 64), :].astype(BF)

    for s in range(SECTIONS):
        for i in range(2):
            arrived(zsend.at[s, i], z_ssem.at[s, i])
            arrived(ysend.at[s, i], y_ssem.at[s, i])
    out = pltpu.make_async_copy(conc, conc_h, out_sem.at[3])
    out.start()
    for c in range(3):
        pltpu.make_async_copy(field.at[c], velocity_h.at[c], out_sem.at[c]).wait()
    out.wait()


def local(force, mask, scalar):
    tables = numpy_tables()
    vm = pltpu.VMEM
    dma = pltpu.SemaphoreType.DMA
    scratch = [vm((3, 8, 64, 512), BF), vm((8, 64, 512), jnp.int32), vm((8, 64, 512), BF)]
    for name in TABLES:
        value = tables[name]
        shape = value.shape[1:] if name in ROTATED else value.shape
        scratch.append(vm(shape, value.dtype))
    scratch += [
        vm((2, 256, 256), F32), vm((2, 256, 256), F32),
        vm((6, 8, 2, 64, 128), BF), vm((2, 6, 2, 256, 256), BF),
        vm((6, 512, 256), BF), vm((2, 6, 512, 256), BF),
        vm((6, 512, 256), BF), vm((2, 6, 512, 256), BF),
        vm((6, 2, 256, 256), BF), vm((2, 6, 8, 2, 64, 128), BF),
        vm((6, 2, 256, 256), F32), vm((6, 2, 256, 256), BF), vm((6, 2, 256, 256), BF),
        vm((512, 512), BF), vm((512, 256), BF), vm((4, 4, 2, 16, 256), F32),
        vm((SECTIONS, 2, 64, 512), BF), vm((SECTIONS, 2, 64, 512), BF),
        vm((SECTIONS, 2, 8, 512), F32), vm((SECTIONS, 2, 8, 512), F32),
        vm((7, 8, 64, 512), F32), vm((2, 10, 80, 512), F32), vm((8, 64, 512), BF),
        dma((5,)), dma((len(TABLES),)),
        dma((4, 6)), dma((4, 6)), dma((4, 6)), dma((4, 6)),
        dma((SECTIONS, 2)), dma((SECTIONS, 2, 4)), dma((SECTIONS, 2)), dma((SECTIONS, 2)),
        dma((4,)),
    ]
    any_spec = pl.BlockSpec(memory_space=pl.ANY)
    velocity, conc = pl.pallas_call(
        mixer_kernel,
        out_shape=(
            jax.ShapeDtypeStruct((3, 8, 64, 512), BF),
            jax.ShapeDtypeStruct((8, 64, 512), BF),
        ),
        in_specs=[any_spec] * (3 + len(TABLES)),
        out_specs=(any_spec, any_spec),
        scratch_shapes=scratch,
        compiler_params=pltpu.CompilerParams(
            collective_id=0, has_side_effects=True, vmem_limit_bytes=62 * 1024 * 1024
        ),
        name="mixer",
    )(
        force,
        mask,
        scalar,
        *[jnp.asarray(tables[name]) for name in TABLES],
    )
    return velocity, conc


def solution(mesh):
    placed = (P(None, "col", "row", None), P("col", "row", None), P("col", "row", None))
    return jax.shard_map(
        local,
        mesh=mesh,
        in_specs=placed,
        out_specs=(P(None, "col", "row", None), P("col", "row", None)),
        check_vma=False,
    )
```

```python
import numpy as np
import jax
import jax.numpy as jnp
import ml_dtypes
from jax import lax
from jax.experimental import pallas as pl
from jax.experimental.pallas import tpu as pltpu
from jax.sharding import PartitionSpec as P

SECTIONS = 5
MESH = pl.DeviceIdType.MESH
BF = jnp.bfloat16
F32 = jnp.float32
TWO_PI = 2.0 * np.pi
PLANE_ORDER = (
    (1, 0), (3, 0), (0, 1), (0, 3), (1, 1), (3, 3), (1, 3), (3, 1),
    (2, 0), (0, 2), (2, 1), (1, 2), (2, 3), (3, 2), (2, 2),
)


def numpy_tables():
    def half(values):
        return values.astype(np.float32).astype(ml_dtypes.bfloat16)

    x = np.arange(512)
    h, ri, d, k = np.meshgrid(np.arange(2), np.arange(2), np.arange(8), np.arange(16), indexing="ij")
    m = (d * 32 + h * 16 + k).reshape(-1)
    ri = ri.reshape(-1)
    angle = (np.outer(x, m) % 512) * (TWO_PI / 512)
    fx = np.where(ri == 0, np.cos(angle), -np.sin(angle)) / np.sqrt(512.0)
    bx = (fx * np.where(m == 0, 1.0, 2.0)).T
    y = np.arange(256)
    angle = (np.outer(y, y) % 256) * (TWO_PI / 256)
    c, s = np.cos(angle) / 16.0, np.sin(angle) / 16.0
    real = np.concatenate([c, s], 1).reshape(16, 1, 16, 512)
    imag = np.concatenate([-s, c], 1).reshape(16, 1, 16, 512)
    ty = np.concatenate([real, imag], 1).reshape(512, 512)
    n = np.arange(16)
    angle = (np.outer(n, n) % 16) * (TWO_PI / 16)
    c, s = np.cos(angle) / 4.0, np.sin(angle) / 4.0
    cs = np.zeros((8, 256, 512))
    csi = np.zeros((8, 256, 512))
    tw = np.zeros((8, 2, 16, 256))
    k = np.arange(16)
    for d in range(8):
        for low in range(2):
            for p in range(8):
                zp = low * 8 + (p - d) % 8
                at = low * 128 + p * 16
                for k2 in range(16):
                    cs[d, at + k, k2 * 16 + k] = c[zp, k2]
                    cs[d, at + k, 256 + k2 * 16 + k] = s[zp, k2]
                    csi[d, k2 * 16 + k, at + k] = c[zp, k2]
                    csi[d, k2 * 16 + k, 256 + at + k] = s[zp, k2]
                tw[d, 0, :, at : at + 16] = np.cos(TWO_PI * zp * n / 256)[:, None] / 4.0
                tw[d, 1, :, at : at + 16] = np.sin(TWO_PI * zp * n / 256)[:, None] / 4.0
    return dict(
        fx=half(fx), bx=half(bx), ty=half(ty), tyi=half(ty.T), cs=half(cs), csi=half(csi),
        tw=tw.astype(np.float32),
    )


TABLES = ("fx", "ty", "tw", "cs", "csi", "tyi", "bx")
ROTATED = ("cs", "tw", "csi")


def radix4(a, sign):
    def add(u, v):
        return u[0] + v[0], u[1] + v[1]

    def sub(u, v):
        return u[0] - v[0], u[1] - v[1]

    t0, t1 = add(a[0], a[2]), sub(a[0], a[2])
    t2, t3 = add(a[1], a[3]), sub(a[1], a[3])
    t3 = (t3[1], -t3[0]) if sign > 0 else (-t3[1], t3[0])
    return add(t0, t2), add(t1, t3), sub(t0, t2), sub(t1, t3)


def turned_by(value, j, sign):
    if j == 0:
        return value
    c, s = float(np.cos(TWO_PI * j / 16)), float(np.sin(TWO_PI * j / 16)) * sign
    re, im = value
    return re * c + im * s, im * c - re * s


def merge(tiles, place):
    for bit in (1, 2, 4):
        take = (place & bit) != 0
        tiles = [jnp.where(take, tiles[(m + bit) % 8], tiles[m]) for m in range(8)]
    return tiles


def dot(a, b):
    return jnp.dot(a, b, preferred_element_type=F32)


def mixer_kernel(*refs):
    force_h, mask_h, scalar_h = refs[:3]
    count = len(TABLES)
    tables_h = dict(zip(TABLES, refs[3 : 3 + count]))
    velocity_h, conc_h = refs[3 + count : 5 + count]
    (field, mask, scalar, *rest) = refs[5 + count :]
    tab = dict(zip(TABLES, rest[:count]))
    (gain, inv, sa, ra, sb, rb, sbi, rbi, sai, rai, spec, first, second, lines, big, mid,
     zsend, zrecv, ysend, yrecv, coef, state, conc,
     in_sem, tab_sem, a_send, a_recv, b_send, b_recv, z_ssem, z_rsem, y_ssem, y_rsem, out_sem) = rest[count:]

    r = lax.axis_index("row")
    col = lax.axis_index("col")
    e = col // 2
    xl = col % 2
    d = xl * 4 + r

    def load(source, target, sem):
        copy = pltpu.make_async_copy(source, target, sem)
        copy.start()
        return copy

    def load_table(name):
        source = tables_h[name]
        sem = tab_sem.at[TABLES.index(name)]
        return load(source.at[d] if name in ROTATED else source, tab[name], sem)

    loads = {0: load(force_h.at[0], field.at[0], in_sem.at[0]), "fx": load_table("fx")}
    for i in (1, 2):
        loads[i] = load(force_h.at[i], field.at[i], in_sem.at[i])
    loads["scalar"] = load(scalar_h, scalar, in_sem.at[4])
    for name in TABLES[1:]:
        loads[name] = load_table(name)
    loads["mask"] = load(mask_h, mask, in_sem.at[3])

    core = r & 1
    x = (r // 2) * 2 + xl
    y_at, z_at = e // 4, e & 3

    def x_peer(step, of_core):
        at = (x + step * (1 + 2 * core)) & 3
        low = at & 1
        row = (at - low) + of_core
        return low * 4 + row, (row, e * 2 + low)

    def plane_peer(dy, dz):
        to = ((y_at + dy + core * (3 * dz - dy)) & 3) * 4 + ((z_at + dz + core * (3 * dy - dz)) & 3)
        return to, (r, to * 2 + xl)

    x_peers = [
        x_peer(step, core if same else 1 - core)
        for step, same in ((1, 1), (3, 1), (1, 0), (3, 0), (2, 1), (2, 0), (0, 0))
    ]
    plane_peers = [plane_peer(dy, dz) for dy, dz in PLANE_ORDER]

    z_up = (r, lax.rem(col + 1, 32))
    z_down = (r, lax.rem(col + 31, 32))
    y_up = (lax.rem(r + 1, 4), col)
    y_down = (lax.rem(r + 3, 4), col)

    barrier = pltpu.get_barrier_semaphore()

    for _, device in x_peers + plane_peers:
        pl.semaphore_signal(barrier, inc=1, device_id=device, device_id_type=MESH)
    across = (r, lax.rem(col + 31 + 2 * xl, 32))
    pl.semaphore_signal(barrier, inc=1, device_id=across, device_id_type=MESH)
    pl.semaphore_wait(barrier, 23)

    def remote(source, target, ssem, rsem, device):
        return pltpu.make_async_remote_copy(
            src_ref=source, dst_ref=target, send_sem=ssem, recv_sem=rsem,
            device_id=device, device_id_type=MESH)

    my_rows = pl.ds(pl.multiple_of(r * 64, 64), 64)
    my_lanes = pl.ds(pl.multiple_of(xl * 128, 128), 128)
    my_slab = pl.ds(pl.multiple_of(e * 32, 32), 32)

    def send_a(t, i):
        target = ra.at[t, i, :, my_rows, my_lanes]
        recv = a_recv.at[2 * t, i]

        for to, device in x_peers:
            remote(sa.at[i, to], target, a_send.at[2 * t, i], recv, device).start()
        pltpu.make_async_copy(sa.at[i, d], target, recv).start()

    def send_ai(t, i):
        target = rai.at[t, i, d]
        recv = a_recv.at[2 * t + 1, i]

        def piece(to):
            rows = pl.ds(pl.multiple_of((to & 3) * 64, 64), 64)
            lanes = pl.ds(pl.multiple_of((to // 4) * 128, 128), 128)
            return sai.at[i, :, rows, lanes]

        for to, device in x_peers:
            remote(piece(to), target, a_send.at[2 * t + 1, i], recv, device).start()
        pltpu.make_async_copy(piece(d), target, recv).start()

    def send_b(source, into, k, t, i):
        target = into.at[t, i, my_slab]
        recv = b_recv.at[k, i]

        for to, device in plane_peers:
            slab = source.at[i, pl.ds(pl.multiple_of(to * 32, 32), 32)]
            remote(slab, target, b_send.at[k, i], recv, device).start()
        pltpu.make_async_copy(source.at[i, my_slab], target, recv).start()

    def arrived(buffer, sem):
        pltpu.make_async_copy(buffer, buffer, sem).wait()

    def sent_a(k, i):
        part = sa.at[i, pl.ds(0, 7)]
        pltpu.make_async_copy(part, part, a_send.at[k, i]).wait()

    def sent_b(k, i):
        part = sb.at[i, pl.ds(0, 480)]
        pltpu.make_async_copy(part, part, b_send.at[k, i]).wait()

    def send_z(s, q):
        rows = pl.ds(16 * q, 16)
        for side, device in ((0, z_down), (1, z_up)):
            remote(zsend.at[s, side, rows], zrecv.at[s, 1 - side, rows],
                   z_ssem.at[s, side], z_rsem.at[s, 1 - side, q], device).start()

    def send_y(s, side):
        remote(ysend.at[s, side], yrecv.at[s, 1 - side], y_ssem.at[s, side], y_rsem.at[s, 1 - side],
               (y_down, y_up)[side]).start()

    place = lax.broadcasted_iota(jnp.int32, (64, 128), 1) // 16

    def x_forward(t, c, h):
        spread = dot(field[c].reshape(512, 512), tab["fx"][:, h * 256 : h * 256 + 256])
        for ri in range(2):
            tiles = []
            for z in range(8):
                tile = spread[z * 64 : z * 64 + 64, ri * 128 : ri * 128 + 128]
                tiles.append(pltpu.roll(tile, 16 * z, 1) if z else tile)
            tiles = merge(tiles, place)
            for to in range(8):
                sa[3 * h + c, to, ri] = tiles[-to % 8].astype(BF)
        send_a(t, 3 * h + c)

    def x_inverse(t, c):
        for j in range(4):
            tiles = [rai[t, 3 * (j // 2) + c, source, j % 2].astype(F32) for source in range(8)]
            tiles = merge(tiles, place)
            for z in range(8):
                tile = tiles[-z % 8]
                tile = pltpu.roll(tile, 128 - 16 * z, 1) if z else tile
                lines[z * 64 : z * 64 + 64, j * 128 : j * 128 + 128] = tile.astype(BF)
        values = dot(lines[...], tab["bx"][...]).astype(BF).reshape(8, 64, 512)
        if t == 0:
            values = (values.astype(F32) * mask[...].astype(F32)).astype(BF)
        field[c] = values

    def y_forward(t, i):
        arrived(ra.at[t, i], a_recv.at[2 * t, i])
        sb[i] = dot(tab["ty"][...], ra[t, i].reshape(512, 256)).astype(BF)
        send_b(sb, rb, 2 * t, t, i)

    def y_inverse(t, i):
        arrived(rbi.at[t, i], b_recv.at[2 * t + 1, i])
        sai[i] = dot(tab["tyi"][...], rbi[t, i]).astype(BF).reshape(2, 256, 256)
        send_ai(t, i)

    def z_forward(t, i):
        arrived(rb.at[t, i], b_recv.at[2 * t, i])
        for half in range(2):
            lanes = slice(half * 128, half * 128 + 128)

            def source(e_from, ri):
                return rb[t, i, e_from * 32 + ri * 16 : e_from * 32 + ri * 16 + 16, lanes].astype(F32)

            for low in range(4):
                out = radix4([(source(low + 4 * j, 0), source(low + 4 * j, 1)) for j in range(4)], 1)
                for k, value in enumerate(out):
                    mid[low, k, 0, :, lanes], mid[low, k, 1, :, lanes] = turned_by(value, low * k, 1)
            for k in range(4):
                out = radix4([(mid[low, k, 0, :, lanes], mid[low, k, 1, :, lanes]) for low in range(4)], 1)
                for high, (re, im) in enumerate(out):
                    k1 = k + 4 * high
                    wc, ws = tab["tw"][0, k1 : k1 + 1, lanes], tab["tw"][1, k1 : k1 + 1, lanes]
                    big[k1 * 16 : k1 * 16 + 16, lanes] = (re * wc + im * ws).astype(BF)
                    big[256 + k1 * 16 : 256 + k1 * 16 + 16, lanes] = (im * wc - re * ws).astype(BF)
        both = dot(big[...], tab["cs"][...])
        spec[i, 0] = both[:256, :256] + both[256:, 256:]
        spec[i, 1] = both[256:, :256] - both[:256, 256:]

    def z_inverse(source, t, i):
        both = dot(source[i].reshape(512, 256), tab["csi"][...])
        for half in range(2):
            lanes = slice(half * 128, half * 128 + 128)
            other = slice(256 + half * 128, 256 + half * 128 + 128)

            def value(k1):
                upper, lower = slice(k1 * 16, k1 * 16 + 16), slice(256 + k1 * 16, 256 + k1 * 16 + 16)
                re = both[upper, lanes] - both[lower, other]
                im = both[lower, lanes] + both[upper, other]
                wc, ws = tab["tw"][0, k1 : k1 + 1, lanes], tab["tw"][1, k1 : k1 + 1, lanes]
                return re * wc - im * ws, im * wc + re * ws

            for low in range(4):
                out = radix4([value(low + 4 * j) for j in range(4)], -1)
                for k, turned in enumerate(out):
                    mid[low, k, 0, :, lanes], mid[low, k, 1, :, lanes] = turned_by(turned, low * k, -1)
            for k in range(4):
                out = radix4([(mid[low, k, 0, :, lanes], mid[low, k, 1, :, lanes]) for low in range(4)], -1)
                for high, (re, im) in enumerate(out):
                    to = (k + 4 * high) * 32
                    sbi[i, to : to + 16, lanes] = re.astype(BF)
                    sbi[i, to + 16 : to + 32, lanes] = im.astype(BF)
        send_b(sbi, rbi, 2 * t + 1, t, i)

    lane = lax.broadcasted_iota(jnp.int32, (16, 256), 1)
    unit_long, unit = np.float32(TWO_PI / 512), np.float32(TWO_PI / 256)
    index_y = e * 16 + lax.broadcasted_iota(jnp.int32, (16, 256), 0)
    wave_y = jnp.where(index_y < 128, index_y, index_y - 256).astype(F32) * unit

    def along_x(h):
        return (d * 32 + h * 16 + (lane & 15)).astype(F32) * unit_long

    def along_z(k1):
        index_z = k1 + 16 * (lane // 16)
        return index_z, jnp.where(index_z < 128, index_z, index_z - 256).astype(F32) * unit

    def factors(step, _):
        h, k1 = step // 16, step & 15
        wave_x = along_x(h)
        index_z, wave_z = along_z(k1)
        ksq = wave_x * wave_x + wave_y * wave_y + wave_z * wave_z
        edge = (index_y == 128) | (index_z == 128)
        rows = pl.ds(pl.multiple_of(k1 * 16, 16), 16)
        gain[h, rows] = jnp.where(edge, 0.0, 1.0 / (0.05 * ksq + 0.5))
        inv[h, rows] = jnp.where(ksq > 0.0, 1.0 / jnp.where(ksq > 0.0, ksq, 1.0), 0.0)
        return _

    def project(t, h):
        wave_x = along_x(h)

        def one(k1, _):
            wave_z = along_z(k1)[1]
            rows = pl.ds(pl.multiple_of(k1 * 16, 16), 16)
            g, n = gain[h, rows], inv[h, rows]
            for ri in range(2):
                w = [spec[3 * h + c, ri, rows] for c in range(3)]
                along = (wave_x * w[0] + wave_y * w[1] + wave_z * w[2]) * n
                for c, wave in enumerate((wave_x, wave_y, wave_z)):
                    value = g * (w[c] - wave * along)
                    if t == 0:
                        first[3 * h + c, ri, rows] = value.astype(BF)
                    else:
                        second[3 * h + c, ri, rows] = (first[3 * h + c, ri, rows].astype(F32) - value).astype(BF)
            return _

        lax.fori_loop(0, 16, one, 0)

    def each(count, step):
        def body(i, _):
            step(i)
            return _

        lax.fori_loop(0, count, body, 0)

    def spectral(t, source):
        def step(n):
            @pl.when(n < 6)
            def _():
                y_forward(t, n)

            @pl.when(((n >= 1) & (n <= 3)) | ((n >= 6) & (n <= 8)))
            def _():
                z_forward(t, jnp.where(n <= 3, n - 1, n - 3))

            @pl.when((n == 3) | (n == 8))
            def _():
                project(t, jnp.where(n == 3, 0, 1))

            @pl.when((n == 3) | (n == 5) | (n == 6) | ((n >= 8) & (n <= 10)))
            def _():
                z_inverse(source, t, jnp.where(n == 3, 0, jnp.where(n <= 6, n - 4, n - 5)))

            @pl.when((n == 5) | (n >= 8))
            def _():
                y_inverse(t, jnp.where(n == 5, 0, n - 7))

        each(13, step)

    loads["fx"].wait()
    for i in range(3):
        loads[i].wait()
    each(3, lambda c: x_forward(0, c, 0))
    each(3, lambda c: x_forward(0, c, 1))
    lax.fori_loop(0, 32, factors, 0)
    loads["scalar"].wait()
    for z in range(8):
        state[0, z + 1, pl.ds(8, 64), :] = scalar[z].astype(F32)
        ysend[0, 0, pl.ds(z, 1), :] = state[0, z + 1, pl.ds(8, 1), :]
        ysend[0, 1, pl.ds(z, 1), :] = state[0, z + 1, pl.ds(71, 1), :]
    zsend[0, 0] = scalar[0]
    zsend[0, 1] = scalar[7]
    for q in range(4):
        send_z(0, q)
    for side in range(2):
        send_y(0, side)
    for name in TABLES[1:]:
        loads[name].wait()
    loads["mask"].wait()
    spectral(0, first)

    def back_in_x(t, c):
        for i in (c, c + 3):
            arrived(rai.at[t, i], a_recv.at[2 * t + 1, i])
        x_inverse(t, c)

    def sent(t, c):
        for i in (c, c + 3):
            sent_b(2 * t, i)
            sent_b(2 * t + 1, i)
            sent_a(2 * t + 1, i)

    def middle(c):
        back_in_x(0, c)
        for i in (c, c + 3):
            sent_a(0, i)
        x_forward(1, c, 0)
        sent(0, c)

    each(3, middle)
    each(3, lambda c: x_forward(1, c, 1))
    spectral(1, second)

    def coefficients(z, c):
        fluid = 0.25 * (1.0 - mask[z].astype(F32))
        u = field[c, z].astype(F32)
        below = fluid * (0.25 + jnp.maximum(u, 0.0))
        above = fluid * (0.25 - jnp.minimum(u, 0.0))
        coef[2 * c, z] = below
        coef[2 * c + 1, z] = above
        start = jnp.where(c == 0, jnp.ones_like(u), coef[6, z])
        coef[6, z] = start - (below + above)
        return c

    def last(c):
        back_in_x(1, c)
        pltpu.make_async_copy(field.at[c], velocity_h.at[c], out_sem.at[c]).start()
        lax.fori_loop(0, 8, coefficients, c)
        for i in (c, c + 3):
            sent_a(2, i)
        sent(1, c)

    each(3, last)

    def section(s, carry):
        now, later = s & 1, (s + 1) & 1

        def block(z, q, below_z, above_z):
            at = 8 + 16 * q
            rows, cells = pl.ds(at, 16), pl.ds(16 * q, 16)
            center = state[now, z, rows]
            new = coef[6, z - 1, cells] * center
            new = new + coef[0, z - 1, cells] * pltpu.roll(center, 1, 1)
            new = new + coef[1, z - 1, cells] * pltpu.roll(center, 511, 1)
            new = new + coef[2, z - 1, cells] * state[now, z, pl.ds(at - 1, 16)]
            new = new + coef[3, z - 1, cells] * state[now, z, pl.ds(at + 1, 16)]
            new = new + coef[4, z - 1, cells] * below_z + coef[5, z - 1, cells] * above_z
            state[later, z, rows] = new
            return new

        for q in (1, 2, 0, 3):
            rows, cells = pl.ds(8 + 16 * q, 16), pl.ds(16 * q, 16)
            if q in (0, 3):
                side = q // 3
                arrived(yrecv.at[s, side], y_rsem.at[s, side])
                for z in range(8):
                    state[now, z + 1, pl.ds(7 + 65 * side, 1), :] = yrecv[s, side, pl.ds(z, 1), :]
            for side in range(2):
                arrived(zrecv.at[s, side, cells], z_rsem.at[s, side, q])
            bottom = block(1, q, zrecv[s, 0, cells].astype(F32), state[now, 2, rows])
            top = block(8, q, state[now, 7, rows], zrecv[s, 1, cells].astype(F32))

            @pl.when(s < SECTIONS - 1)
            def _():
                zsend[s + 1, 0, cells] = bottom.astype(BF)
                zsend[s + 1, 1, cells] = top.astype(BF)
                send_z(s + 1, q)

            for z in range(2, 8):
                block(z, q, state[now, z - 1, rows], state[now, z + 1, rows])
            if q in (0, 3):
                side = q // 3

                @pl.when(s < SECTIONS - 1)
                def _():
                    for z in range(8):
                        ysend[s + 1, side, pl.ds(z, 1), :] = state[later, z + 1, pl.ds(8 + 63 * side, 1), :]
                    send_y(s + 1, side)
        return carry

    lax.fori_loop(0, SECTIONS, section, 0)
    for z in range(8):
        conc[z] = state[SECTIONS % 2, z + 1, pl.ds(8, 64), :].astype(BF)

    for s in range(SECTIONS):
        for i in range(2):
            arrived(zsend.at[s, i], z_ssem.at[s, i])
            arrived(ysend.at[s, i], y_ssem.at[s, i])
    out = pltpu.make_async_copy(conc, conc_h, out_sem.at[3])
    out.start()
    for c in range(3):
        pltpu.make_async_copy(field.at[c], velocity_h.at[c], out_sem.at[c]).wait()
    out.wait()


def place_kernel(velocity_in, conc_in, velocity, conc, held, in_sem, out_sem):
    pairs = [(velocity_in.at[c], held.at[c], velocity.at[c]) for c in range(3)] + [(conc_in, held.at[3], conc)]
    loads = [pltpu.make_async_copy(a, b, in_sem.at[i]) for i, (a, b, _) in enumerate(pairs)]
    stores = [pltpu.make_async_copy(b, c, out_sem.at[i]) for i, (_, b, c) in enumerate(pairs)]
    for copy in loads:
        copy.start()
    for load, store in zip(loads, stores):
        load.wait()
        store.start()
    for copy in stores:
        copy.wait()


def local(force, mask, scalar):
    tables = numpy_tables()
    vm = pltpu.VMEM
    dma = pltpu.SemaphoreType.DMA
    scratch = [vm((3, 8, 64, 512), BF), vm((8, 64, 512), jnp.int32), vm((8, 64, 512), BF)]
    for name in TABLES:
        value = tables[name]
        shape = value.shape[1:] if name in ROTATED else value.shape
        scratch.append(vm(shape, value.dtype))
    scratch += [
        vm((2, 256, 256), F32), vm((2, 256, 256), F32),
        vm((6, 8, 2, 64, 128), BF), vm((2, 6, 2, 256, 256), BF),
        vm((6, 512, 256), BF), vm((2, 6, 512, 256), BF),
        vm((6, 512, 256), BF), vm((2, 6, 512, 256), BF),
        vm((6, 2, 256, 256), BF), vm((2, 6, 8, 2, 64, 128), BF),
        vm((6, 2, 256, 256), F32), vm((6, 2, 256, 256), BF), vm((6, 2, 256, 256), BF),
        vm((512, 512), BF), vm((512, 256), BF), vm((4, 4, 2, 16, 256), F32),
        vm((SECTIONS, 2, 64, 512), BF), vm((SECTIONS, 2, 64, 512), BF),
        vm((SECTIONS, 2, 8, 512), F32), vm((SECTIONS, 2, 8, 512), F32),
        vm((7, 8, 64, 512), F32), vm((2, 10, 80, 512), F32), vm((8, 64, 512), BF),
        dma((5,)), dma((len(TABLES),)),
        dma((4, 6)), dma((4, 6)), dma((4, 6)), dma((4, 6)),
        dma((SECTIONS, 2)), dma((SECTIONS, 2, 4)), dma((SECTIONS, 2)), dma((SECTIONS, 2)),
        dma((4,)),
    ]
    any_spec = pl.BlockSpec(memory_space=pl.ANY)
    velocity, conc = pl.pallas_call(
        mixer_kernel,
        out_shape=(
            jax.ShapeDtypeStruct((3, 8, 64, 512), BF),
            jax.ShapeDtypeStruct((8, 64, 512), BF),
        ),
        in_specs=[any_spec] * (3 + len(TABLES)),
        out_specs=(any_spec, any_spec),
        scratch_shapes=scratch,
        compiler_params=pltpu.CompilerParams(
            collective_id=0, has_side_effects=True, vmem_limit_bytes=62 * 1024 * 1024
        ),
        name="mixer",
    )(
        force,
        mask,
        scalar,
        *[jnp.asarray(tables[name]) for name in TABLES],
    )
    return pl.pallas_call(
        place_kernel,
        out_shape=(
            jax.ShapeDtypeStruct((3, 8, 64, 512), BF),
            jax.ShapeDtypeStruct((8, 64, 512), BF),
        ),
        in_specs=[any_spec] * 2,
        out_specs=(any_spec, any_spec),
        scratch_shapes=[vm((4, 8, 64, 512), BF), dma((4,)), dma((4,))],
        name="place",
    )(velocity, conc)


def solution(mesh):
    placed = (P(None, "col", "row", None), P("col", "row", None), P("col", "row", None))
    return jax.shard_map(
        local,
        mesh=mesh,
        in_specs=placed,
        out_specs=(P(None, "col", "row", None), P("col", "row", None)),
        check_vma=False,
    )
```

```python
import numpy as np
import jax
import jax.numpy as jnp
import ml_dtypes
from jax import lax
from jax.experimental import pallas as pl
from jax.experimental.pallas import tpu as pltpu
from jax.sharding import PartitionSpec as P

SECTIONS = 5
MESH = pl.DeviceIdType.MESH
BF = jnp.bfloat16
F32 = jnp.float32
TWO_PI = 2.0 * np.pi
PLANE_ORDER = (
    (1, 0), (3, 0), (0, 1), (0, 3), (1, 1), (3, 3), (1, 3), (3, 1),
    (2, 0), (0, 2), (2, 1), (1, 2), (2, 3), (3, 2), (2, 2),
)


def numpy_tables():
    def half(values):
        return values.astype(np.float32).astype(ml_dtypes.bfloat16)

    x = np.arange(512)
    ri, d, k = (v.reshape(-1) for v in np.meshgrid(np.arange(2), np.arange(8), np.arange(16), indexing="ij"))
    e1, ri1, k1 = (v.reshape(-1) for v in np.meshgrid(np.arange(16), np.arange(2), np.arange(8), indexing="ij"))
    m = np.concatenate([d * 32 + k, (e1 // 2) * 32 + 16 + (e1 % 2) * 8 + k1])
    ri = np.concatenate([ri, ri1])
    angle = (np.outer(x, m) % 512) * (TWO_PI / 512)
    fx = np.where(ri == 0, np.cos(angle), -np.sin(angle)) / np.sqrt(512.0)
    bx = (fx * np.where(m == 0, 1.0, 2.0)).T
    y = np.arange(256)
    angle = (np.outer(y, y) % 256) * (TWO_PI / 256)
    c, s = np.cos(angle) / 16.0, np.sin(angle) / 16.0
    real = np.concatenate([c, s], 1).reshape(16, 1, 16, 512)
    imag = np.concatenate([-s, c], 1).reshape(16, 1, 16, 512)
    ty = np.concatenate([real, imag], 1).reshape(512, 512)
    uy = np.concatenate([c, s], 1)
    uyi = np.concatenate([c, -s], 1)
    n = np.arange(16)
    angle = (np.outer(n, n) % 16) * (TWO_PI / 16)
    c, s = np.cos(angle) / 4.0, np.sin(angle) / 4.0
    cs = np.zeros((8, 256, 512))
    csi = np.zeros((8, 256, 512))
    tw = np.zeros((8, 2, 16, 256))
    k = np.arange(16)
    for d in range(8):
        for low in range(2):
            for p in range(8):
                zp = low * 8 + (p - d) % 8
                at = low * 128 + p * 16
                for k2 in range(16):
                    cs[d, at + k, k2 * 16 + k] = c[zp, k2]
                    cs[d, at + k, 256 + k2 * 16 + k] = s[zp, k2]
                    csi[d, k2 * 16 + k, at + k] = c[zp, k2]
                    csi[d, k2 * 16 + k, 256 + at + k] = s[zp, k2]
                tw[d, 0, :, at : at + 16] = np.cos(TWO_PI * zp * n / 256)[:, None] / 4.0
                tw[d, 1, :, at : at + 16] = np.sin(TWO_PI * zp * n / 256)[:, None] / 4.0
    utw = np.zeros((16, 2, 16, 128))
    uz = np.zeros((8, 256, 256))
    k = np.arange(8)
    for turn in range(8):
        for low in range(2):
            for p in range(8):
                zp = low * 8 + (p - turn) % 8
                utw[low * 8 + turn, 0, :, p * 16 : p * 16 + 16] = np.cos(TWO_PI * zp * n / 256)[:, None] / 4.0
                utw[low * 8 + turn, 1, :, p * 16 : p * 16 + 16] = np.sin(TWO_PI * zp * n / 256)[:, None] / 4.0
                at = low * 128 + p * 16
                for k2 in range(16):
                    to = k2 * 16
                    uz[turn, at + k, to + k] = c[zp, k2]
                    uz[turn, at + 8 + k, to + k] = s[zp, k2]
                    uz[turn, at + k, to + 8 + k] = -s[zp, k2]
                    uz[turn, at + 8 + k, to + 8 + k] = c[zp, k2]
    return dict(
        uy=half(uy), uyi=half(uyi), uz=half(uz), uzi=half(uz.transpose(0, 2, 1)), utw=utw.astype(np.float32),
        fx=half(fx), bx=half(bx), ty=half(ty), tyi=half(ty.T), cs=half(cs), csi=half(csi),
        tw=tw.astype(np.float32),
    )


TABLES = ("fx", "ty", "utw", "tw", "cs", "uy", "uz", "csi", "uzi", "tyi", "uyi", "bx")
BY_D = ("cs", "tw", "csi")
BY_E = ("uz", "uzi")
VARIED = BY_D + BY_E + ("utw",)


def radix4(a, sign):
    def add(u, v):
        return u[0] + v[0], u[1] + v[1]

    def sub(u, v):
        return u[0] - v[0], u[1] - v[1]

    t0, t1 = add(a[0], a[2]), sub(a[0], a[2])
    t2, t3 = add(a[1], a[3]), sub(a[1], a[3])
    t3 = (t3[1], -t3[0]) if sign > 0 else (-t3[1], t3[0])
    return add(t0, t2), add(t1, t3), sub(t0, t2), sub(t1, t3)


def turned_by(value, j, sign):
    if j == 0:
        return value
    c, s = float(np.cos(TWO_PI * j / 16)), float(np.sin(TWO_PI * j / 16)) * sign
    re, im = value
    return re * c + im * s, im * c - re * s


def times_minus_i(value):
    imag = (lax.broadcasted_iota(jnp.int32, value.shape, 1) & 8) != 0
    return jnp.where(imag, -pltpu.roll(value, 8, 1), pltpu.roll(value, 120, 1))


def packed_radix4(a, sign):
    t0, t1, t2 = a[0] + a[2], a[0] - a[2], a[1] + a[3]
    t3 = times_minus_i(a[1] - a[3])
    if sign < 0:
        t3 = -t3
    return t0 + t2, t1 + t3, t0 - t2, t1 - t3


def packed_turned(value, j, sign):
    if j == 0:
        return value
    c, s = float(np.cos(TWO_PI * j / 16)), float(np.sin(TWO_PI * j / 16)) * sign
    return value * c + times_minus_i(value) * s


def packed_dft16(values, sign):
    parts = [packed_radix4(values[low::4], sign) for low in range(4)]
    parts = [[packed_turned(v, low * k, sign) for k, v in enumerate(parts[low])] for low in range(4)]
    out = [None] * 16
    for k in range(4):
        out[k::4] = packed_radix4([parts[low][k] for low in range(4)], sign)
    return out


def merge(tiles, place):
    for bit in (1, 2, 4):
        take = (place & bit) != 0
        tiles = [jnp.where(take, tiles[(m + bit) % 8], tiles[m]) for m in range(8)]
    return tiles


def dot(a, b):
    return jnp.dot(a, b, preferred_element_type=F32)


def mixer_kernel(*refs):
    force_h, mask_h, scalar_h = refs[:3]
    count = len(TABLES)
    tables_h = dict(zip(TABLES, refs[3 : 3 + count]))
    velocity_h, conc_h = refs[3 + count : 5 + count]
    (field, mask, scalar, *rest) = refs[5 + count :]
    tab = dict(zip(TABLES, rest[:count]))
    (gain, inv, sa, ra, sb, rb, sbi, rbi, sai, rai, spec, first, second, lines, big, mid,
     gain1, inv1, su, ru, sv, rv, svi, rvi, sui, rui, spec1, first1, second1, stacked,
     u_send, u_recv, v_send, v_recv,
     zsend, zrecv, ysend, yrecv, coef, state, conc,
     in_sem, tab_sem, a_send, a_recv, b_send, b_recv, z_ssem, z_rsem, y_ssem, y_rsem, out_sem) = rest[count:]

    r = lax.axis_index("row")
    col = lax.axis_index("col")
    e = col // 2
    xl = col % 2
    d = xl * 4 + r

    def load(source, target, sem):
        copy = pltpu.make_async_copy(source, target, sem)
        copy.start()
        return copy

    def load_table(name):
        source = tables_h[name]
        sem = tab_sem.at[TABLES.index(name)]
        if name in VARIED:
            source = source.at[d if name in BY_D else (e & 7) + (8 * xl if name == "utw" else 0)]
        return load(source, tab[name], sem)

    loads = {0: load(force_h.at[0], field.at[0], in_sem.at[0]), "fx": load_table("fx")}
    for i in (1, 2):
        loads[i] = load(force_h.at[i], field.at[i], in_sem.at[i])
    loads["scalar"] = load(scalar_h, scalar, in_sem.at[4])
    for name in TABLES[1:]:
        loads[name] = load_table(name)
    loads["mask"] = load(mask_h, mask, in_sem.at[3])

    core = r & 1
    x = (r // 2) * 2 + xl
    y_at, z_at = e // 4, e & 3

    def x_peer(step, of_core):
        at = (x + step * (1 + 2 * core)) & 3
        low = at & 1
        row = (at - low) + of_core
        return low * 4 + row, (row, e * 2 + low)

    def plane_peer(dy, dz):
        to = ((y_at + dy + core * (3 * dz - dy)) & 3) * 4 + ((z_at + dz + core * (3 * dy - dz)) & 3)
        return to, (r, to * 2 + xl)

    x_peers = [
        x_peer(step, core if same else 1 - core)
        for step, same in ((1, 1), (3, 1), (1, 0), (3, 0), (2, 1), (2, 0), (0, 0))
    ]
    plane_peers = [plane_peer(dy, dz) for dy, dz in PLANE_ORDER]

    z_up = (r, lax.rem(col + 1, 32))
    z_down = (r, lax.rem(col + 31, 32))
    y_up = (lax.rem(r + 1, 4), col)
    y_down = (lax.rem(r + 3, 4), col)

    barrier = pltpu.get_barrier_semaphore()

    for _, device in x_peers + plane_peers:
        pl.semaphore_signal(barrier, inc=1, device_id=device, device_id_type=MESH)
    across = (r, lax.rem(col + 31 + 2 * xl, 32))
    pl.semaphore_signal(barrier, inc=1, device_id=across, device_id_type=MESH)
    pl.semaphore_wait(barrier, 23)

    def remote(source, target, ssem, rsem, device):
        return pltpu.make_async_remote_copy(
            src_ref=source, dst_ref=target, send_sem=ssem, recv_sem=rsem,
            device_id=device, device_id_type=MESH)

    my_rows = pl.ds(pl.multiple_of(r * 64, 64), 64)
    my_lanes = pl.ds(pl.multiple_of(xl * 128, 128), 128)
    my_slab = pl.ds(pl.multiple_of(e * 32, 32), 32)

    def send_a(t, i):
        target = ra.at[t, i, :, my_rows, my_lanes]
        recv = a_recv.at[2 * t, i]

        for to, device in x_peers:
            remote(sa.at[i, to], target, a_send.at[2 * t, i], recv, device).start()
        pltpu.make_async_copy(sa.at[i, d], target, recv).start()

    def send_ai(t, i):
        target = rai.at[t, i, d]
        recv = a_recv.at[2 * t + 1, i]

        def piece(to):
            rows = pl.ds(pl.multiple_of((to & 3) * 64, 64), 64)
            lanes = pl.ds(pl.multiple_of((to // 4) * 128, 128), 128)
            return sai.at[i, :, rows, lanes]

        for to, device in x_peers:
            remote(piece(to), target, a_send.at[2 * t + 1, i], recv, device).start()
        pltpu.make_async_copy(piece(d), target, recv).start()

    def send_b(source, into, k, t, i):
        target = into.at[t, i, my_slab]
        recv = b_recv.at[k, i]

        for to, device in plane_peers:
            slab = source.at[i, pl.ds(pl.multiple_of(to * 32, 32), 32)]
            remote(slab, target, b_send.at[k, i], recv, device).start()
        pltpu.make_async_copy(source.at[i, my_slab], target, recv).start()

    def send_u(source, into, k, t, c):
        target = into.at[t, c, e]
        recv = u_recv.at[k, c]
        for to, device in plane_peers:
            remote(source.at[c, to], target, u_send.at[k, c], recv, device).start()
        pltpu.make_async_copy(source.at[c, e], target, recv).start()

    def send_v(t, c):
        target = rv.at[t, c, :, my_rows, my_lanes]
        recv = v_recv.at[2 * t, c]
        for to, device in x_peers:
            remote(sv.at[c, pl.ds(2 * to, 2)], target, v_send.at[2 * t, c], recv, device).start()
        pltpu.make_async_copy(sv.at[c, pl.ds(2 * d, 2)], target, recv).start()

    def send_vi(t, c):
        target = rvi.at[t, c, pl.ds(2 * d, 2)]
        recv = v_recv.at[2 * t + 1, c]

        def piece(to):
            rows = pl.ds(pl.multiple_of((to & 3) * 64, 64), 64)
            lanes = pl.ds(pl.multiple_of((to // 4) * 128, 128), 128)
            return svi.at[c, :, rows, lanes]

        for to, device in x_peers:
            remote(piece(to), target, v_send.at[2 * t + 1, c], recv, device).start()
        pltpu.make_async_copy(piece(d), target, recv).start()

    def arrived(buffer, sem):
        pltpu.make_async_copy(buffer, buffer, sem).wait()

    def sent_a(k, i):
        arrived(sa.at[i, pl.ds(0, 7)], a_send.at[k, i])

    def sent_b(k, i):
        arrived(sb.at[i, pl.ds(0, 480)], b_send.at[k, i])

    def sent_u(k, i):
        arrived(su.at[i, pl.ds(0, 15)], u_send.at[k, i])

    def sent_v(k, i):
        arrived(sv.at[i, pl.ds(0, 14)], v_send.at[k, i])

    def send_z(s, q):
        rows = pl.ds(16 * q, 16)
        for side, device in ((0, z_down), (1, z_up)):
            remote(zsend.at[s, side, rows], zrecv.at[s, 1 - side, rows],
                   z_ssem.at[s, side], z_rsem.at[s, 1 - side, q], device).start()

    def send_y(s, side):
        remote(ysend.at[s, side], yrecv.at[s, 1 - side], y_ssem.at[s, side], y_rsem.at[s, 1 - side],
               (y_down, y_up)[side]).start()

    place = lax.broadcasted_iota(jnp.int32, (64, 128), 1) // 16

    def x_forward(t, c):
        spread = dot(field[c].reshape(512, 512), tab["fx"][:, 0:256])
        for ri in range(2):
            tiles = []
            for z in range(8):
                tile = spread[z * 64 : z * 64 + 64, ri * 128 : ri * 128 + 128]
                tiles.append(pltpu.roll(tile, 16 * z, 1) if z else tile)
            tiles = merge(tiles, place)
            for to in range(8):
                sa[c, to, ri] = tiles[-to % 8].astype(BF)
        send_a(t, c)

    def x_forward1(t, c):
        spread = dot(field[c].reshape(512, 512), tab["fx"][:, 256:512])
        for j in range(2):
            tiles = []
            for z in range(8):
                tile = spread[z * 64 : z * 64 + 64, j * 128 : j * 128 + 128]
                tiles.append(pltpu.roll(tile, 16 * z, 1) if z else tile)
            tiles = merge(tiles, place)
            for to in range(8):
                su[c, 8 * j + to] = tiles[-to % 8].astype(BF)
        send_u(su, ru, 2 * t, t, c)

    def x_inverse(t, c):
        for j in range(4):
            if j < 2:
                tiles = [rai[t, c, source, j].astype(F32) for source in range(8)]
            else:
                tiles = [rui[t, c, 8 * (j - 2) + source].astype(F32) for source in range(8)]
            tiles = merge(tiles, place)
            for z in range(8):
                tile = tiles[-z % 8]
                tile = pltpu.roll(tile, 128 - 16 * z, 1) if z else tile
                lines[z * 64 : z * 64 + 64, j * 128 : j * 128 + 128] = tile.astype(BF)
        values = dot(lines[...], tab["bx"][...]).astype(BF).reshape(8, 64, 512)
        if t == 0:
            values = (values.astype(F32) * mask[...].astype(F32)).astype(BF)
        field[c] = values

    def y_forward(t, i):
        arrived(ra.at[t, i], a_recv.at[2 * t, i])
        sb[i] = dot(tab["ty"][...], ra[t, i].reshape(512, 256)).astype(BF)
        send_b(sb, rb, 2 * t, t, i)

    def y_inverse(t, i):
        arrived(rbi.at[t, i], b_recv.at[2 * t + 1, i])
        sai[i] = dot(tab["tyi"][...], rbi[t, i]).astype(BF).reshape(2, 256, 256)
        send_ai(t, i)

    def z_forward(t, i):
        arrived(rb.at[t, i], b_recv.at[2 * t, i])
        for half in range(2):
            lanes = slice(half * 128, half * 128 + 128)

            def source(e_from, ri):
                return rb[t, i, e_from * 32 + ri * 16 : e_from * 32 + ri * 16 + 16, lanes].astype(F32)

            for low in range(4):
                out = radix4([(source(low + 4 * j, 0), source(low + 4 * j, 1)) for j in range(4)], 1)
                for k, value in enumerate(out):
                    mid[low, k, 0, :, lanes], mid[low, k, 1, :, lanes] = turned_by(value, low * k, 1)
            for k in range(4):
                out = radix4([(mid[low, k, 0, :, lanes], mid[low, k, 1, :, lanes]) for low in range(4)], 1)
                for high, (re, im) in enumerate(out):
                    k1 = k + 4 * high
                    wc, ws = tab["tw"][0, k1 : k1 + 1, lanes], tab["tw"][1, k1 : k1 + 1, lanes]
                    big[k1 * 16 : k1 * 16 + 16, lanes] = (re * wc + im * ws).astype(BF)
                    big[256 + k1 * 16 : 256 + k1 * 16 + 16, lanes] = (im * wc - re * ws).astype(BF)
        both = dot(big[...], tab["cs"][...])
        spec[i, 0] = both[:256, :256] + both[256:, 256:]
        spec[i, 1] = both[256:, :256] - both[:256, 256:]

    def z_inverse(source, t, i):
        both = dot(source[i].reshape(512, 256), tab["csi"][...])
        for half in range(2):
            lanes = slice(half * 128, half * 128 + 128)
            other = slice(256 + half * 128, 256 + half * 128 + 128)

            def value(k1):
                upper, lower = slice(k1 * 16, k1 * 16 + 16), slice(256 + k1 * 16, 256 + k1 * 16 + 16)
                re = both[upper, lanes] - both[lower, other]
                im = both[lower, lanes] + both[upper, other]
                wc, ws = tab["tw"][0, k1 : k1 + 1, lanes], tab["tw"][1, k1 : k1 + 1, lanes]
                return re * wc - im * ws, im * wc + re * ws

            for low in range(4):
                out = radix4([value(low + 4 * j) for j in range(4)], -1)
                for k, turned in enumerate(out):
                    mid[low, k, 0, :, lanes], mid[low, k, 1, :, lanes] = turned_by(turned, low * k, -1)
            for k in range(4):
                out = radix4([(mid[low, k, 0, :, lanes], mid[low, k, 1, :, lanes]) for low in range(4)], -1)
                for high, (re, im) in enumerate(out):
                    to = (k + 4 * high) * 32
                    sbi[i, to : to + 16, lanes] = re.astype(BF)
                    sbi[i, to + 16 : to + 32, lanes] = im.astype(BF)
        send_b(sbi, rbi, 2 * t + 1, t, i)

    def v_forward(t, c):
        arrived(ru.at[t, c], u_recv.at[2 * t, c])

        def some(n, carry):
            rows = pl.ds(pl.multiple_of(n * 16, 16), 16)
            out = packed_dft16([ru[t, c, j, rows].astype(F32) for j in range(16)], 1)
            for k1, value in enumerate(out):
                wc, ws = tab["utw"][0, k1 : k1 + 1], tab["utw"][1, k1 : k1 + 1]
                sv[c, k1, rows] = (value * wc + times_minus_i(value) * ws).astype(BF)
            return carry

        lax.fori_loop(0, 4, some, 0)
        send_v(t, c)

    def v_inverse(t, c):
        arrived(rvi.at[t, c], v_recv.at[2 * t + 1, c])

        def some(n, carry):
            rows = pl.ds(pl.multiple_of(n * 16, 16), 16)
            values = []
            for k1 in range(16):
                value = rvi[t, c, k1, rows].astype(F32)
                wc, ws = tab["utw"][0, k1 : k1 + 1], tab["utw"][1, k1 : k1 + 1]
                values.append(value * wc - times_minus_i(value) * ws)
            for j, value in enumerate(packed_dft16(values, -1)):
                sui[c, j, rows] = value.astype(BF)
            return carry

        lax.fori_loop(0, 4, some, 0)
        send_u(sui, rui, 2 * t + 1, t, c)

    def y_product(table, values, wide):
        for half in range(2):
            lanes = slice(half * 128, half * 128 + 128)
            stacked[256:512, lanes] = times_minus_i(wide[:, lanes]).astype(BF)
        stacked[0:256, :] = values
        return dot(table, stacked[...]).astype(BF)

    def w_forward(t, c):
        arrived(rv.at[t, c], v_recv.at[2 * t, c])
        for k1 in range(2):
            values = rv[t, c, k1]
            big[k1 * 256 : k1 * 256 + 256, :] = y_product(tab["uy"][...], values, values.astype(F32))
        spec1[c] = dot(big[...], tab["uz"][...])

    def w_inverse(source, t, c):
        wide = dot(source[c], tab["uzi"][...])
        for k1 in range(2):
            part = wide[k1 * 256 : k1 * 256 + 256]
            svi[c, k1] = y_product(tab["uyi"][...], part.astype(BF), part)
        send_vi(t, c)

    lane = lax.broadcasted_iota(jnp.int32, (16, 256), 1)
    unit_long, unit = np.float32(TWO_PI / 512), np.float32(TWO_PI / 256)
    index_y = e * 16 + lax.broadcasted_iota(jnp.int32, (16, 256), 0)
    wave_y = jnp.where(index_y < 128, index_y, index_y - 256).astype(F32) * unit

    wave_x = (d * 32 + (lane & 15)).astype(F32) * unit_long
    wave_x1 = ((e // 2) * 32 + 16 + (e & 1) * 8 + (lane & 7)).astype(F32) * unit_long

    def along_z(k1):
        index_z = k1 + 16 * (lane // 16)
        return index_z, jnp.where(index_z < 128, index_z, index_z - 256).astype(F32) * unit

    def at_rows(n):
        return pl.ds(pl.multiple_of(n * 16, 16), 16)

    def along_y1(n):
        index = (n & 15) * 16 + lax.broadcasted_iota(jnp.int32, (16, 256), 0)
        return index, jnp.where(index < 128, index, index - 256).astype(F32) * unit

    def scales(kx, ky, kz, edge):
        ksq = kx * kx + ky * ky + kz * kz
        return (
            jnp.where(edge, 0.0, 1.0 / (0.05 * ksq + 0.5)),
            jnp.where(ksq > 0.0, 1.0 / jnp.where(ksq > 0.0, ksq, 1.0), 0.0),
        )

    def factors(n, carry):
        index_z, wave_z = along_z(n)
        gain[at_rows(n)], inv[at_rows(n)] = scales(wave_x, wave_y, wave_z, (index_y == 128) | (index_z == 128))
        return carry

    def factors1(n, carry):
        index_z, wave_z = along_z(2 * d + n // 16)
        index, wave = along_y1(n)
        gain1[at_rows(n)], inv1[at_rows(n)] = scales(wave_x1, wave, wave_z, (index == 128) | (index_z == 128))
        return carry

    def projected(w, waves, g, n):
        along = (waves[0] * w[0] + waves[1] * w[1] + waves[2] * w[2]) * n
        return [g * (w[c] - waves[c] * along) for c in range(3)]

    def project(t):
        def one(n, carry):
            rows = at_rows(n)
            waves = (wave_x, wave_y, along_z(n)[1])
            for ri in range(2):
                out = projected([spec[c, ri, rows] for c in range(3)], waves, gain[rows], inv[rows])
                for c in range(3):
                    if t == 0:
                        first[c, ri, rows] = out[c].astype(BF)
                    else:
                        second[c, ri, rows] = (first[c, ri, rows].astype(F32) - out[c]).astype(BF)
            return carry

        lax.fori_loop(0, 16, one, 0)

    def project1(t):
        def one(n, carry):
            rows = at_rows(n)
            waves = (wave_x1, along_y1(n)[1], along_z(2 * d + n // 16)[1])
            out = projected([spec1[c, rows] for c in range(3)], waves, gain1[rows], inv1[rows])
            for c in range(3):
                if t == 0:
                    first1[c, rows] = out[c].astype(BF)
                else:
                    second1[c, rows] = (first1[c, rows].astype(F32) - out[c]).astype(BF)
            return carry

        lax.fori_loop(0, 32, one, 0)

    def each(count, step):
        def body(i, _):
            step(i)
            return _

        lax.fori_loop(0, count, body, 0)

    def spectral(t, source, source1):
        def out(c):
            y_forward(t, c)
            v_forward(t, c)

        def inner(c):
            w_forward(t, c)
            z_forward(t, c)

        def outer(c):
            w_inverse(source1, t, c)
            z_inverse(source, t, c)

        def back(c):
            v_inverse(t, c)
            y_inverse(t, c)

        each(3, out)
        each(3, inner)
        project1(t)
        project(t)
        each(3, outer)
        each(3, back)

    loads["fx"].wait()
    for i in range(3):
        loads[i].wait()
    def start(c):
        x_forward(0, c)
        x_forward1(0, c)

    each(3, start)
    lax.fori_loop(0, 16, factors, 0)
    lax.fori_loop(0, 32, factors1, 0)
    loads["scalar"].wait()
    for z in range(8):
        state[0, z + 1, pl.ds(8, 64), :] = scalar[z].astype(F32)
        ysend[0, 0, pl.ds(z, 1), :] = state[0, z + 1, pl.ds(8, 1), :]
        ysend[0, 1, pl.ds(z, 1), :] = state[0, z + 1, pl.ds(71, 1), :]
    zsend[0, 0] = scalar[0]
    zsend[0, 1] = scalar[7]
    for q in range(4):
        send_z(0, q)
    for side in range(2):
        send_y(0, side)
    for name in TABLES[1:]:
        loads[name].wait()
    loads["mask"].wait()
    spectral(0, first, first1)

    def back_in_x(t, c):
        arrived(rai.at[t, c], a_recv.at[2 * t + 1, c])
        arrived(rui.at[t, c], u_recv.at[2 * t + 1, c])
        x_inverse(t, c)

    def sent(t, c):
        for k in (2 * t, 2 * t + 1):
            sent_a(k, c)
            sent_b(k, c)
            sent_u(k, c)
            sent_v(k, c)

    def middle(c):
        back_in_x(0, c)
        sent(0, c)
        x_forward(1, c)
        x_forward1(1, c)

    each(3, middle)
    spectral(1, second, second1)

    def coefficients(z, c):
        fluid = 0.25 * (1.0 - mask[z].astype(F32))
        u = field[c, z].astype(F32)
        below = fluid * (0.25 + jnp.maximum(u, 0.0))
        above = fluid * (0.25 - jnp.minimum(u, 0.0))
        coef[2 * c, z] = below
        coef[2 * c + 1, z] = above
        start = jnp.where(c == 0, jnp.ones_like(u), coef[6, z])
        coef[6, z] = start - (below + above)
        return c

    def last(c):
        back_in_x(1, c)
        pltpu.make_async_copy(field.at[c], velocity_h.at[c], out_sem.at[c]).start()
        lax.fori_loop(0, 8, coefficients, c)
        sent(1, c)

    each(3, last)

    def section(s, carry):
        now, later = s & 1, (s + 1) & 1

        def block(z, q, below_z, above_z):
            at = 8 + 16 * q
            rows, cells = pl.ds(at, 16), pl.ds(16 * q, 16)
            center = state[now, z, rows]
            new = coef[6, z - 1, cells] * center
            new = new + coef[0, z - 1, cells] * pltpu.roll(center, 1, 1)
            new = new + coef[1, z - 1, cells] * pltpu.roll(center, 511, 1)
            new = new + coef[2, z - 1, cells] * state[now, z, pl.ds(at - 1, 16)]
            new = new + coef[3, z - 1, cells] * state[now, z, pl.ds(at + 1, 16)]
            new = new + coef[4, z - 1, cells] * below_z + coef[5, z - 1, cells] * above_z
            state[later, z, rows] = new
            return new

        for q in (1, 2, 0, 3):
            rows, cells = pl.ds(8 + 16 * q, 16), pl.ds(16 * q, 16)
            if q in (0, 3):
                side = q // 3
                arrived(yrecv.at[s, side], y_rsem.at[s, side])
                for z in range(8):
                    state[now, z + 1, pl.ds(7 + 65 * side, 1), :] = yrecv[s, side, pl.ds(z, 1), :]
            for side in range(2):
                arrived(zrecv.at[s, side, cells], z_rsem.at[s, side, q])
            bottom = block(1, q, zrecv[s, 0, cells].astype(F32), state[now, 2, rows])
            top = block(8, q, state[now, 7, rows], zrecv[s, 1, cells].astype(F32))

            @pl.when(s < SECTIONS - 1)
            def _():
                zsend[s + 1, 0, cells] = bottom.astype(BF)
                zsend[s + 1, 1, cells] = top.astype(BF)
                send_z(s + 1, q)

            for z in range(2, 8):
                block(z, q, state[now, z - 1, rows], state[now, z + 1, rows])
            if q in (0, 3):
                side = q // 3

                @pl.when(s < SECTIONS - 1)
                def _():
                    for z in range(8):
                        ysend[s + 1, side, pl.ds(z, 1), :] = state[later, z + 1, pl.ds(8 + 63 * side, 1), :]
                    send_y(s + 1, side)
        return carry

    lax.fori_loop(0, SECTIONS, section, 0)
    for z in range(8):
        conc[z] = state[SECTIONS % 2, z + 1, pl.ds(8, 64), :].astype(BF)

    for s in range(SECTIONS):
        for i in range(2):
            arrived(zsend.at[s, i], z_ssem.at[s, i])
            arrived(ysend.at[s, i], y_ssem.at[s, i])
    out = pltpu.make_async_copy(conc, conc_h, out_sem.at[3])
    out.start()
    for c in range(3):
        pltpu.make_async_copy(field.at[c], velocity_h.at[c], out_sem.at[c]).wait()
    out.wait()


def place_kernel(velocity_in, conc_in, velocity, conc, held, in_sem, out_sem):
    pairs = [(velocity_in.at[c], held.at[c], velocity.at[c]) for c in range(3)] + [(conc_in, held.at[3], conc)]
    loads = [pltpu.make_async_copy(a, b, in_sem.at[i]) for i, (a, b, _) in enumerate(pairs)]
    stores = [pltpu.make_async_copy(b, c, out_sem.at[i]) for i, (_, b, c) in enumerate(pairs)]
    for copy in loads:
        copy.start()
    for load, store in zip(loads, stores):
        load.wait()
        store.start()
    for copy in stores:
        copy.wait()


def local(force, mask, scalar):
    tables = numpy_tables()
    vm = pltpu.VMEM
    dma = pltpu.SemaphoreType.DMA
    scratch = [vm((3, 8, 64, 512), BF), vm((8, 64, 512), jnp.int32), vm((8, 64, 512), BF)]
    for name in TABLES:
        value = tables[name]
        shape = value.shape[1:] if name in VARIED else value.shape
        scratch.append(vm(shape, value.dtype))
    scratch += [
        vm((256, 256), F32), vm((256, 256), F32),
        vm((3, 8, 2, 64, 128), BF), vm((2, 3, 2, 256, 256), BF),
        vm((3, 512, 256), BF), vm((2, 3, 512, 256), BF),
        vm((3, 512, 256), BF), vm((2, 3, 512, 256), BF),
        vm((3, 2, 256, 256), BF), vm((2, 3, 8, 2, 64, 128), BF),
        vm((3, 2, 256, 256), F32), vm((3, 2, 256, 256), BF), vm((3, 2, 256, 256), BF),
        vm((512, 512), BF), vm((512, 256), BF), vm((4, 4, 2, 16, 256), F32),
        vm((512, 256), F32), vm((512, 256), F32),
        vm((3, 16, 64, 128), BF), vm((2, 3, 16, 64, 128), BF),
        vm((3, 16, 64, 128), BF), vm((2, 3, 2, 256, 256), BF),
        vm((3, 2, 256, 256), BF), vm((2, 3, 16, 64, 128), BF),
        vm((3, 16, 64, 128), BF), vm((2, 3, 16, 64, 128), BF),
        vm((3, 512, 256), F32), vm((3, 512, 256), BF), vm((3, 512, 256), BF),
        vm((512, 256), BF),
        dma((4, 3)), dma((4, 3)), dma((4, 3)), dma((4, 3)),
        vm((SECTIONS, 2, 64, 512), BF), vm((SECTIONS, 2, 64, 512), BF),
        vm((SECTIONS, 2, 8, 512), F32), vm((SECTIONS, 2, 8, 512), F32),
        vm((7, 8, 64, 512), F32), vm((2, 10, 80, 512), F32), vm((8, 64, 512), BF),
        dma((5,)), dma((len(TABLES),)),
        dma((4, 3)), dma((4, 3)), dma((4, 3)), dma((4, 3)),
        dma((SECTIONS, 2)), dma((SECTIONS, 2, 4)), dma((SECTIONS, 2)), dma((SECTIONS, 2)),
        dma((4,)),
    ]
    any_spec = pl.BlockSpec(memory_space=pl.ANY)
    velocity, conc = pl.pallas_call(
        mixer_kernel,
        out_shape=(
            jax.ShapeDtypeStruct((3, 8, 64, 512), BF),
            jax.ShapeDtypeStruct((8, 64, 512), BF),
        ),
        in_specs=[any_spec] * (3 + len(TABLES)),
        out_specs=(any_spec, any_spec),
        scratch_shapes=scratch,
        compiler_params=pltpu.CompilerParams(
            collective_id=0, has_side_effects=True, vmem_limit_bytes=62 * 1024 * 1024
        ),
        name="mixer",
    )(
        force,
        mask,
        scalar,
        *[jnp.asarray(tables[name]) for name in TABLES],
    )
    return pl.pallas_call(
        place_kernel,
        out_shape=(
            jax.ShapeDtypeStruct((3, 8, 64, 512), BF),
            jax.ShapeDtypeStruct((8, 64, 512), BF),
        ),
        in_specs=[any_spec] * 2,
        out_specs=(any_spec, any_spec),
        scratch_shapes=[vm((4, 8, 64, 512), BF), dma((4,)), dma((4,))],
        name="place",
    )(velocity, conc)


def solution(mesh):
    placed = (P(None, "col", "row", None), P("col", "row", None), P("col", "row", None))
    return jax.shard_map(
        local,
        mesh=mesh,
        in_specs=placed,
        out_specs=(P(None, "col", "row", None), P("col", "row", None)),
        check_vma=False,
    )
```

```python
import numpy as np
import jax
import jax.numpy as jnp
import ml_dtypes
from jax import lax
from jax.experimental import pallas as pl
from jax.experimental.pallas import tpu as pltpu
from jax.sharding import PartitionSpec as P

SECTIONS = 5
MESH = pl.DeviceIdType.MESH
BF = jnp.bfloat16
F32 = jnp.float32
TWO_PI = 2.0 * np.pi
PLANE_ORDER = (
    (1, 0), (3, 0), (0, 1), (0, 3), (1, 1), (3, 3), (1, 3), (3, 1),
    (2, 0), (0, 2), (2, 1), (1, 2), (2, 3), (3, 2), (2, 2),
)


def numpy_tables():
    def half(values):
        return values.astype(np.float32).astype(ml_dtypes.bfloat16)

    x = np.arange(512)
    ri, d, k = (v.reshape(-1) for v in np.meshgrid(np.arange(2), np.arange(8), np.arange(16), indexing="ij"))
    e1, ri1, k1 = (v.reshape(-1) for v in np.meshgrid(np.arange(16), np.arange(2), np.arange(8), indexing="ij"))
    m = np.concatenate([d * 32 + k, (e1 // 2) * 32 + 16 + (e1 % 2) * 8 + k1])
    ri = np.concatenate([ri, ri1])
    angle = (np.outer(x, m) % 512) * (TWO_PI / 512)
    fx = np.where(ri == 0, np.cos(angle), -np.sin(angle)) / np.sqrt(512.0)
    bx = (fx * np.where(m == 0, 1.0, 2.0)).T
    y = np.arange(256)
    angle = (np.outer(y, y) % 256) * (TWO_PI / 256)
    c, s = np.cos(angle) / 16.0, np.sin(angle) / 16.0
    real = np.concatenate([c, s], 1).reshape(16, 1, 16, 512)
    imag = np.concatenate([-s, c], 1).reshape(16, 1, 16, 512)
    ty = np.concatenate([real, imag], 1).reshape(512, 512)
    uy = np.concatenate([c, s], 1)
    uyi = np.concatenate([c, -s], 1)
    n = np.arange(16)
    angle = (np.outer(n, n) % 16) * (TWO_PI / 16)
    c, s = np.cos(angle) / 4.0, np.sin(angle) / 4.0
    cs = np.zeros((8, 256, 512))
    csi = np.zeros((8, 256, 512))
    tw = np.zeros((8, 2, 16, 256))
    k = np.arange(16)
    for d in range(8):
        for low in range(2):
            for p in range(8):
                zp = low * 8 + (p - d) % 8
                at = low * 128 + p * 16
                for k2 in range(16):
                    cs[d, at + k, k2 * 16 + k] = c[zp, k2]
                    cs[d, at + k, 256 + k2 * 16 + k] = s[zp, k2]
                    csi[d, k2 * 16 + k, at + k] = c[zp, k2]
                    csi[d, k2 * 16 + k, 256 + at + k] = s[zp, k2]
                tw[d, 0, :, at : at + 16] = np.cos(TWO_PI * zp * n / 256)[:, None] / 4.0
                tw[d, 1, :, at : at + 16] = np.sin(TWO_PI * zp * n / 256)[:, None] / 4.0
    utw = np.zeros((16, 2, 16, 128))
    uz = np.zeros((8, 256, 256))
    k = np.arange(8)
    for turn in range(8):
        for low in range(2):
            for p in range(8):
                zp = low * 8 + (p - turn) % 8
                utw[low * 8 + turn, 0, :, p * 16 : p * 16 + 16] = np.cos(TWO_PI * zp * n / 256)[:, None] / 4.0
                utw[low * 8 + turn, 1, :, p * 16 : p * 16 + 16] = np.sin(TWO_PI * zp * n / 256)[:, None] / 4.0
                at = low * 128 + p * 16
                for k2 in range(16):
                    to = k2 * 16
                    uz[turn, at + k, to + k] = c[zp, k2]
                    uz[turn, at + 8 + k, to + k] = s[zp, k2]
                    uz[turn, at + k, to + 8 + k] = -s[zp, k2]
                    uz[turn, at + 8 + k, to + 8 + k] = c[zp, k2]
    return dict(
        uy=half(uy), uyi=half(uyi), uz=half(uz), uzi=half(uz.transpose(0, 2, 1)), utw=utw.astype(np.float32),
        fx=half(fx), bx=half(bx), ty=half(ty), tyi=half(ty.T), cs=half(cs), csi=half(csi),
        tw=tw.astype(np.float32),
    )


TABLES = ("fx", "ty", "utw", "tw", "cs", "uy", "uz", "csi", "uzi", "tyi", "uyi", "bx")
BY_D = ("cs", "tw", "csi")
BY_E = ("uz", "uzi")
VARIED = BY_D + BY_E + ("utw",)


def radix4(a, sign):
    def add(u, v):
        return u[0] + v[0], u[1] + v[1]

    def sub(u, v):
        return u[0] - v[0], u[1] - v[1]

    t0, t1 = add(a[0], a[2]), sub(a[0], a[2])
    t2, t3 = add(a[1], a[3]), sub(a[1], a[3])
    t3 = (t3[1], -t3[0]) if sign > 0 else (-t3[1], t3[0])
    return add(t0, t2), add(t1, t3), sub(t0, t2), sub(t1, t3)


def turned_by(value, j, sign):
    if j == 0:
        return value
    c, s = float(np.cos(TWO_PI * j / 16)), float(np.sin(TWO_PI * j / 16)) * sign
    re, im = value
    return re * c + im * s, im * c - re * s


def times_minus_i(value):
    imag = (lax.broadcasted_iota(jnp.int32, value.shape, 1) & 8) != 0
    return jnp.where(imag, -pltpu.roll(value, 8, 1), pltpu.roll(value, 120, 1))


def packed_radix4(a, sign):
    t0, t1, t2 = a[0] + a[2], a[0] - a[2], a[1] + a[3]
    t3 = times_minus_i(a[1] - a[3])
    if sign < 0:
        t3 = -t3
    return t0 + t2, t1 + t3, t0 - t2, t1 - t3


def packed_turned(value, j, sign):
    if j == 0:
        return value
    c, s = float(np.cos(TWO_PI * j / 16)), float(np.sin(TWO_PI * j / 16)) * sign
    return value * c + times_minus_i(value) * s


def packed_dft16(values, sign):
    parts = [packed_radix4(values[low::4], sign) for low in range(4)]
    parts = [[packed_turned(v, low * k, sign) for k, v in enumerate(parts[low])] for low in range(4)]
    out = [None] * 16
    for k in range(4):
        out[k::4] = packed_radix4([parts[low][k] for low in range(4)], sign)
    return out


def merge(tiles, place):
    for bit in (1, 2, 4):
        take = (place & bit) != 0
        tiles = [jnp.where(take, tiles[(m + bit) % 8], tiles[m]) for m in range(8)]
    return tiles


def dot(a, b):
    return jnp.dot(a, b, preferred_element_type=F32)


def mixer_kernel(*refs):
    force_h, mask_h, scalar_h = refs[:3]
    count = len(TABLES)
    tables_h = dict(zip(TABLES, refs[3 : 3 + count]))
    velocity_h, conc_h = refs[3 + count : 5 + count]
    (field, mask, scalar, *rest) = refs[5 + count :]
    tab = dict(zip(TABLES, rest[:count]))
    (gain, inv, sa, ra, sb, rb, sbi, rbi, sai, rai, spec, first, second, lines, big, mid,
     gain1, inv1, su, ru, sv, rv, svi, rvi, sui, rui, spec1, first1, second1, stacked, dots, dots1, summed,
     u_send, u_recv, v_send, v_recv,
     zsend, zrecv, ysend, yrecv, edge, coef, state, conc,
     in_sem, tab_sem, a_send, a_recv, b_send, b_recv, z_ssem, z_rsem, y_ssem, y_rsem, out_sem) = rest[count:]

    r = lax.axis_index("row")
    col = lax.axis_index("col")
    e = col // 2
    xl = col % 2
    d = xl * 4 + r

    def load(source, target, sem):
        copy = pltpu.make_async_copy(source, target, sem)
        copy.start()
        return copy

    def load_table(name):
        source = tables_h[name]
        sem = tab_sem.at[TABLES.index(name)]
        if name in VARIED:
            source = source.at[d if name in BY_D else (e & 7) + (8 * xl if name == "utw" else 0)]
        return load(source, tab[name], sem)

    loads = {0: load(force_h.at[0], field.at[0], in_sem.at[0]), "fx": load_table("fx")}
    for i in (1, 2):
        loads[i] = load(force_h.at[i], field.at[i], in_sem.at[i])
    loads["scalar"] = load(scalar_h, scalar, in_sem.at[4])
    for name in TABLES[1:]:
        loads[name] = load_table(name)
    loads["mask"] = load(mask_h, mask, in_sem.at[3])

    core = r & 1
    x = (r // 2) * 2 + xl
    y_at, z_at = e // 4, e & 3

    def x_peer(step, of_core):
        at = (x + step * (1 + 2 * core)) & 3
        low = at & 1
        row = (at - low) + of_core
        return low * 4 + row, (row, e * 2 + low)

    def plane_peer(dy, dz):
        to = ((y_at + dy + core * (3 * dz - dy)) & 3) * 4 + ((z_at + dz + core * (3 * dy - dz)) & 3)
        return to, (r, to * 2 + xl)

    x_peers = [
        x_peer(step, core if same else 1 - core)
        for step, same in ((1, 1), (3, 1), (1, 0), (3, 0), (2, 1), (2, 0), (0, 0))
    ]
    plane_peers = [plane_peer(dy, dz) for dy, dz in PLANE_ORDER]

    z_up = (r, lax.rem(col + 1, 32))
    z_down = (r, lax.rem(col + 31, 32))
    y_up = (lax.rem(r + 1, 4), col)
    y_down = (lax.rem(r + 3, 4), col)

    barrier = pltpu.get_barrier_semaphore()

    for _, device in x_peers + plane_peers:
        pl.semaphore_signal(barrier, inc=1, device_id=device, device_id_type=MESH)
    across = (r, lax.rem(col + 31 + 2 * xl, 32))
    pl.semaphore_signal(barrier, inc=1, device_id=across, device_id_type=MESH)
    pl.semaphore_wait(barrier, 23)

    def remote(source, target, ssem, rsem, device):
        return pltpu.make_async_remote_copy(
            src_ref=source, dst_ref=target, send_sem=ssem, recv_sem=rsem,
            device_id=device, device_id_type=MESH)

    my_rows = pl.ds(pl.multiple_of(r * 64, 64), 64)
    my_lanes = pl.ds(pl.multiple_of(xl * 128, 128), 128)
    my_slab = pl.ds(pl.multiple_of(e * 32, 32), 32)

    def send_a(t, i):
        target = ra.at[t, i, :, my_rows, my_lanes]
        recv = a_recv.at[2 * t, i]

        for to, device in x_peers:
            remote(sa.at[i, to], target, a_send.at[2 * t, i], recv, device).start()
        pltpu.make_async_copy(sa.at[i, d], target, recv).start()

    def send_ai(t, i):
        target = rai.at[t, i, d]
        recv = a_recv.at[2 * t + 1, i]

        def piece(to):
            rows = pl.ds(pl.multiple_of((to & 3) * 64, 64), 64)
            lanes = pl.ds(pl.multiple_of((to // 4) * 128, 128), 128)
            return sai.at[i, :, rows, lanes]

        for to, device in x_peers:
            remote(piece(to), target, a_send.at[2 * t + 1, i], recv, device).start()
        pltpu.make_async_copy(piece(d), target, recv).start()

    def send_b(source, into, k, t, i):
        target = into.at[t, i, my_slab]
        recv = b_recv.at[k, i]

        for to, device in plane_peers:
            slab = source.at[i, pl.ds(pl.multiple_of(to * 32, 32), 32)]
            remote(slab, target, b_send.at[k, i], recv, device).start()
        pltpu.make_async_copy(source.at[i, my_slab], target, recv).start()

    def send_u(source, into, k, t, c):
        target = into.at[t, c, e]
        recv = u_recv.at[k, c]
        for to, device in plane_peers:
            remote(source.at[c, to], target, u_send.at[k, c], recv, device).start()
        pltpu.make_async_copy(source.at[c, e], target, recv).start()

    def send_v(t, c):
        target = rv.at[t, c, :, my_rows, my_lanes]
        recv = v_recv.at[2 * t, c]
        for to, device in x_peers:
            remote(sv.at[c, pl.ds(2 * to, 2)], target, v_send.at[2 * t, c], recv, device).start()
        pltpu.make_async_copy(sv.at[c, pl.ds(2 * d, 2)], target, recv).start()

    def send_vi(t, c):
        target = rvi.at[t, c, pl.ds(2 * d, 2)]
        recv = v_recv.at[2 * t + 1, c]

        def piece(to):
            rows = pl.ds(pl.multiple_of((to & 3) * 64, 64), 64)
            lanes = pl.ds(pl.multiple_of((to // 4) * 128, 128), 128)
            return svi.at[c, :, rows, lanes]

        for to, device in x_peers:
            remote(piece(to), target, v_send.at[2 * t + 1, c], recv, device).start()
        pltpu.make_async_copy(piece(d), target, recv).start()

    def arrived(buffer, sem):
        pltpu.make_async_copy(buffer, buffer, sem).wait()

    def sent_a(k, i):
        arrived(sa.at[i, pl.ds(0, 7)], a_send.at[k, i])

    def sent_b(k, i):
        arrived(sb.at[i, pl.ds(0, 480)], b_send.at[k, i])

    def sent_u(k, i):
        arrived(su.at[i, pl.ds(0, 15)], u_send.at[k, i])

    def sent_v(k, i):
        arrived(sv.at[i, pl.ds(0, 14)], v_send.at[k, i])

    def send_z(s, q):
        rows = pl.ds(16 * q, 16)
        for side, device in ((0, z_down), (1, z_up)):
            remote(zsend.at[s, side, rows], zrecv.at[s, 1 - side, rows],
                   z_ssem.at[s, side], z_rsem.at[s, 1 - side, q], device).start()

    def pack_edge(s, side):
        value = edge[...]
        ysend[s, side] = jnp.concatenate([value[:, 0:256], value[:, 256:512]], axis=0).astype(BF)

    def send_y(s, side):
        remote(ysend.at[s, side], yrecv.at[s, 1 - side], y_ssem.at[s, side], y_rsem.at[s, 1 - side],
               (y_down, y_up)[side]).start()

    place = lax.broadcasted_iota(jnp.int32, (64, 128), 1) // 16

    def x_forward(t, c):
        spread = dot(field[c].reshape(512, 512), tab["fx"][:, 0:256])
        for ri in range(2):
            tiles = []
            for z in range(8):
                tile = spread[z * 64 : z * 64 + 64, ri * 128 : ri * 128 + 128]
                tiles.append(pltpu.roll(tile, 16 * z, 1) if z else tile)
            tiles = merge(tiles, place)
            for to in range(8):
                sa[c, to, ri] = tiles[-to % 8].astype(BF)
        send_a(t, c)

    def x_forward1(t, c):
        spread = dot(field[c].reshape(512, 512), tab["fx"][:, 256:512])
        for j in range(2):
            tiles = []
            for z in range(8):
                tile = spread[z * 64 : z * 64 + 64, j * 128 : j * 128 + 128]
                tiles.append(pltpu.roll(tile, 16 * z, 1) if z else tile)
            tiles = merge(tiles, place)
            for to in range(8):
                su[c, 8 * j + to] = tiles[-to % 8].astype(BF)
        send_u(su, ru, 2 * t, t, c)

    def x_inverse(t, c):
        def gather(j):
            if j < 2:
                tiles = [rai[t, c, source, j].astype(F32) for source in range(8)]
            else:
                tiles = [rui[t, c, 8 * (j - 2) + source].astype(F32) for source in range(8)]
            tiles = merge(tiles, place)
            for z in range(8):
                tile = tiles[-z % 8]
                tile = pltpu.roll(tile, 128 - 16 * z, 1) if z else tile
                lines[z * 64 : z * 64 + 64, j * 128 : j * 128 + 128] = tile.astype(BF)

        arrived(rai.at[t, c], a_recv.at[2 * t + 1, c])
        gather(0)
        gather(1)
        summed[...] = dot(lines[:, 0:256], tab["bx"][0:256, :])
        arrived(rui.at[t, c], u_recv.at[2 * t + 1, c])
        gather(2)
        gather(3)
        values = (summed[...] + dot(lines[:, 256:512], tab["bx"][256:512, :])).astype(BF).reshape(8, 64, 512)
        if t == 0:
            values = (values.astype(F32) * mask[...].astype(F32)).astype(BF)
        field[c] = values

    def y_forward(t, i):
        arrived(ra.at[t, i], a_recv.at[2 * t, i])
        sb[i] = dot(tab["ty"][...], ra[t, i].reshape(512, 256)).astype(BF)
        send_b(sb, rb, 2 * t, t, i)

    def y_inverse(t, i):
        arrived(rbi.at[t, i], b_recv.at[2 * t + 1, i])
        sai[i] = dot(tab["tyi"][...], rbi[t, i]).astype(BF).reshape(2, 256, 256)
        send_ai(t, i)

    def z_forward(t, i):
        arrived(rb.at[t, i], b_recv.at[2 * t, i])
        for half in range(2):
            lanes = slice(half * 128, half * 128 + 128)

            def source(e_from, ri):
                return rb[t, i, e_from * 32 + ri * 16 : e_from * 32 + ri * 16 + 16, lanes].astype(F32)

            for low in range(4):
                out = radix4([(source(low + 4 * j, 0), source(low + 4 * j, 1)) for j in range(4)], 1)
                for k, value in enumerate(out):
                    mid[low, k, 0, :, lanes], mid[low, k, 1, :, lanes] = turned_by(value, low * k, 1)
            for k in range(4):
                out = radix4([(mid[low, k, 0, :, lanes], mid[low, k, 1, :, lanes]) for low in range(4)], 1)
                for high, (re, im) in enumerate(out):
                    k1 = k + 4 * high
                    wc, ws = tab["tw"][0, k1 : k1 + 1, lanes], tab["tw"][1, k1 : k1 + 1, lanes]
                    big[k1 * 16 : k1 * 16 + 16, lanes] = (re * wc + im * ws).astype(BF)
                    big[256 + k1 * 16 : 256 + k1 * 16 + 16, lanes] = (im * wc - re * ws).astype(BF)
        both = dot(big[...], tab["cs"][...])
        spec[i, 0] = both[:256, :256] + both[256:, 256:]
        spec[i, 1] = both[256:, :256] - both[:256, 256:]

    def z_inverse(source, t, i):
        both = dot(source[i].reshape(512, 256), tab["csi"][...])
        for half in range(2):
            lanes = slice(half * 128, half * 128 + 128)
            other = slice(256 + half * 128, 256 + half * 128 + 128)

            def value(k1):
                upper, lower = slice(k1 * 16, k1 * 16 + 16), slice(256 + k1 * 16, 256 + k1 * 16 + 16)
                re = both[upper, lanes] - both[lower, other]
                im = both[lower, lanes] + both[upper, other]
                wc, ws = tab["tw"][0, k1 : k1 + 1, lanes], tab["tw"][1, k1 : k1 + 1, lanes]
                return re * wc - im * ws, im * wc + re * ws

            for low in range(4):
                out = radix4([value(low + 4 * j) for j in range(4)], -1)
                for k, turned in enumerate(out):
                    mid[low, k, 0, :, lanes], mid[low, k, 1, :, lanes] = turned_by(turned, low * k, -1)
            for k in range(4):
                out = radix4([(mid[low, k, 0, :, lanes], mid[low, k, 1, :, lanes]) for low in range(4)], -1)
                for high, (re, im) in enumerate(out):
                    to = (k + 4 * high) * 32
                    sbi[i, to : to + 16, lanes] = re.astype(BF)
                    sbi[i, to + 16 : to + 32, lanes] = im.astype(BF)
        send_b(sbi, rbi, 2 * t + 1, t, i)

    def v_forward(t, c):
        arrived(ru.at[t, c], u_recv.at[2 * t, c])

        def some(n, carry):
            rows = pl.ds(pl.multiple_of(n * 16, 16), 16)
            out = packed_dft16([ru[t, c, j, rows].astype(F32) for j in range(16)], 1)
            for k1, value in enumerate(out):
                wc, ws = tab["utw"][0, k1 : k1 + 1], tab["utw"][1, k1 : k1 + 1]
                sv[c, k1, rows] = (value * wc + times_minus_i(value) * ws).astype(BF)
            return carry

        lax.fori_loop(0, 4, some, 0)
        send_v(t, c)

    def v_inverse(t, c):
        arrived(rvi.at[t, c], v_recv.at[2 * t + 1, c])

        def some(n, carry):
            rows = pl.ds(pl.multiple_of(n * 16, 16), 16)
            values = []
            for k1 in range(16):
                value = rvi[t, c, k1, rows].astype(F32)
                wc, ws = tab["utw"][0, k1 : k1 + 1], tab["utw"][1, k1 : k1 + 1]
                values.append(value * wc - times_minus_i(value) * ws)
            for j, value in enumerate(packed_dft16(values, -1)):
                sui[c, j, rows] = value.astype(BF)
            return carry

        lax.fori_loop(0, 4, some, 0)
        send_u(sui, rui, 2 * t + 1, t, c)

    def y_product(table, values, wide):
        for half in range(2):
            lanes = slice(half * 128, half * 128 + 128)
            stacked[256:512, lanes] = times_minus_i(wide[:, lanes]).astype(BF)
        stacked[0:256, :] = values
        return dot(table, stacked[...]).astype(BF)

    def w_forward(t, c):
        arrived(rv.at[t, c], v_recv.at[2 * t, c])
        for k1 in range(2):
            values = rv[t, c, k1]
            big[k1 * 256 : k1 * 256 + 256, :] = y_product(tab["uy"][...], values, values.astype(F32))
        spec1[c] = dot(big[...], tab["uz"][...])

    def w_inverse(source, t, c):
        wide = dot(source[c], tab["uzi"][...])
        for k1 in range(2):
            part = wide[k1 * 256 : k1 * 256 + 256]
            svi[c, k1] = y_product(tab["uyi"][...], part.astype(BF), part)
        send_vi(t, c)

    lane = lax.broadcasted_iota(jnp.int32, (16, 256), 1)
    unit_long, unit = np.float32(TWO_PI / 512), np.float32(TWO_PI / 256)
    index_y = e * 16 + lax.broadcasted_iota(jnp.int32, (16, 256), 0)
    wave_y = jnp.where(index_y < 128, index_y, index_y - 256).astype(F32) * unit

    wave_x = (d * 32 + (lane & 15)).astype(F32) * unit_long
    wave_x1 = ((e // 2) * 32 + 16 + (e & 1) * 8 + (lane & 7)).astype(F32) * unit_long

    def along_z(k1):
        index_z = k1 + 16 * (lane // 16)
        return index_z, jnp.where(index_z < 128, index_z, index_z - 256).astype(F32) * unit

    def at_rows(n):
        return pl.ds(pl.multiple_of(n * 16, 16), 16)

    def along_y1(n):
        index = (n & 15) * 16 + lax.broadcasted_iota(jnp.int32, (16, 256), 0)
        return index, jnp.where(index < 128, index, index - 256).astype(F32) * unit

    def scales(kx, ky, kz, edge):
        ksq = kx * kx + ky * ky + kz * kz
        return (
            jnp.where(edge, 0.0, 1.0 / (0.05 * ksq + 0.5)),
            jnp.where(ksq > 0.0, 1.0 / jnp.where(ksq > 0.0, ksq, 1.0), 0.0),
        )

    def factors(n, carry):
        index_z, wave_z = along_z(n)
        gain[at_rows(n)], inv[at_rows(n)] = scales(wave_x, wave_y, wave_z, (index_y == 128) | (index_z == 128))
        return carry

    def factors1(n, carry):
        index_z, wave_z = along_z(2 * d + n // 16)
        index, wave = along_y1(n)
        gain1[at_rows(n)], inv1[at_rows(n)] = scales(wave_x1, wave, wave_z, (index == 128) | (index_z == 128))
        return carry

    def parts():
        def one(n, carry):
            rows = at_rows(n)
            for ri in range(2):
                dots[ri, rows] = wave_x * spec[0, ri, rows] + wave_y * spec[1, ri, rows]
            return carry

        lax.fori_loop(0, 16, one, 0)

    def keep(t, kept, result, at, value):
        if t == 0:
            kept[at] = value.astype(BF)
        else:
            result[at] = (kept[at].astype(F32) - value).astype(BF)

    def project_x(t):
        def one(n, carry):
            rows = at_rows(n)
            wave_z = along_z(n)[1]
            for ri in range(2):
                along = (dots[ri, rows] + wave_z * spec[2, ri, rows]) * inv[rows]
                dots[ri, rows] = along
                keep(t, first, second, (0, ri, rows), gain[rows] * (spec[0, ri, rows] - wave_x * along))
            return carry

        lax.fori_loop(0, 16, one, 0)

    def project_yz(t):
        def one(n, carry):
            rows = at_rows(n)
            waves = (wave_x, wave_y, along_z(n)[1])
            for ri in range(2):
                along = dots[ri, rows]
                for c in (1, 2):
                    keep(t, first, second, (c, ri, rows), gain[rows] * (spec[c, ri, rows] - waves[c] * along))
            return carry

        lax.fori_loop(0, 16, one, 0)

    def parts1():
        def one(n, carry):
            rows = at_rows(n)
            dots1[rows] = wave_x1 * spec1[0, rows] + along_y1(n)[1] * spec1[1, rows]
            return carry

        lax.fori_loop(0, 32, one, 0)

    def project1_x(t):
        def one(n, carry):
            rows = at_rows(n)
            along = (dots1[rows] + along_z(2 * d + n // 16)[1] * spec1[2, rows]) * inv1[rows]
            dots1[rows] = along
            keep(t, first1, second1, (0, rows), gain1[rows] * (spec1[0, rows] - wave_x1 * along))
            return carry

        lax.fori_loop(0, 32, one, 0)

    def project1_yz(t):
        def one(n, carry):
            rows = at_rows(n)
            waves = (wave_x1, along_y1(n)[1], along_z(2 * d + n // 16)[1])
            along = dots1[rows]
            for c in (1, 2):
                keep(t, first1, second1, (c, rows), gain1[rows] * (spec1[c, rows] - waves[c] * along))
            return carry

        lax.fori_loop(0, 32, one, 0)

    def each(count, step):
        def body(i, _):
            step(i)
            return _

        lax.fori_loop(0, count, body, 0)

    def spectral(t, source, source1):
        def out(c):
            y_forward(t, c)
            v_forward(t, c)

        def inner(c):
            w_forward(t, c)
            z_forward(t, c)

        def outer(c):
            w_inverse(source1, t, c + 1)
            z_inverse(source, t, c + 1)

        def back(c):
            v_inverse(t, c)
            y_inverse(t, c)

        each(3, out)
        each(2, inner)
        parts1()
        parts()
        w_forward(t, 2)
        project1_x(t)
        w_inverse(source1, t, 0)
        z_forward(t, 2)
        project_x(t)
        z_inverse(source, t, 0)
        project1_yz(t)
        project_yz(t)
        each(2, outer)
        each(3, back)

    loads["fx"].wait()
    for i in range(3):
        loads[i].wait()
    def start(c):
        x_forward(0, c)
        x_forward1(0, c)

    each(3, start)
    lax.fori_loop(0, 16, factors, 0)
    lax.fori_loop(0, 32, factors1, 0)
    loads["scalar"].wait()
    for z in range(8):
        state[0, z + 1, pl.ds(8, 64), :] = scalar[z].astype(F32)
    zsend[0, 0] = scalar[0]
    zsend[0, 1] = scalar[7]
    for q in range(4):
        send_z(0, q)
    for side in range(2):
        for z in range(8):
            edge[pl.ds(z, 1), :] = state[0, z + 1, pl.ds(8 + 63 * side, 1), :]
        pack_edge(0, side)
        send_y(0, side)
    for name in TABLES[1:]:
        loads[name].wait()
    loads["mask"].wait()
    spectral(0, first, first1)

    def sent(t, c):
        for k in (2 * t, 2 * t + 1):
            sent_a(k, c)
            sent_b(k, c)
            sent_u(k, c)
            sent_v(k, c)

    def middle(c):
        x_inverse(0, c)
        sent(0, c)
        x_forward(1, c)
        x_forward1(1, c)

    each(3, middle)
    spectral(1, second, second1)

    def coefficients(z, c):
        fluid = 0.25 * (1.0 - mask[z].astype(F32))
        u = field[c, z].astype(F32)
        below = fluid * (0.25 + jnp.maximum(u, 0.0))
        above = fluid * (0.25 - jnp.minimum(u, 0.0))
        coef[2 * c, z] = below
        coef[2 * c + 1, z] = above
        start = jnp.where(c == 0, jnp.ones_like(u), coef[6, z])
        coef[6, z] = start - (below + above)
        return c

    def last(c):
        x_inverse(1, c)
        pltpu.make_async_copy(field.at[c], velocity_h.at[c], out_sem.at[c]).start()
        lax.fori_loop(0, 8, coefficients, c)
        sent(1, c)

    each(3, last)

    def section(s, carry):
        now, later = s & 1, (s + 1) & 1

        def block(z, q, below_z, above_z):
            at = 8 + 16 * q
            rows, cells = pl.ds(at, 16), pl.ds(16 * q, 16)
            center = state[now, z, rows]
            new = coef[6, z - 1, cells] * center
            new = new + coef[0, z - 1, cells] * pltpu.roll(center, 1, 1)
            new = new + coef[1, z - 1, cells] * pltpu.roll(center, 511, 1)
            new = new + coef[2, z - 1, cells] * state[now, z, pl.ds(at - 1, 16)]
            new = new + coef[3, z - 1, cells] * state[now, z, pl.ds(at + 1, 16)]
            new = new + coef[4, z - 1, cells] * below_z + coef[5, z - 1, cells] * above_z
            state[later, z, rows] = new
            return new

        for q in (1, 2, 0, 3):
            rows, cells = pl.ds(8 + 16 * q, 16), pl.ds(16 * q, 16)
            if q in (0, 3):
                side = q // 3
                arrived(yrecv.at[s, side], y_rsem.at[s, side])
                halo = yrecv[s, side].astype(F32)
                for z in range(8):
                    for half in range(2):
                        lanes = slice(half * 256, half * 256 + 256)
                        state[now, z + 1, pl.ds(7 + 65 * side, 1), lanes] = halo[8 * half + z : 8 * half + z + 1]
            for side in range(2):
                arrived(zrecv.at[s, side, cells], z_rsem.at[s, side, q])
            bottom = block(1, q, zrecv[s, 0, cells].astype(F32), state[now, 2, rows])
            top = block(8, q, state[now, 7, rows], zrecv[s, 1, cells].astype(F32))

            @pl.when(s < SECTIONS - 1)
            def _():
                zsend[s + 1, 0, cells] = bottom.astype(BF)
                zsend[s + 1, 1, cells] = top.astype(BF)
                send_z(s + 1, q)

            for z in range(2, 8):
                block(z, q, state[now, z - 1, rows], state[now, z + 1, rows])
            if q in (0, 3):
                side = q // 3

                @pl.when(s < SECTIONS - 1)
                def _():
                    for z in range(8):
                        edge[pl.ds(z, 1), :] = state[later, z + 1, pl.ds(8 + 63 * side, 1), :]
                    pack_edge(s + 1, side)
                    send_y(s + 1, side)
        return carry

    lax.fori_loop(0, SECTIONS, section, 0)
    for z in range(8):
        conc[z] = state[SECTIONS % 2, z + 1, pl.ds(8, 64), :].astype(BF)

    for s in range(SECTIONS):
        for i in range(2):
            arrived(zsend.at[s, i], z_ssem.at[s, i])
            arrived(ysend.at[s, i], y_ssem.at[s, i])
    out = pltpu.make_async_copy(conc, conc_h, out_sem.at[3])
    out.start()
    for c in range(3):
        pltpu.make_async_copy(field.at[c], velocity_h.at[c], out_sem.at[c]).wait()
    out.wait()


def place_kernel(velocity_in, conc_in, velocity, conc, held, in_sem, out_sem):
    pairs = []
    for half in range(2):
        planes = pl.ds(4 * half, 4)
        pairs += [(velocity_in.at[c, planes], held.at[c, planes], velocity.at[c, planes]) for c in range(3)]
        pairs.append((conc_in.at[planes], held.at[3, planes], conc.at[planes]))
    loads = [pltpu.make_async_copy(a, b, in_sem.at[i]) for i, (a, b, _) in enumerate(pairs)]
    stores = [pltpu.make_async_copy(b, c, out_sem.at[i]) for i, (_, b, c) in enumerate(pairs)]
    for copy in loads:
        copy.start()
    for load, store in zip(loads, stores):
        load.wait()
        store.start()
    for copy in stores:
        copy.wait()


def local(force, mask, scalar):
    tables = numpy_tables()
    vm = pltpu.VMEM
    dma = pltpu.SemaphoreType.DMA
    scratch = [vm((3, 8, 64, 512), BF), vm((8, 64, 512), jnp.int32), vm((8, 64, 512), BF)]
    for name in TABLES:
        value = tables[name]
        shape = value.shape[1:] if name in VARIED else value.shape
        scratch.append(vm(shape, value.dtype))
    scratch += [
        vm((256, 256), F32), vm((256, 256), F32),
        vm((3, 8, 2, 64, 128), BF), vm((2, 3, 2, 256, 256), BF),
        vm((3, 512, 256), BF), vm((2, 3, 512, 256), BF),
        vm((3, 512, 256), BF), vm((2, 3, 512, 256), BF),
        vm((3, 2, 256, 256), BF), vm((2, 3, 8, 2, 64, 128), BF),
        vm((3, 2, 256, 256), F32), vm((3, 2, 256, 256), BF), vm((3, 2, 256, 256), BF),
        vm((512, 512), BF), vm((512, 256), BF), vm((4, 4, 2, 16, 256), F32),
        vm((512, 256), F32), vm((512, 256), F32),
        vm((3, 16, 64, 128), BF), vm((2, 3, 16, 64, 128), BF),
        vm((3, 16, 64, 128), BF), vm((2, 3, 2, 256, 256), BF),
        vm((3, 2, 256, 256), BF), vm((2, 3, 16, 64, 128), BF),
        vm((3, 16, 64, 128), BF), vm((2, 3, 16, 64, 128), BF),
        vm((3, 512, 256), F32), vm((3, 512, 256), BF), vm((3, 512, 256), BF),
        vm((512, 256), BF), vm((2, 256, 256), F32), vm((512, 256), F32),
        vm((512, 512), F32),
        dma((4, 3)), dma((4, 3)), dma((4, 3)), dma((4, 3)),
        vm((SECTIONS, 2, 64, 512), BF), vm((SECTIONS, 2, 64, 512), BF),
        vm((SECTIONS, 2, 16, 256), BF), vm((SECTIONS, 2, 16, 256), BF), vm((8, 512), F32),
        vm((7, 8, 64, 512), F32), vm((2, 10, 80, 512), F32), vm((8, 64, 512), BF),
        dma((5,)), dma((len(TABLES),)),
        dma((4, 3)), dma((4, 3)), dma((4, 3)), dma((4, 3)),
        dma((SECTIONS, 2)), dma((SECTIONS, 2, 4)), dma((SECTIONS, 2)), dma((SECTIONS, 2)),
        dma((4,)),
    ]
    any_spec = pl.BlockSpec(memory_space=pl.ANY)
    velocity, conc = pl.pallas_call(
        mixer_kernel,
        out_shape=(
            jax.ShapeDtypeStruct((3, 8, 64, 512), BF),
            jax.ShapeDtypeStruct((8, 64, 512), BF),
        ),
        in_specs=[any_spec] * (3 + len(TABLES)),
        out_specs=(any_spec, any_spec),
        scratch_shapes=scratch,
        compiler_params=pltpu.CompilerParams(
            collective_id=0, has_side_effects=True, vmem_limit_bytes=62 * 1024 * 1024
        ),
        name="mixer",
    )(
        force,
        mask,
        scalar,
        *[jnp.asarray(tables[name]) for name in TABLES],
    )
    return pl.pallas_call(
        place_kernel,
        out_shape=(
            jax.ShapeDtypeStruct((3, 8, 64, 512), BF),
            jax.ShapeDtypeStruct((8, 64, 512), BF),
        ),
        in_specs=[any_spec] * 2,
        out_specs=(any_spec, any_spec),
        scratch_shapes=[vm((4, 8, 64, 512), BF), dma((8,)), dma((8,))],
        name="place",
    )(velocity, conc)


def solution(mesh):
    placed = (P(None, "col", "row", None), P("col", "row", None), P("col", "row", None))
    return jax.shard_map(
        local,
        mesh=mesh,
        in_specs=placed,
        out_specs=(P(None, "col", "row", None), P("col", "row", None)),
        check_vma=False,
    )
```

```python
import numpy as np
import jax
import jax.numpy as jnp
import ml_dtypes
from jax import lax
from jax.experimental import pallas as pl
from jax.experimental.pallas import tpu as pltpu
from jax.sharding import PartitionSpec as P

SECTIONS = 5
MESH = pl.DeviceIdType.MESH
BF = jnp.bfloat16
F32 = jnp.float32
TWO_PI = 2.0 * np.pi
PLANE_ORDER = (
    (1, 0), (3, 0), (0, 1), (0, 3), (1, 1), (3, 3), (1, 3), (3, 1),
    (2, 0), (0, 2), (2, 1), (1, 2), (2, 3), (3, 2), (2, 2),
)


def numpy_tables():
    def half(values):
        return values.astype(np.float32).astype(ml_dtypes.bfloat16)

    x = np.arange(512)
    ri, d, k = (v.reshape(-1) for v in np.meshgrid(np.arange(2), np.arange(8), np.arange(16), indexing="ij"))
    e1, ri1, k1 = (v.reshape(-1) for v in np.meshgrid(np.arange(16), np.arange(2), np.arange(8), indexing="ij"))
    m = np.concatenate([d * 32 + k, (e1 // 2) * 32 + 16 + (e1 % 2) * 8 + k1])
    ri = np.concatenate([ri, ri1])
    angle = (np.outer(x, m) % 512) * (TWO_PI / 512)
    fx = np.where(ri == 0, np.cos(angle), -np.sin(angle)) / np.sqrt(512.0)
    bx = (fx * np.where(m == 0, 1.0, 2.0)).T
    y = np.arange(256)
    angle = (np.outer(y, y) % 256) * (TWO_PI / 256)
    c, s = np.cos(angle) / 16.0, np.sin(angle) / 16.0
    real = np.concatenate([c, s], 1).reshape(16, 1, 16, 512)
    imag = np.concatenate([-s, c], 1).reshape(16, 1, 16, 512)
    ty = np.concatenate([real, imag], 1).reshape(512, 512)
    uy = np.concatenate([c, s], 1)
    uyi = np.concatenate([c, -s], 1)
    n = np.arange(16)
    angle = (np.outer(n, n) % 16) * (TWO_PI / 16)
    c, s = np.cos(angle) / 4.0, np.sin(angle) / 4.0
    cs = np.zeros((8, 256, 512))
    csi = np.zeros((8, 256, 512))
    tw = np.zeros((8, 2, 16, 256))
    k = np.arange(16)
    for d in range(8):
        for low in range(2):
            for p in range(8):
                zp = low * 8 + (p - d) % 8
                at = low * 128 + p * 16
                for k2 in range(16):
                    cs[d, at + k, k2 * 16 + k] = c[zp, k2]
                    cs[d, at + k, 256 + k2 * 16 + k] = s[zp, k2]
                    csi[d, k2 * 16 + k, at + k] = c[zp, k2]
                    csi[d, k2 * 16 + k, 256 + at + k] = s[zp, k2]
                tw[d, 0, :, at : at + 16] = np.cos(TWO_PI * zp * n / 256)[:, None] / 4.0
                tw[d, 1, :, at : at + 16] = np.sin(TWO_PI * zp * n / 256)[:, None] / 4.0
    utw = np.zeros((16, 2, 16, 128))
    uz = np.zeros((8, 256, 256))
    k = np.arange(8)
    for turn in range(8):
        for low in range(2):
            for p in range(8):
                zp = low * 8 + (p - turn) % 8
                utw[low * 8 + turn, 0, :, p * 16 : p * 16 + 16] = np.cos(TWO_PI * zp * n / 256)[:, None] / 4.0
                utw[low * 8 + turn, 1, :, p * 16 : p * 16 + 16] = np.sin(TWO_PI * zp * n / 256)[:, None] / 4.0
                at = low * 128 + p * 16
                for k2 in range(16):
                    to = k2 * 16
                    uz[turn, at + k, to + k] = c[zp, k2]
                    uz[turn, at + 8 + k, to + k] = s[zp, k2]
                    uz[turn, at + k, to + 8 + k] = -s[zp, k2]
                    uz[turn, at + 8 + k, to + 8 + k] = c[zp, k2]
    return dict(
        uy=half(uy), uyi=half(uyi), uz=half(uz), uzi=half(uz.transpose(0, 2, 1)), utw=utw.astype(np.float32),
        fx=half(fx), bx=half(bx), ty=half(ty), tyi=half(ty.T), cs=half(cs), csi=half(csi),
        tw=tw.astype(np.float32),
    )


TABLES = ("fx", "ty", "utw", "tw", "cs", "uy", "uz", "csi", "uzi", "tyi", "uyi", "bx")
BY_D = ("cs", "tw", "csi")
BY_E = ("uz", "uzi")
VARIED = BY_D + BY_E + ("utw",)


def radix4(a, sign):
    def add(u, v):
        return u[0] + v[0], u[1] + v[1]

    def sub(u, v):
        return u[0] - v[0], u[1] - v[1]

    t0, t1 = add(a[0], a[2]), sub(a[0], a[2])
    t2, t3 = add(a[1], a[3]), sub(a[1], a[3])
    t3 = (t3[1], -t3[0]) if sign > 0 else (-t3[1], t3[0])
    return add(t0, t2), add(t1, t3), sub(t0, t2), sub(t1, t3)


def turned_by(value, j, sign):
    if j == 0:
        return value
    c, s = float(np.cos(TWO_PI * j / 16)), float(np.sin(TWO_PI * j / 16)) * sign
    re, im = value
    return re * c + im * s, im * c - re * s


def times_minus_i(value):
    imag = (lax.broadcasted_iota(jnp.int32, value.shape, 1) & 8) != 0
    return jnp.where(imag, -pltpu.roll(value, 8, 1), pltpu.roll(value, 120, 1))


def packed_radix4(a, sign):
    t0, t1, t2 = a[0] + a[2], a[0] - a[2], a[1] + a[3]
    t3 = times_minus_i(a[1] - a[3])
    if sign < 0:
        t3 = -t3
    return t0 + t2, t1 + t3, t0 - t2, t1 - t3


def packed_turned(value, j, sign):
    if j == 0:
        return value
    c, s = float(np.cos(TWO_PI * j / 16)), float(np.sin(TWO_PI * j / 16)) * sign
    return value * c + times_minus_i(value) * s


def packed_dft16(values, sign):
    parts = [packed_radix4(values[low::4], sign) for low in range(4)]
    parts = [[packed_turned(v, low * k, sign) for k, v in enumerate(parts[low])] for low in range(4)]
    out = [None] * 16
    for k in range(4):
        out[k::4] = packed_radix4([parts[low][k] for low in range(4)], sign)
    return out


def merge(tiles, place):
    for bit in (1, 2, 4):
        take = (place & bit) != 0
        tiles = [jnp.where(take, tiles[(m + bit) % 8], tiles[m]) for m in range(8)]
    return tiles


def dot(a, b):
    return jnp.dot(a, b, preferred_element_type=F32)


def mixer_kernel(*refs):
    force_h, mask_h, scalar_h = refs[:3]
    count = len(TABLES)
    tables_h = dict(zip(TABLES, refs[3 : 3 + count]))
    velocity_h, conc_h = refs[3 + count : 5 + count]
    (field, mask, scalar, *rest) = refs[5 + count :]
    tab = dict(zip(TABLES, rest[:count]))
    (gain, inv, sa, ra, sb, rb, sbi, rbi, sai, rai, spec, first, second, lines, big, mid,
     gain1, inv1, su, ru, sv, rv, svi, rvi, sui, rui, spec1, first1, second1, stacked, dots, dots1, summed, big1,
     u_send, u_recv, v_send, v_recv,
     zsend, zrecv, ysend, yrecv, edge, coef, state, conc,
     in_sem, tab_sem, a_send, a_recv, b_send, b_recv, z_ssem, z_rsem, y_ssem, y_rsem, out_sem) = rest[count:]

    r = lax.axis_index("row")
    col = lax.axis_index("col")
    e = col // 2
    xl = col % 2
    d = xl * 4 + r

    def load(source, target, sem):
        copy = pltpu.make_async_copy(source, target, sem)
        copy.start()
        return copy

    def load_table(name):
        source = tables_h[name]
        sem = tab_sem.at[TABLES.index(name)]
        if name in VARIED:
            source = source.at[d if name in BY_D else (e & 7) + (8 * xl if name == "utw" else 0)]
        return load(source, tab[name], sem)

    loads = {0: load(force_h.at[0], field.at[0], in_sem.at[0]), "fx": load_table("fx")}
    for i in (1, 2):
        loads[i] = load(force_h.at[i], field.at[i], in_sem.at[i])
    loads["scalar"] = load(scalar_h, scalar, in_sem.at[4])
    for name in TABLES[1:]:
        loads[name] = load_table(name)
    loads["mask"] = load(mask_h, mask, in_sem.at[3])

    core = r & 1
    x = (r // 2) * 2 + xl
    y_at, z_at = e // 4, e & 3

    def x_peer(step, of_core):
        at = (x + step * (1 + 2 * core)) & 3
        low = at & 1
        row = (at - low) + of_core
        return low * 4 + row, (row, e * 2 + low)

    def plane_peer(dy, dz):
        to = ((y_at + dy + core * (3 * dz - dy)) & 3) * 4 + ((z_at + dz + core * (3 * dy - dz)) & 3)
        return to, (r, to * 2 + xl)

    x_peers = [
        x_peer(step, core if same else 1 - core)
        for step, same in ((1, 1), (3, 1), (1, 0), (3, 0), (2, 1), (2, 0), (0, 0))
    ]
    plane_peers = [plane_peer(dy, dz) for dy, dz in PLANE_ORDER]

    z_up = (r, lax.rem(col + 1, 32))
    z_down = (r, lax.rem(col + 31, 32))
    y_up = (lax.rem(r + 1, 4), col)
    y_down = (lax.rem(r + 3, 4), col)

    barrier = pltpu.get_barrier_semaphore()

    for _, device in x_peers + plane_peers:
        pl.semaphore_signal(barrier, inc=1, device_id=device, device_id_type=MESH)
    across = (r, lax.rem(col + 31 + 2 * xl, 32))
    pl.semaphore_signal(barrier, inc=1, device_id=across, device_id_type=MESH)
    pl.semaphore_wait(barrier, 23)

    def remote(source, target, ssem, rsem, device):
        return pltpu.make_async_remote_copy(
            src_ref=source, dst_ref=target, send_sem=ssem, recv_sem=rsem,
            device_id=device, device_id_type=MESH)

    my_rows = pl.ds(pl.multiple_of(r * 64, 64), 64)
    my_slab = pl.ds(pl.multiple_of(e * 32, 32), 32)

    def send_a(t, i):
        target = ra.at[t, i, :, xl, my_rows]
        recv = a_recv.at[2 * t, i]

        for to, device in x_peers:
            remote(sa.at[i, to], target, a_send.at[2 * t, i], recv, device).start()
        pltpu.make_async_copy(sa.at[i, d], target, recv).start()

    def send_ai(t, i):
        target = rai.at[t, i, d]
        recv = a_recv.at[2 * t + 1, i]

        def piece(to):
            rows = pl.ds(pl.multiple_of((to & 3) * 64, 64), 64)
            return sai.at[i, :, to // 4, rows]

        for to, device in x_peers:
            remote(piece(to), target, a_send.at[2 * t + 1, i], recv, device).start()
        pltpu.make_async_copy(piece(d), target, recv).start()

    def send_b(source, into, k, t, i):
        target = into.at[t, i, my_slab]
        recv = b_recv.at[k, i]

        for to, device in plane_peers:
            slab = source.at[i, pl.ds(pl.multiple_of(to * 32, 32), 32)]
            remote(slab, target, b_send.at[k, i], recv, device).start()
        pltpu.make_async_copy(source.at[i, my_slab], target, recv).start()

    def send_u(source, into, k, t, c):
        target = into.at[t, c, e]
        recv = u_recv.at[k, c]
        for to, device in plane_peers:
            remote(source.at[c, to], target, u_send.at[k, c], recv, device).start()
        pltpu.make_async_copy(source.at[c, e], target, recv).start()

    def send_v(t, c):
        target = rv.at[t, c, :, xl, my_rows]
        recv = v_recv.at[2 * t, c]
        for to, device in x_peers:
            remote(sv.at[c, pl.ds(2 * to, 2)], target, v_send.at[2 * t, c], recv, device).start()
        pltpu.make_async_copy(sv.at[c, pl.ds(2 * d, 2)], target, recv).start()

    def send_vi(t, c):
        target = rvi.at[t, c, pl.ds(2 * d, 2)]
        recv = v_recv.at[2 * t + 1, c]

        def piece(to):
            rows = pl.ds(pl.multiple_of((to & 3) * 64, 64), 64)
            return svi.at[c, :, to // 4, rows]

        for to, device in x_peers:
            remote(piece(to), target, v_send.at[2 * t + 1, c], recv, device).start()
        pltpu.make_async_copy(piece(d), target, recv).start()

    def arrived(buffer, sem):
        pltpu.make_async_copy(buffer, buffer, sem).wait()

    def sent_a(k, i):
        arrived(sa.at[i, pl.ds(0, 7)], a_send.at[k, i])

    def sent_b(k, i):
        arrived(sb.at[i, pl.ds(0, 480)], b_send.at[k, i])

    def sent_u(k, i):
        arrived(su.at[i, pl.ds(0, 15)], u_send.at[k, i])

    def sent_v(k, i):
        arrived(sv.at[i, pl.ds(0, 14)], v_send.at[k, i])

    def send_z(s, q):
        rows = pl.ds(16 * q, 16)
        for side, device in ((0, z_down), (1, z_up)):
            remote(zsend.at[s, side, rows], zrecv.at[s, 1 - side, rows],
                   z_ssem.at[s, side], z_rsem.at[s, 1 - side, q], device).start()

    def pack_edge(s, side):
        value = edge[...]
        ysend[s, side] = jnp.concatenate([value[:, 0:256], value[:, 256:512]], axis=0).astype(BF)

    def send_y(s, side):
        remote(ysend.at[s, side], yrecv.at[s, 1 - side], y_ssem.at[s, side], y_rsem.at[s, 1 - side],
               (y_down, y_up)[side]).start()

    place = lax.broadcasted_iota(jnp.int32, (64, 128), 1) // 16

    def x_forward(t, c):
        spread = dot(field[c].reshape(512, 512), tab["fx"][:, 0:256])
        for ri in range(2):
            tiles = []
            for z in range(8):
                tile = spread[z * 64 : z * 64 + 64, ri * 128 : ri * 128 + 128]
                tiles.append(pltpu.roll(tile, 16 * z, 1) if z else tile)
            tiles = merge(tiles, place)
            for to in range(8):
                sa[c, to, ri] = tiles[-to % 8].astype(BF)
        send_a(t, c)

    def x_forward1(t, c):
        spread = dot(field[c].reshape(512, 512), tab["fx"][:, 256:512])
        for j in range(2):
            tiles = []
            for z in range(8):
                tile = spread[z * 64 : z * 64 + 64, j * 128 : j * 128 + 128]
                tiles.append(pltpu.roll(tile, 16 * z, 1) if z else tile)
            tiles = merge(tiles, place)
            for to in range(8):
                su[c, 8 * j + to] = tiles[-to % 8].astype(BF)
        send_u(su, ru, 2 * t, t, c)

    def x_inverse(t, c):
        def gather(j):
            if j < 2:
                tiles = [rai[t, c, source, j].astype(F32) for source in range(8)]
            else:
                tiles = [rui[t, c, 8 * (j - 2) + source].astype(F32) for source in range(8)]
            tiles = merge(tiles, place)
            for z in range(8):
                tile = tiles[-z % 8]
                tile = pltpu.roll(tile, 128 - 16 * z, 1) if z else tile
                lines[z * 64 : z * 64 + 64, j * 128 : j * 128 + 128] = tile.astype(BF)

        arrived(rai.at[t, c], a_recv.at[2 * t + 1, c])
        gather(0)
        gather(1)
        summed[...] = dot(lines[:, 0:256], tab["bx"][0:256, :])
        arrived(rui.at[t, c], u_recv.at[2 * t + 1, c])
        gather(2)
        gather(3)
        values = (summed[...] + dot(lines[:, 256:512], tab["bx"][256:512, :])).astype(BF).reshape(8, 64, 512)
        if t == 0:
            values = (values.astype(F32) * mask[...].astype(F32)).astype(BF)
        field[c] = values

    def y_forward(t, i):
        arrived(ra.at[t, i], a_recv.at[2 * t, i])
        sides = [ra[t, i, :, side].reshape(512, 128) for side in range(2)]
        sb[i] = dot(tab["ty"][...], jnp.concatenate(sides, axis=1)).astype(BF)
        send_b(sb, rb, 2 * t, t, i)

    def y_inverse(t, i):
        arrived(rbi.at[t, i], b_recv.at[2 * t + 1, i])
        out = dot(tab["tyi"][...], rbi[t, i]).astype(BF)
        for side in range(2):
            sai[i, :, side] = out[:, side * 128 : side * 128 + 128].reshape(2, 256, 128)
        send_ai(t, i)

    def z_forward(t, i):
        for half in range(2):
            lanes = slice(half * 128, half * 128 + 128)

            def source(e_from, ri):
                return rb[t, i, e_from * 32 + ri * 16 : e_from * 32 + ri * 16 + 16, lanes].astype(F32)

            for low in range(4):
                out = radix4([(source(low + 4 * j, 0), source(low + 4 * j, 1)) for j in range(4)], 1)
                for k, value in enumerate(out):
                    mid[low, k, 0, :, lanes], mid[low, k, 1, :, lanes] = turned_by(value, low * k, 1)
            for k in range(4):
                out = radix4([(mid[low, k, 0, :, lanes], mid[low, k, 1, :, lanes]) for low in range(4)], 1)
                for high, (re, im) in enumerate(out):
                    k1 = k + 4 * high
                    wc, ws = tab["tw"][0, k1 : k1 + 1, lanes], tab["tw"][1, k1 : k1 + 1, lanes]
                    big[k1 * 16 : k1 * 16 + 16, lanes] = (re * wc + im * ws).astype(BF)
                    big[256 + k1 * 16 : 256 + k1 * 16 + 16, lanes] = (im * wc - re * ws).astype(BF)
        both = dot(big[...], tab["cs"][...])
        spec[i, 0] = both[:256, :256] + both[256:, 256:]
        spec[i, 1] = both[256:, :256] - both[:256, 256:]

    def z_inverse(source, t, i):
        both = dot(source[i].reshape(512, 256), tab["csi"][...])
        for half in range(2):
            lanes = slice(half * 128, half * 128 + 128)
            other = slice(256 + half * 128, 256 + half * 128 + 128)

            def value(k1):
                upper, lower = slice(k1 * 16, k1 * 16 + 16), slice(256 + k1 * 16, 256 + k1 * 16 + 16)
                re = both[upper, lanes] - both[lower, other]
                im = both[lower, lanes] + both[upper, other]
                wc, ws = tab["tw"][0, k1 : k1 + 1, lanes], tab["tw"][1, k1 : k1 + 1, lanes]
                return re * wc - im * ws, im * wc + re * ws

            for low in range(4):
                out = radix4([value(low + 4 * j) for j in range(4)], -1)
                for k, turned in enumerate(out):
                    mid[low, k, 0, :, lanes], mid[low, k, 1, :, lanes] = turned_by(turned, low * k, -1)
            for k in range(4):
                out = radix4([(mid[low, k, 0, :, lanes], mid[low, k, 1, :, lanes]) for low in range(4)], -1)
                for high, (re, im) in enumerate(out):
                    to = (k + 4 * high) * 32
                    sbi[i, to : to + 16, lanes] = re.astype(BF)
                    sbi[i, to + 16 : to + 32, lanes] = im.astype(BF)
        send_b(sbi, rbi, 2 * t + 1, t, i)

    def v_forward(t, c):
        arrived(ru.at[t, c], u_recv.at[2 * t, c])

        def some(n, carry):
            rows = pl.ds(pl.multiple_of(n * 16, 16), 16)
            out = packed_dft16([ru[t, c, j, rows].astype(F32) for j in range(16)], 1)
            for k1, value in enumerate(out):
                wc, ws = tab["utw"][0, k1 : k1 + 1], tab["utw"][1, k1 : k1 + 1]
                sv[c, k1, rows] = (value * wc + times_minus_i(value) * ws).astype(BF)
            return carry

        lax.fori_loop(0, 4, some, 0)
        send_v(t, c)

    def v_inverse(t, c):
        arrived(rvi.at[t, c], v_recv.at[2 * t + 1, c])

        def some(n, carry):
            rows = pl.ds(pl.multiple_of(n * 16, 16), 16)
            values = []
            for k1 in range(16):
                value = rvi[t, c, k1, rows].astype(F32)
                wc, ws = tab["utw"][0, k1 : k1 + 1], tab["utw"][1, k1 : k1 + 1]
                values.append(value * wc - times_minus_i(value) * ws)
            for j, value in enumerate(packed_dft16(values, -1)):
                sui[c, j, rows] = value.astype(BF)
            return carry

        lax.fori_loop(0, 4, some, 0)
        send_u(sui, rui, 2 * t + 1, t, c)

    def y_product(table, values, wide):
        for half in range(2):
            lanes = slice(half * 128, half * 128 + 128)
            stacked[256:512, lanes] = times_minus_i(wide[:, lanes]).astype(BF)
        stacked[0:256, :] = values
        return dot(table, stacked[...]).astype(BF)

    def w_forward(t, c):
        for k1 in range(2):
            values = jnp.concatenate([rv[t, c, k1, 0], rv[t, c, k1, 1]], axis=1)
            big1[k1 * 256 : k1 * 256 + 256, :] = y_product(tab["uy"][...], values, values.astype(F32))
        spec1[c] = dot(big1[...], tab["uz"][...])

    def w_inverse(source, t, c):
        wide = dot(source[c], tab["uzi"][...])
        for k1 in range(2):
            part = wide[k1 * 256 : k1 * 256 + 256]
            out = y_product(tab["uyi"][...], part.astype(BF), part)
            for side in range(2):
                svi[c, k1, side] = out[:, side * 128 : side * 128 + 128]
        send_vi(t, c)

    lane = lax.broadcasted_iota(jnp.int32, (16, 256), 1)
    unit_long, unit = np.float32(TWO_PI / 512), np.float32(TWO_PI / 256)
    index_y = e * 16 + lax.broadcasted_iota(jnp.int32, (16, 256), 0)
    wave_y = jnp.where(index_y < 128, index_y, index_y - 256).astype(F32) * unit

    wave_x = (d * 32 + (lane & 15)).astype(F32) * unit_long
    wave_x1 = ((e // 2) * 32 + 16 + (e & 1) * 8 + (lane & 7)).astype(F32) * unit_long

    def along_z(k1):
        index_z = k1 + 16 * (lane // 16)
        return index_z, jnp.where(index_z < 128, index_z, index_z - 256).astype(F32) * unit

    def at_rows(n):
        return pl.ds(pl.multiple_of(n * 16, 16), 16)

    def along_y1(n):
        index = (n & 15) * 16 + lax.broadcasted_iota(jnp.int32, (16, 256), 0)
        return index, jnp.where(index < 128, index, index - 256).astype(F32) * unit

    def scales(kx, ky, kz, edge):
        ksq = kx * kx + ky * ky + kz * kz
        return (
            jnp.where(edge, 0.0, 1.0 / (0.05 * ksq + 0.5)),
            jnp.where(ksq > 0.0, 1.0 / jnp.where(ksq > 0.0, ksq, 1.0), 0.0),
        )

    def factors(n, carry):
        index_z, wave_z = along_z(n)
        gain[at_rows(n)], inv[at_rows(n)] = scales(wave_x, wave_y, wave_z, (index_y == 128) | (index_z == 128))
        return carry

    def factors1(n, carry):
        index_z, wave_z = along_z(2 * d + n // 16)
        index, wave = along_y1(n)
        gain1[at_rows(n)], inv1[at_rows(n)] = scales(wave_x1, wave, wave_z, (index == 128) | (index_z == 128))
        return carry

    def parts():
        def one(n, carry):
            rows = at_rows(n)
            for ri in range(2):
                dots[ri, rows] = wave_x * spec[0, ri, rows] + wave_y * spec[1, ri, rows]
            return carry

        lax.fori_loop(0, 16, one, 0)

    def keep(t, kept, result, at, value):
        if t == 0:
            kept[at] = value.astype(BF)
        else:
            result[at] = (kept[at].astype(F32) - value).astype(BF)

    def project_x(t):
        def one(n, carry):
            rows = at_rows(n)
            wave_z = along_z(n)[1]
            for ri in range(2):
                along = (dots[ri, rows] + wave_z * spec[2, ri, rows]) * inv[rows]
                dots[ri, rows] = along
                keep(t, first, second, (0, ri, rows), gain[rows] * (spec[0, ri, rows] - wave_x * along))
            return carry

        lax.fori_loop(0, 16, one, 0)

    def project_yz(t):
        def one(n, carry):
            rows = at_rows(n)
            waves = (wave_x, wave_y, along_z(n)[1])
            for ri in range(2):
                along = dots[ri, rows]
                for c in (1, 2):
                    keep(t, first, second, (c, ri, rows), gain[rows] * (spec[c, ri, rows] - waves[c] * along))
            return carry

        lax.fori_loop(0, 16, one, 0)

    def parts1():
        def one(n, carry):
            rows = at_rows(n)
            dots1[rows] = wave_x1 * spec1[0, rows] + along_y1(n)[1] * spec1[1, rows]
            return carry

        lax.fori_loop(0, 32, one, 0)

    def project1_x(t):
        def one(n, carry):
            rows = at_rows(n)
            along = (dots1[rows] + along_z(2 * d + n // 16)[1] * spec1[2, rows]) * inv1[rows]
            dots1[rows] = along
            keep(t, first1, second1, (0, rows), gain1[rows] * (spec1[0, rows] - wave_x1 * along))
            return carry

        lax.fori_loop(0, 32, one, 0)

    def project1_yz(t):
        def one(n, carry):
            rows = at_rows(n)
            waves = (wave_x1, along_y1(n)[1], along_z(2 * d + n // 16)[1])
            along = dots1[rows]
            for c in (1, 2):
                keep(t, first1, second1, (c, rows), gain1[rows] * (spec1[c, rows] - waves[c] * along))
            return carry

        lax.fori_loop(0, 32, one, 0)

    def each(count, step):
        def body(i, _):
            step(i)
            return _

        lax.fori_loop(0, count, body, 0)

    def spectral(t, source, source1):
        def out(c):
            y_forward(t, c)
            v_forward(t, c)

        def inner_arrived(c):
            arrived(rv.at[t, c], v_recv.at[2 * t, c])
            arrived(rb.at[t, c], b_recv.at[2 * t, c])

        def inner(c):
            inner_arrived(c)
            w_forward(t, c)
            z_forward(t, c)

        def outer(c):
            w_inverse(source1, t, c + 1)
            z_inverse(source, t, c + 1)

        def back(c):
            v_inverse(t, c)
            y_inverse(t, c)

        each(3, out)
        each(2, inner)
        parts1()
        parts()
        inner_arrived(2)
        w_forward(t, 2)
        z_forward(t, 2)
        project1_x(t)
        w_inverse(source1, t, 0)
        project_x(t)
        z_inverse(source, t, 0)
        project1_yz(t)
        project_yz(t)
        each(2, outer)
        each(3, back)

    loads["fx"].wait()
    for i in range(3):
        loads[i].wait()
    def start(c):
        x_forward(0, c)
        x_forward1(0, c)

    each(3, start)
    lax.fori_loop(0, 16, factors, 0)
    lax.fori_loop(0, 32, factors1, 0)
    loads["scalar"].wait()
    for z in range(8):
        state[0, z + 1, pl.ds(8, 64), :] = scalar[z].astype(F32)
    zsend[0, 0] = scalar[0]
    zsend[0, 1] = scalar[7]
    for q in range(4):
        send_z(0, q)
    for side in range(2):
        for z in range(8):
            edge[pl.ds(z, 1), :] = state[0, z + 1, pl.ds(8 + 63 * side, 1), :]
        pack_edge(0, side)
        send_y(0, side)
    for name in TABLES[1:]:
        loads[name].wait()
    loads["mask"].wait()
    spectral(0, first, first1)

    def sent(t, c):
        for k in (2 * t, 2 * t + 1):
            sent_a(k, c)
            sent_b(k, c)
            sent_u(k, c)
            sent_v(k, c)

    def middle(c):
        x_inverse(0, c)
        sent(0, c)
        x_forward(1, c)
        x_forward1(1, c)

    each(3, middle)
    spectral(1, second, second1)

    def coefficients(z, c):
        fluid = 0.25 * (1.0 - mask[z].astype(F32))
        u = field[c, z].astype(F32)
        below = fluid * (0.25 + jnp.maximum(u, 0.0))
        above = fluid * (0.25 - jnp.minimum(u, 0.0))
        coef[2 * c, z] = below
        coef[2 * c + 1, z] = above
        start = jnp.where(c == 0, jnp.ones_like(u), coef[6, z])
        coef[6, z] = start - (below + above)
        return c

    def last(c):
        x_inverse(1, c)
        pltpu.make_async_copy(field.at[c], velocity_h.at[c], out_sem.at[c]).start()
        lax.fori_loop(0, 8, coefficients, c)
        sent(1, c)

    each(3, last)

    def section(s, carry):
        now, later = s & 1, (s + 1) & 1

        def block(z, q, below_z, above_z):
            at = 8 + 16 * q
            rows, cells = pl.ds(at, 16), pl.ds(16 * q, 16)
            center = state[now, z, rows]
            new = coef[6, z - 1, cells] * center
            new = new + coef[0, z - 1, cells] * pltpu.roll(center, 1, 1)
            new = new + coef[1, z - 1, cells] * pltpu.roll(center, 511, 1)
            new = new + coef[2, z - 1, cells] * state[now, z, pl.ds(at - 1, 16)]
            new = new + coef[3, z - 1, cells] * state[now, z, pl.ds(at + 1, 16)]
            new = new + coef[4, z - 1, cells] * below_z + coef[5, z - 1, cells] * above_z
            state[later, z, rows] = new
            return new

        for q in (1, 2, 0, 3):
            rows, cells = pl.ds(8 + 16 * q, 16), pl.ds(16 * q, 16)
            if q in (0, 3):
                side = q // 3
                arrived(yrecv.at[s, side], y_rsem.at[s, side])
                halo = yrecv[s, side].astype(F32)
                for z in range(8):
                    for half in range(2):
                        lanes = slice(half * 256, half * 256 + 256)
                        state[now, z + 1, pl.ds(7 + 65 * side, 1), lanes] = halo[8 * half + z : 8 * half + z + 1]
            for side in range(2):
                arrived(zrecv.at[s, side, cells], z_rsem.at[s, side, q])
            bottom = block(1, q, zrecv[s, 0, cells].astype(F32), state[now, 2, rows])
            top = block(8, q, state[now, 7, rows], zrecv[s, 1, cells].astype(F32))

            @pl.when(s < SECTIONS - 1)
            def _():
                zsend[s + 1, 0, cells] = bottom.astype(BF)
                zsend[s + 1, 1, cells] = top.astype(BF)
                send_z(s + 1, q)

            for z in range(2, 8):
                block(z, q, state[now, z - 1, rows], state[now, z + 1, rows])
            if q in (0, 3):
                side = q // 3

                @pl.when(s < SECTIONS - 1)
                def _():
                    for z in range(8):
                        edge[pl.ds(z, 1), :] = state[later, z + 1, pl.ds(8 + 63 * side, 1), :]
                    pack_edge(s + 1, side)
                    send_y(s + 1, side)
        return carry

    lax.fori_loop(0, SECTIONS, section, 0)
    for z in range(8):
        conc[z] = state[SECTIONS % 2, z + 1, pl.ds(8, 64), :].astype(BF)

    for s in range(SECTIONS):
        for i in range(2):
            arrived(zsend.at[s, i], z_ssem.at[s, i])
            arrived(ysend.at[s, i], y_ssem.at[s, i])
    out = pltpu.make_async_copy(conc, conc_h, out_sem.at[3])
    out.start()
    for c in range(3):
        pltpu.make_async_copy(field.at[c], velocity_h.at[c], out_sem.at[c]).wait()
    out.wait()


def place_kernel(velocity_in, conc_in, velocity, conc, held, in_sem, out_sem):
    pairs = []
    for half in range(2):
        planes = pl.ds(4 * half, 4)
        pairs += [(velocity_in.at[c, planes], held.at[c, planes], velocity.at[c, planes]) for c in range(3)]
        pairs.append((conc_in.at[planes], held.at[3, planes], conc.at[planes]))
    loads = [pltpu.make_async_copy(a, b, in_sem.at[i]) for i, (a, b, _) in enumerate(pairs)]
    stores = [pltpu.make_async_copy(b, c, out_sem.at[i]) for i, (_, b, c) in enumerate(pairs)]
    for copy in loads:
        copy.start()
    for load, store in zip(loads, stores):
        load.wait()
        store.start()
    for copy in stores:
        copy.wait()


def local(force, mask, scalar):
    tables = numpy_tables()
    vm = pltpu.VMEM
    dma = pltpu.SemaphoreType.DMA
    scratch = [vm((3, 8, 64, 512), BF), vm((8, 64, 512), jnp.int32), vm((8, 64, 512), BF)]
    for name in TABLES:
        value = tables[name]
        shape = value.shape[1:] if name in VARIED else value.shape
        scratch.append(vm(shape, value.dtype))
    scratch += [
        vm((256, 256), F32), vm((256, 256), F32),
        vm((3, 8, 2, 64, 128), BF), vm((2, 3, 2, 2, 256, 128), BF),
        vm((3, 512, 256), BF), vm((2, 3, 512, 256), BF),
        vm((3, 512, 256), BF), vm((2, 3, 512, 256), BF),
        vm((3, 2, 2, 256, 128), BF), vm((2, 3, 8, 2, 64, 128), BF),
        vm((3, 2, 256, 256), F32), vm((3, 2, 256, 256), BF), vm((3, 2, 256, 256), BF),
        vm((512, 512), BF), vm((512, 256), BF), vm((4, 4, 2, 16, 256), F32),
        vm((512, 256), F32), vm((512, 256), F32),
        vm((3, 16, 64, 128), BF), vm((2, 3, 16, 64, 128), BF),
        vm((3, 16, 64, 128), BF), vm((2, 3, 2, 2, 256, 128), BF),
        vm((3, 2, 2, 256, 128), BF), vm((2, 3, 16, 64, 128), BF),
        vm((3, 16, 64, 128), BF), vm((2, 3, 16, 64, 128), BF),
        vm((3, 512, 256), F32), vm((3, 512, 256), BF), vm((3, 512, 256), BF),
        vm((512, 256), BF), vm((2, 256, 256), F32), vm((512, 256), F32),
        vm((512, 512), F32), vm((512, 256), BF),
        dma((4, 3)), dma((4, 3)), dma((4, 3)), dma((4, 3)),
        vm((SECTIONS, 2, 64, 512), BF), vm((SECTIONS, 2, 64, 512), BF),
        vm((SECTIONS, 2, 16, 256), BF), vm((SECTIONS, 2, 16, 256), BF), vm((8, 512), F32),
        vm((7, 8, 64, 512), F32), vm((2, 10, 80, 512), F32), vm((8, 64, 512), BF),
        dma((5,)), dma((len(TABLES),)),
        dma((4, 3)), dma((4, 3)), dma((4, 3)), dma((4, 3)),
        dma((SECTIONS, 2)), dma((SECTIONS, 2, 4)), dma((SECTIONS, 2)), dma((SECTIONS, 2)),
        dma((4,)),
    ]
    any_spec = pl.BlockSpec(memory_space=pl.ANY)
    velocity, conc = pl.pallas_call(
        mixer_kernel,
        out_shape=(
            jax.ShapeDtypeStruct((3, 8, 64, 512), BF),
            jax.ShapeDtypeStruct((8, 64, 512), BF),
        ),
        in_specs=[any_spec] * (3 + len(TABLES)),
        out_specs=(any_spec, any_spec),
        scratch_shapes=scratch,
        compiler_params=pltpu.CompilerParams(
            collective_id=0, has_side_effects=True, vmem_limit_bytes=62 * 1024 * 1024
        ),
        name="mixer",
    )(
        force,
        mask,
        scalar,
        *[jnp.asarray(tables[name]) for name in TABLES],
    )
    return pl.pallas_call(
        place_kernel,
        out_shape=(
            jax.ShapeDtypeStruct((3, 8, 64, 512), BF),
            jax.ShapeDtypeStruct((8, 64, 512), BF),
        ),
        in_specs=[any_spec] * 2,
        out_specs=(any_spec, any_spec),
        scratch_shapes=[vm((4, 8, 64, 512), BF), dma((8,)), dma((8,))],
        name="place",
    )(velocity, conc)


def solution(mesh):
    placed = (P(None, "col", "row", None), P("col", "row", None), P("col", "row", None))
    return jax.shard_map(
        local,
        mesh=mesh,
        in_specs=placed,
        out_specs=(P(None, "col", "row", None), P("col", "row", None)),
        check_vma=False,
    )
```

```python
import numpy as np
import jax
import jax.numpy as jnp
import ml_dtypes
from jax import lax
from jax.experimental import pallas as pl
from jax.experimental.pallas import tpu as pltpu
from jax.sharding import PartitionSpec as P

SECTIONS = 5
MESH = pl.DeviceIdType.MESH
BF = jnp.bfloat16
F32 = jnp.float32
TWO_PI = 2.0 * np.pi
PLANE_ORDER = (
    (2, 2), (2, 1), (1, 2), (2, 3), (3, 2), (2, 0), (0, 2), (1, 1), (3, 3), (1, 3), (3, 1),
    (1, 0), (3, 0), (0, 1), (0, 3),
)


def numpy_tables():
    def half(values):
        return values.astype(np.float32).astype(ml_dtypes.bfloat16)

    x = np.arange(512)
    ri, d, k = (v.reshape(-1) for v in np.meshgrid(np.arange(2), np.arange(8), np.arange(16), indexing="ij"))
    e1, ri1, k1 = (v.reshape(-1) for v in np.meshgrid(np.arange(16), np.arange(2), np.arange(8), indexing="ij"))
    m = np.concatenate([d * 32 + k, (e1 // 2) * 32 + 16 + (e1 % 2) * 8 + k1])
    ri = np.concatenate([ri, ri1])
    angle = (np.outer(x, m) % 512) * (TWO_PI / 512)
    fx = np.where(ri == 0, np.cos(angle), -np.sin(angle)) / np.sqrt(512.0)
    bx = (fx * np.where(m == 0, 1.0, 2.0)).T
    y = np.arange(256)
    angle = (np.outer(y, y) % 256) * (TWO_PI / 256)
    c, s = np.cos(angle) / 16.0, np.sin(angle) / 16.0
    real = np.concatenate([c, s], 1).reshape(16, 1, 16, 512)
    imag = np.concatenate([-s, c], 1).reshape(16, 1, 16, 512)
    ty = np.concatenate([real, imag], 1).reshape(512, 512)
    uy = np.concatenate([c, s], 1)
    uyi = np.concatenate([c, -s], 1)
    n = np.arange(16)
    angle = (np.outer(n, n) % 16) * (TWO_PI / 16)
    c, s = np.cos(angle) / 4.0, np.sin(angle) / 4.0
    cs = np.zeros((8, 256, 512))
    csi = np.zeros((8, 256, 512))
    tw = np.zeros((8, 2, 16, 256))
    k = np.arange(16)
    for d in range(8):
        for low in range(2):
            for p in range(8):
                zp = low * 8 + (p - d) % 8
                at = low * 128 + p * 16
                for k2 in range(16):
                    cs[d, at + k, k2 * 16 + k] = c[zp, k2]
                    cs[d, at + k, 256 + k2 * 16 + k] = s[zp, k2]
                    csi[d, k2 * 16 + k, at + k] = c[zp, k2]
                    csi[d, k2 * 16 + k, 256 + at + k] = s[zp, k2]
                tw[d, 0, :, at : at + 16] = np.cos(TWO_PI * zp * n / 256)[:, None] / 4.0
                tw[d, 1, :, at : at + 16] = np.sin(TWO_PI * zp * n / 256)[:, None] / 4.0
    utw = np.zeros((16, 2, 16, 128))
    uz = np.zeros((8, 256, 256))
    k = np.arange(8)
    for turn in range(8):
        for low in range(2):
            for p in range(8):
                zp = low * 8 + (p - turn) % 8
                utw[low * 8 + turn, 0, :, p * 16 : p * 16 + 16] = np.cos(TWO_PI * zp * n / 256)[:, None] / 4.0
                utw[low * 8 + turn, 1, :, p * 16 : p * 16 + 16] = np.sin(TWO_PI * zp * n / 256)[:, None] / 4.0
                at = low * 128 + p * 16
                for k2 in range(16):
                    to = k2 * 16
                    uz[turn, at + k, to + k] = c[zp, k2]
                    uz[turn, at + 8 + k, to + k] = s[zp, k2]
                    uz[turn, at + k, to + 8 + k] = -s[zp, k2]
                    uz[turn, at + 8 + k, to + 8 + k] = c[zp, k2]
    return dict(
        uy=half(uy), uyi=half(uyi), uz=half(uz), uzi=half(uz.transpose(0, 2, 1)), utw=utw.astype(np.float32),
        fx=half(fx), bx=half(bx), ty=half(ty), tyi=half(ty.T), cs=half(cs), csi=half(csi),
        tw=tw.astype(np.float32),
    )


TABLES = ("fx", "ty", "utw", "tw", "cs", "uy", "uz", "csi", "uzi", "tyi", "uyi", "bx")
BY_D = ("cs", "tw", "csi")
BY_E = ("uz", "uzi")
VARIED = BY_D + BY_E + ("utw",)


def radix4(a, sign):
    def add(u, v):
        return u[0] + v[0], u[1] + v[1]

    def sub(u, v):
        return u[0] - v[0], u[1] - v[1]

    t0, t1 = add(a[0], a[2]), sub(a[0], a[2])
    t2, t3 = add(a[1], a[3]), sub(a[1], a[3])
    t3 = (t3[1], -t3[0]) if sign > 0 else (-t3[1], t3[0])
    return add(t0, t2), add(t1, t3), sub(t0, t2), sub(t1, t3)


def turned_by(value, j, sign):
    if j == 0:
        return value
    c, s = float(np.cos(TWO_PI * j / 16)), float(np.sin(TWO_PI * j / 16)) * sign
    re, im = value
    return re * c + im * s, im * c - re * s


def times_minus_i(value):
    imag = (lax.broadcasted_iota(jnp.int32, value.shape, 1) & 8) != 0
    return jnp.where(imag, -pltpu.roll(value, 8, 1), pltpu.roll(value, 120, 1))


def packed_radix4(a, sign):
    t0, t1, t2 = a[0] + a[2], a[0] - a[2], a[1] + a[3]
    t3 = times_minus_i(a[1] - a[3])
    if sign < 0:
        t3 = -t3
    return t0 + t2, t1 + t3, t0 - t2, t1 - t3


def packed_turned(value, j, sign):
    if j == 0:
        return value
    c, s = float(np.cos(TWO_PI * j / 16)), float(np.sin(TWO_PI * j / 16)) * sign
    return value * c + times_minus_i(value) * s


def packed_dft16(values, sign):
    parts = [packed_radix4(values[low::4], sign) for low in range(4)]
    parts = [[packed_turned(v, low * k, sign) for k, v in enumerate(parts[low])] for low in range(4)]
    out = [None] * 16
    for k in range(4):
        out[k::4] = packed_radix4([parts[low][k] for low in range(4)], sign)
    return out


def merge(tiles, place):
    for bit in (1, 2, 4):
        take = (place & bit) != 0
        tiles = [jnp.where(take, tiles[(m + bit) % 8], tiles[m]) for m in range(8)]
    return tiles


def dot(a, b):
    return jnp.dot(a, b, preferred_element_type=F32)


def mixer_kernel(*refs):
    force_h, mask_h, scalar_h = refs[:3]
    count = len(TABLES)
    tables_h = dict(zip(TABLES, refs[3 : 3 + count]))
    velocity_h, conc_h = refs[3 + count : 5 + count]
    (field, mask, scalar, *rest) = refs[5 + count :]
    tab = dict(zip(TABLES, rest[:count]))
    (gain, inv, sa, ra, sb, rb, sbi, rbi, sai, rai, spec, first, second, lines, big, mid,
     gain1, inv1, su, ru, sv, rv, svi, rvi, sui, rui, spec1, first1, second1, stacked, dots, dots1, summed, big1,
     u_send, u_recv, v_send, v_recv,
     zsend, zrecv, ysend, yrecv, edge, coef, state, conc,
     in_sem, tab_sem, a_send, a_recv, b_send, b_recv, z_ssem, z_rsem, y_ssem, y_rsem, out_sem) = rest[count:]

    r = lax.axis_index("row")
    col = lax.axis_index("col")
    e = col // 2
    xl = col % 2
    d = xl * 4 + r

    def load(source, target, sem):
        copy = pltpu.make_async_copy(source, target, sem)
        copy.start()
        return copy

    def load_table(name):
        source = tables_h[name]
        sem = tab_sem.at[TABLES.index(name)]
        if name in VARIED:
            source = source.at[d if name in BY_D else (e & 7) + (8 * xl if name == "utw" else 0)]
        return load(source, tab[name], sem)

    loads = {0: load(force_h.at[0], field.at[0], in_sem.at[0]), "fx": load_table("fx")}
    for i in (1, 2):
        loads[i] = load(force_h.at[i], field.at[i], in_sem.at[i])
    loads["scalar"] = load(scalar_h, scalar, in_sem.at[4])
    for name in TABLES[1:]:
        loads[name] = load_table(name)
    loads["mask"] = load(mask_h, mask, in_sem.at[3])

    core = r & 1
    x = (r // 2) * 2 + xl
    y_at, z_at = e // 4, e & 3

    def x_peer(step, of_core):
        at = (x + step * (1 + 2 * core)) & 3
        low = at & 1
        row = (at - low) + of_core
        return low * 4 + row, (row, e * 2 + low)

    def plane_peer(dy, dz):
        to = ((y_at + dy + core * (3 * dz - dy)) & 3) * 4 + ((z_at + dz + core * (3 * dy - dz)) & 3)
        return to, (r, to * 2 + xl)

    x_peers = [
        x_peer(step, core if same else 1 - core)
        for step, same in ((2, 1), (2, 0), (1, 1), (3, 1), (1, 0), (3, 0), (0, 0))
    ]
    plane_peers = [plane_peer(dy, dz) for dy, dz in PLANE_ORDER]

    y_up = (lax.rem(r + 1, 4), col)
    y_down = (lax.rem(r + 3, 4), col)

    barrier = pltpu.get_barrier_semaphore()

    for _, device in x_peers + plane_peers:
        pl.semaphore_signal(barrier, inc=1, device_id=device, device_id_type=MESH)
    across = (r, lax.rem(col + 31 + 2 * xl, 32))
    pl.semaphore_signal(barrier, inc=1, device_id=across, device_id_type=MESH)
    pl.semaphore_wait(barrier, 23)

    def remote(source, target, ssem, rsem, device):
        return pltpu.make_async_remote_copy(
            src_ref=source, dst_ref=target, send_sem=ssem, recv_sem=rsem,
            device_id=device, device_id_type=MESH)

    my_rows = pl.ds(pl.multiple_of(r * 64, 64), 64)
    my_slab = pl.ds(pl.multiple_of(e * 32, 32), 32)

    def send_a(t, i):
        target = ra.at[t, i, :, xl, my_rows]
        recv = a_recv.at[2 * t, i]

        for to, device in x_peers:
            remote(sa.at[i, to], target, a_send.at[2 * t, i], recv, device).start()
        pltpu.make_async_copy(sa.at[i, d], target, recv).start()

    def send_ai(t, i):
        target = rai.at[t, i, d]
        recv = a_recv.at[2 * t + 1, i]

        def piece(to):
            rows = pl.ds(pl.multiple_of((to & 3) * 64, 64), 64)
            return sai.at[i, :, to // 4, rows]

        for to, device in x_peers:
            remote(piece(to), target, a_send.at[2 * t + 1, i], recv, device).start()
        pltpu.make_async_copy(piece(d), target, recv).start()

    def send_b(source, into, k, t, i):
        target = into.at[t, i, my_slab]
        recv = b_recv.at[k, i]

        for to, device in plane_peers:
            slab = source.at[i, pl.ds(pl.multiple_of(to * 32, 32), 32)]
            remote(slab, target, b_send.at[k, i], recv, device).start()
        pltpu.make_async_copy(source.at[i, my_slab], target, recv).start()

    def send_u(source, into, k, t, c):
        target = into.at[t, c, e]
        recv = u_recv.at[k, c]
        for to, device in plane_peers:
            remote(source.at[c, to], target, u_send.at[k, c], recv, device).start()
        pltpu.make_async_copy(source.at[c, e], target, recv).start()

    def send_v(t, c):
        target = rv.at[t, c, :, xl, my_rows]
        recv = v_recv.at[2 * t, c]
        for to, device in x_peers:
            remote(sv.at[c, pl.ds(2 * to, 2)], target, v_send.at[2 * t, c], recv, device).start()
        pltpu.make_async_copy(sv.at[c, pl.ds(2 * d, 2)], target, recv).start()

    def send_vi(t, c):
        target = rvi.at[t, c, pl.ds(2 * d, 2)]
        recv = v_recv.at[2 * t + 1, c]

        def piece(to):
            rows = pl.ds(pl.multiple_of((to & 3) * 64, 64), 64)
            return svi.at[c, :, to // 4, rows]

        for to, device in x_peers:
            remote(piece(to), target, v_send.at[2 * t + 1, c], recv, device).start()
        pltpu.make_async_copy(piece(d), target, recv).start()

    def arrived(buffer, sem):
        pltpu.make_async_copy(buffer, buffer, sem).wait()

    def sent_a(k, i):
        arrived(sa.at[i, pl.ds(0, 7)], a_send.at[k, i])

    def sent_b(k, i):
        arrived(sb.at[i, pl.ds(0, 480)], b_send.at[k, i])

    def sent_u(k, i):
        arrived(su.at[i, pl.ds(0, 15)], u_send.at[k, i])

    def sent_v(k, i):
        arrived(sv.at[i, pl.ds(0, 14)], v_send.at[k, i])

    near, far = 1 - xl, xl

    def send_z(s, side, q):
        rows = pl.ds(16 * q, 16)
        remote(zsend.at[s, side, rows], zrecv.at[s, 1 - side, rows], z_ssem.at[s, side],
               z_rsem.at[s, 1 - side, q], (r, (col + 2 * side + 31) & 31)).start()

    def pack_edge(s, side):
        value = edge[...]
        ysend[s, side] = jnp.concatenate([value[:, 0:256], value[:, 256:512]], axis=0).astype(BF)

    def send_y(s, side):
        remote(ysend.at[s, side], yrecv.at[s, 1 - side], y_ssem.at[s, side], y_rsem.at[s, 1 - side],
               (y_down, y_up)[side]).start()

    place = lax.broadcasted_iota(jnp.int32, (64, 128), 1) // 16

    def x_forward(t, c):
        spread = dot(field[c].reshape(512, 512), tab["fx"][:, 0:256])
        for ri in range(2):
            tiles = []
            for z in range(8):
                tile = spread[z * 64 : z * 64 + 64, ri * 128 : ri * 128 + 128]
                tiles.append(pltpu.roll(tile, 16 * z, 1) if z else tile)
            tiles = merge(tiles, place)
            for to in range(8):
                sa[c, to, ri] = tiles[-to % 8].astype(BF)
        send_a(t, c)

    def x_forward1(t, c):
        spread = dot(field[c].reshape(512, 512), tab["fx"][:, 256:512])
        for j in range(2):
            tiles = []
            for z in range(8):
                tile = spread[z * 64 : z * 64 + 64, j * 128 : j * 128 + 128]
                tiles.append(pltpu.roll(tile, 16 * z, 1) if z else tile)
            tiles = merge(tiles, place)
            for to in range(8):
                su[c, 8 * j + to] = tiles[-to % 8].astype(BF)
        send_u(su, ru, 2 * t, t, c)

    def x_inverse(t, c):
        def gather(j):
            if j < 2:
                tiles = [rai[t, c, source, j].astype(F32) for source in range(8)]
            else:
                tiles = [rui[t, c, 8 * (j - 2) + source].astype(F32) for source in range(8)]
            tiles = merge(tiles, place)
            for z in range(8):
                tile = tiles[-z % 8]
                tile = pltpu.roll(tile, 128 - 16 * z, 1) if z else tile
                lines[z * 64 : z * 64 + 64, j * 128 : j * 128 + 128] = tile.astype(BF)

        arrived(rai.at[t, c], a_recv.at[2 * t + 1, c])
        gather(0)
        gather(1)
        summed[...] = dot(lines[:, 0:256], tab["bx"][0:256, :])
        arrived(rui.at[t, c], u_recv.at[2 * t + 1, c])
        gather(2)
        gather(3)
        values = (summed[...] + dot(lines[:, 256:512], tab["bx"][256:512, :])).astype(BF).reshape(8, 64, 512)
        if t == 0:
            values = (values.astype(F32) * mask[...].astype(F32)).astype(BF)
        field[c] = values

    def y_forward(t, i):
        arrived(ra.at[t, i], a_recv.at[2 * t, i])
        sides = [ra[t, i, :, side].reshape(512, 128) for side in range(2)]
        sb[i] = dot(tab["ty"][...], jnp.concatenate(sides, axis=1)).astype(BF)
        send_b(sb, rb, 2 * t, t, i)

    def y_inverse(t, i):
        arrived(rbi.at[t, i], b_recv.at[2 * t + 1, i])
        out = dot(tab["tyi"][...], rbi[t, i]).astype(BF)
        for side in range(2):
            sai[i, :, side] = out[:, side * 128 : side * 128 + 128].reshape(2, 256, 128)
        send_ai(t, i)

    def z_forward(t, i):
        for half in range(2):
            lanes = slice(half * 128, half * 128 + 128)

            def source(e_from, ri):
                return rb[t, i, e_from * 32 + ri * 16 : e_from * 32 + ri * 16 + 16, lanes].astype(F32)

            for low in range(4):
                out = radix4([(source(low + 4 * j, 0), source(low + 4 * j, 1)) for j in range(4)], 1)
                for k, value in enumerate(out):
                    mid[low, k, 0, :, lanes], mid[low, k, 1, :, lanes] = turned_by(value, low * k, 1)
            for k in range(4):
                out = radix4([(mid[low, k, 0, :, lanes], mid[low, k, 1, :, lanes]) for low in range(4)], 1)
                for high, (re, im) in enumerate(out):
                    k1 = k + 4 * high
                    wc, ws = tab["tw"][0, k1 : k1 + 1, lanes], tab["tw"][1, k1 : k1 + 1, lanes]
                    big[k1 * 16 : k1 * 16 + 16, lanes] = (re * wc + im * ws).astype(BF)
                    big[256 + k1 * 16 : 256 + k1 * 16 + 16, lanes] = (im * wc - re * ws).astype(BF)
        both = dot(big[...], tab["cs"][...])
        spec[i, 0] = both[:256, :256] + both[256:, 256:]
        spec[i, 1] = both[256:, :256] - both[:256, 256:]

    def z_inverse(source, t, i):
        both = dot(source[i].reshape(512, 256), tab["csi"][...])
        for half in range(2):
            lanes = slice(half * 128, half * 128 + 128)
            other = slice(256 + half * 128, 256 + half * 128 + 128)

            def value(k1):
                upper, lower = slice(k1 * 16, k1 * 16 + 16), slice(256 + k1 * 16, 256 + k1 * 16 + 16)
                re = both[upper, lanes] - both[lower, other]
                im = both[lower, lanes] + both[upper, other]
                wc, ws = tab["tw"][0, k1 : k1 + 1, lanes], tab["tw"][1, k1 : k1 + 1, lanes]
                return re * wc - im * ws, im * wc + re * ws

            for low in range(4):
                out = radix4([value(low + 4 * j) for j in range(4)], -1)
                for k, turned in enumerate(out):
                    mid[low, k, 0, :, lanes], mid[low, k, 1, :, lanes] = turned_by(turned, low * k, -1)
            for k in range(4):
                out = radix4([(mid[low, k, 0, :, lanes], mid[low, k, 1, :, lanes]) for low in range(4)], -1)
                for high, (re, im) in enumerate(out):
                    to = (k + 4 * high) * 32
                    sbi[i, to : to + 16, lanes] = re.astype(BF)
                    sbi[i, to + 16 : to + 32, lanes] = im.astype(BF)
        send_b(sbi, rbi, 2 * t + 1, t, i)

    def v_forward(t, c):
        arrived(ru.at[t, c], u_recv.at[2 * t, c])

        def some(n, carry):
            rows = pl.ds(pl.multiple_of(n * 16, 16), 16)
            out = packed_dft16([ru[t, c, j, rows].astype(F32) for j in range(16)], 1)
            for k1, value in enumerate(out):
                wc, ws = tab["utw"][0, k1 : k1 + 1], tab["utw"][1, k1 : k1 + 1]
                sv[c, k1, rows] = (value * wc + times_minus_i(value) * ws).astype(BF)
            return carry

        lax.fori_loop(0, 4, some, 0)
        send_v(t, c)

    def v_inverse(t, c):
        arrived(rvi.at[t, c], v_recv.at[2 * t + 1, c])

        def some(n, carry):
            rows = pl.ds(pl.multiple_of(n * 16, 16), 16)
            values = []
            for k1 in range(16):
                value = rvi[t, c, k1, rows].astype(F32)
                wc, ws = tab["utw"][0, k1 : k1 + 1], tab["utw"][1, k1 : k1 + 1]
                values.append(value * wc - times_minus_i(value) * ws)
            for j, value in enumerate(packed_dft16(values, -1)):
                sui[c, j, rows] = value.astype(BF)
            return carry

        lax.fori_loop(0, 4, some, 0)
        send_u(sui, rui, 2 * t + 1, t, c)

    def y_product(table, values, wide):
        for half in range(2):
            lanes = slice(half * 128, half * 128 + 128)
            stacked[256:512, lanes] = times_minus_i(wide[:, lanes]).astype(BF)
        stacked[0:256, :] = values
        return dot(table, stacked[...]).astype(BF)

    def w_forward(t, c):
        for k1 in range(2):
            values = jnp.concatenate([rv[t, c, k1, 0], rv[t, c, k1, 1]], axis=1)
            big1[k1 * 256 : k1 * 256 + 256, :] = y_product(tab["uy"][...], values, values.astype(F32))
        spec1[c] = dot(big1[...], tab["uz"][...])

    def w_inverse(source, t, c):
        wide = dot(source[c], tab["uzi"][...])
        for k1 in range(2):
            part = wide[k1 * 256 : k1 * 256 + 256]
            out = y_product(tab["uyi"][...], part.astype(BF), part)
            for side in range(2):
                svi[c, k1, side] = out[:, side * 128 : side * 128 + 128]
        send_vi(t, c)

    lane = lax.broadcasted_iota(jnp.int32, (16, 256), 1)
    unit_long, unit = np.float32(TWO_PI / 512), np.float32(TWO_PI / 256)
    index_y = e * 16 + lax.broadcasted_iota(jnp.int32, (16, 256), 0)
    wave_y = jnp.where(index_y < 128, index_y, index_y - 256).astype(F32) * unit

    wave_x = (d * 32 + (lane & 15)).astype(F32) * unit_long
    wave_x1 = ((e // 2) * 32 + 16 + (e & 1) * 8 + (lane & 7)).astype(F32) * unit_long

    def along_z(k1):
        index_z = k1 + 16 * (lane // 16)
        return index_z, jnp.where(index_z < 128, index_z, index_z - 256).astype(F32) * unit

    def at_rows(n):
        return pl.ds(pl.multiple_of(n * 16, 16), 16)

    def along_y1(n):
        index = (n & 15) * 16 + lax.broadcasted_iota(jnp.int32, (16, 256), 0)
        return index, jnp.where(index < 128, index, index - 256).astype(F32) * unit

    def scales(kx, ky, kz, edge):
        ksq = kx * kx + ky * ky + kz * kz
        return (
            jnp.where(edge, 0.0, 1.0 / (0.05 * ksq + 0.5)),
            jnp.where(ksq > 0.0, 1.0 / jnp.where(ksq > 0.0, ksq, 1.0), 0.0),
        )

    def factors(n, carry):
        index_z, wave_z = along_z(n)
        gain[at_rows(n)], inv[at_rows(n)] = scales(wave_x, wave_y, wave_z, (index_y == 128) | (index_z == 128))
        return carry

    def factors1(n, carry):
        index_z, wave_z = along_z(2 * d + n // 16)
        index, wave = along_y1(n)
        gain1[at_rows(n)], inv1[at_rows(n)] = scales(wave_x1, wave, wave_z, (index == 128) | (index_z == 128))
        return carry

    def parts():
        def one(n, carry):
            rows = at_rows(n)
            for ri in range(2):
                dots[ri, rows] = wave_x * spec[0, ri, rows] + wave_y * spec[1, ri, rows]
            return carry

        lax.fori_loop(0, 16, one, 0)

    def keep(t, kept, result, at, value):
        if t == 0:
            kept[at] = value.astype(BF)
        else:
            result[at] = (kept[at].astype(F32) - value).astype(BF)

    def project_x(t):
        def one(n, carry):
            rows = at_rows(n)
            wave_z = along_z(n)[1]
            for ri in range(2):
                along = (dots[ri, rows] + wave_z * spec[2, ri, rows]) * inv[rows]
                dots[ri, rows] = along
                keep(t, first, second, (0, ri, rows), gain[rows] * (spec[0, ri, rows] - wave_x * along))
            return carry

        lax.fori_loop(0, 16, one, 0)

    def project_yz(t):
        def one(n, carry):
            rows = at_rows(n)
            waves = (wave_x, wave_y, along_z(n)[1])
            for ri in range(2):
                along = dots[ri, rows]
                for c in (1, 2):
                    keep(t, first, second, (c, ri, rows), gain[rows] * (spec[c, ri, rows] - waves[c] * along))
            return carry

        lax.fori_loop(0, 16, one, 0)

    def parts1():
        def one(n, carry):
            rows = at_rows(n)
            dots1[rows] = wave_x1 * spec1[0, rows] + along_y1(n)[1] * spec1[1, rows]
            return carry

        lax.fori_loop(0, 32, one, 0)

    def project1_x(t):
        def one(n, carry):
            rows = at_rows(n)
            along = (dots1[rows] + along_z(2 * d + n // 16)[1] * spec1[2, rows]) * inv1[rows]
            dots1[rows] = along
            keep(t, first1, second1, (0, rows), gain1[rows] * (spec1[0, rows] - wave_x1 * along))
            return carry

        lax.fori_loop(0, 32, one, 0)

    def project1_yz(t):
        def one(n, carry):
            rows = at_rows(n)
            waves = (wave_x1, along_y1(n)[1], along_z(2 * d + n // 16)[1])
            along = dots1[rows]
            for c in (1, 2):
                keep(t, first1, second1, (c, rows), gain1[rows] * (spec1[c, rows] - waves[c] * along))
            return carry

        lax.fori_loop(0, 32, one, 0)

    def each(count, step):
        def body(i, _):
            step(i)
            return _

        lax.fori_loop(0, count, body, 0)

    def spectral(t, source, source1):
        def out(c):
            y_forward(t, c)
            v_forward(t, c)

        def inner_arrived(c):
            arrived(rv.at[t, c], v_recv.at[2 * t, c])
            arrived(rb.at[t, c], b_recv.at[2 * t, c])

        def inner(c):
            inner_arrived(c)
            w_forward(t, c)
            z_forward(t, c)

        def outer(c):
            w_inverse(source1, t, c + 1)
            z_inverse(source, t, c + 1)

        def back(c):
            v_inverse(t, c)
            y_inverse(t, c)

        each(3, out)
        each(2, inner)
        parts1()
        parts()
        inner_arrived(2)
        w_forward(t, 2)
        z_forward(t, 2)
        project1_x(t)
        w_inverse(source1, t, 0)
        project_x(t)
        z_inverse(source, t, 0)
        project1_yz(t)
        project_yz(t)
        each(2, outer)
        each(3, back)

    loads["fx"].wait()
    for i in range(3):
        loads[i].wait()
    def start(c):
        x_forward(0, c)
        x_forward1(0, c)

    each(3, start)
    lax.fori_loop(0, 16, factors, 0)
    lax.fori_loop(0, 32, factors1, 0)
    loads["scalar"].wait()
    for z in range(8):
        state[0, z + 1, pl.ds(8, 64), :] = scalar[z].astype(F32)
    zsend[0, 0] = scalar[0]
    zsend[0, 1] = scalar[7]
    for side in (far, near):
        for q in range(4):
            send_z(0, side, q)
    for side in range(2):
        for z in range(8):
            edge[pl.ds(z, 1), :] = state[0, z + 1, pl.ds(8 + 63 * side, 1), :]
        pack_edge(0, side)
        send_y(0, side)
    for name in TABLES[1:]:
        loads[name].wait()
    loads["mask"].wait()
    spectral(0, first, first1)

    def sent(t, c):
        for k in (2 * t, 2 * t + 1):
            sent_a(k, c)
            sent_b(k, c)
            sent_u(k, c)
            sent_v(k, c)

    def middle(c):
        x_inverse(0, c)
        sent(0, c)
        x_forward(1, c)
        x_forward1(1, c)

    each(3, middle)
    spectral(1, second, second1)

    def coefficients(z, c):
        fluid = 0.25 * (1.0 - mask[z].astype(F32))
        u = field[c, z].astype(F32)
        below = fluid * (0.25 + jnp.maximum(u, 0.0))
        above = fluid * (0.25 - jnp.minimum(u, 0.0))
        coef[2 * c, z] = below
        coef[2 * c + 1, z] = above
        start = jnp.where(c == 0, jnp.ones_like(u), coef[6, z])
        coef[6, z] = start - (below + above)
        return c

    def last(c):
        x_inverse(1, c)
        pltpu.make_async_copy(field.at[c], velocity_h.at[c], out_sem.at[c]).start()
        lax.fori_loop(0, 8, coefficients, c)
        sent(1, c)

    each(3, last)

    def section(s, carry):
        now, later = s & 1, (s + 1) & 1

        def block(z, q):
            at = 8 + 16 * q
            rows, cells = pl.ds(at, 16), pl.ds(16 * q, 16)
            center = state[now, z, rows]
            new = coef[6, z - 1, cells] * center
            new = new + coef[0, z - 1, cells] * pltpu.roll(center, 1, 1)
            new = new + coef[1, z - 1, cells] * pltpu.roll(center, 511, 1)
            new = new + coef[2, z - 1, cells] * state[now, z, pl.ds(at - 1, 16)]
            new = new + coef[3, z - 1, cells] * state[now, z, pl.ds(at + 1, 16)]
            new = new + coef[4, z - 1, cells] * state[now, z - 1, rows]
            new = new + coef[5, z - 1, cells] * state[now, z + 1, rows]
            state[later, z, rows] = new
            return new

        def outer_block(side, q):
            cells = pl.ds(16 * q, 16)
            arrived(zrecv.at[s, side, cells], z_rsem.at[s, side, q])
            state[now, 9 * side, pl.ds(8 + 16 * q, 16)] = zrecv[s, side, cells].astype(F32)
            face = block(1 + 7 * side, q)

            @pl.when(s < SECTIONS - 1)
            def _():
                zsend[s + 1, side, cells] = face.astype(BF)
                send_z(s + 1, side, q)

        for q in (1, 2, 0, 3):
            if q in (0, 3):
                side = q // 3
                arrived(yrecv.at[s, side], y_rsem.at[s, side])
                halo = yrecv[s, side].astype(F32)
                for z in range(8):
                    for half in range(2):
                        lanes = slice(half * 256, half * 256 + 256)
                        state[now, z + 1, pl.ds(7 + 65 * side, 1), lanes] = halo[8 * half + z : 8 * half + z + 1]
            outer_block(near, q)
            for z in range(2, 8):
                block(z, q)

        for q in (0, 3, 1, 2):
            outer_block(far, q)
            if q in (0, 3):
                side = q // 3

                @pl.when(s < SECTIONS - 1)
                def _():
                    for z in range(8):
                        edge[pl.ds(z, 1), :] = state[later, z + 1, pl.ds(8 + 63 * side, 1), :]
                    pack_edge(s + 1, side)
                    send_y(s + 1, side)
        return carry

    lax.fori_loop(0, SECTIONS, section, 0)
    for z in range(8):
        conc[z] = state[SECTIONS % 2, z + 1, pl.ds(8, 64), :].astype(BF)

    for s in range(SECTIONS):
        for i in range(2):
            arrived(zsend.at[s, i], z_ssem.at[s, i])
            arrived(ysend.at[s, i], y_ssem.at[s, i])
    out = pltpu.make_async_copy(conc, conc_h, out_sem.at[3])
    out.start()
    for c in range(3):
        pltpu.make_async_copy(field.at[c], velocity_h.at[c], out_sem.at[c]).wait()
    out.wait()


def place_kernel(velocity_in, conc_in, velocity, conc, held, in_sem, out_sem):
    pairs = []
    for half in range(2):
        planes = pl.ds(4 * half, 4)
        pairs += [(velocity_in.at[c, planes], held.at[c, planes], velocity.at[c, planes]) for c in range(3)]
        pairs.append((conc_in.at[planes], held.at[3, planes], conc.at[planes]))
    loads = [pltpu.make_async_copy(a, b, in_sem.at[i]) for i, (a, b, _) in enumerate(pairs)]
    stores = [pltpu.make_async_copy(b, c, out_sem.at[i]) for i, (_, b, c) in enumerate(pairs)]
    for copy in loads:
        copy.start()
    for load, store in zip(loads, stores):
        load.wait()
        store.start()
    for copy in stores:
        copy.wait()


def local(force, mask, scalar):
    tables = numpy_tables()
    vm = pltpu.VMEM
    dma = pltpu.SemaphoreType.DMA
    scratch = [vm((3, 8, 64, 512), BF), vm((8, 64, 512), jnp.int32), vm((8, 64, 512), BF)]
    for name in TABLES:
        value = tables[name]
        shape = value.shape[1:] if name in VARIED else value.shape
        scratch.append(vm(shape, value.dtype))
    scratch += [
        vm((256, 256), F32), vm((256, 256), F32),
        vm((3, 8, 2, 64, 128), BF), vm((2, 3, 2, 2, 256, 128), BF),
        vm((3, 512, 256), BF), vm((2, 3, 512, 256), BF),
        vm((3, 512, 256), BF), vm((2, 3, 512, 256), BF),
        vm((3, 2, 2, 256, 128), BF), vm((2, 3, 8, 2, 64, 128), BF),
        vm((3, 2, 256, 256), F32), vm((3, 2, 256, 256), BF), vm((3, 2, 256, 256), BF),
        vm((512, 512), BF), vm((512, 256), BF), vm((4, 4, 2, 16, 256), F32),
        vm((512, 256), F32), vm((512, 256), F32),
        vm((3, 16, 64, 128), BF), vm((2, 3, 16, 64, 128), BF),
        vm((3, 16, 64, 128), BF), vm((2, 3, 2, 2, 256, 128), BF),
        vm((3, 2, 2, 256, 128), BF), vm((2, 3, 16, 64, 128), BF),
        vm((3, 16, 64, 128), BF), vm((2, 3, 16, 64, 128), BF),
        vm((3, 512, 256), F32), vm((3, 512, 256), BF), vm((3, 512, 256), BF),
        vm((512, 256), BF), vm((2, 256, 256), F32), vm((512, 256), F32),
        vm((512, 512), F32), vm((512, 256), BF),
        dma((4, 3)), dma((4, 3)), dma((4, 3)), dma((4, 3)),
        vm((SECTIONS, 2, 64, 512), BF), vm((SECTIONS, 2, 64, 512), BF),
        vm((SECTIONS, 2, 16, 256), BF), vm((SECTIONS, 2, 16, 256), BF), vm((8, 512), F32),
        vm((7, 8, 64, 512), F32), vm((2, 10, 80, 512), F32), vm((8, 64, 512), BF),
        dma((5,)), dma((len(TABLES),)),
        dma((4, 3)), dma((4, 3)), dma((4, 3)), dma((4, 3)),
        dma((SECTIONS, 2)), dma((SECTIONS, 2, 4)), dma((SECTIONS, 2)), dma((SECTIONS, 2)),
        dma((4,)),
    ]
    any_spec = pl.BlockSpec(memory_space=pl.ANY)
    velocity, conc = pl.pallas_call(
        mixer_kernel,
        out_shape=(
            jax.ShapeDtypeStruct((3, 8, 64, 512), BF),
            jax.ShapeDtypeStruct((8, 64, 512), BF),
        ),
        in_specs=[any_spec] * (3 + len(TABLES)),
        out_specs=(any_spec, any_spec),
        scratch_shapes=scratch,
        compiler_params=pltpu.CompilerParams(
            collective_id=0, has_side_effects=True, vmem_limit_bytes=62 * 1024 * 1024
        ),
        name="mixer",
    )(
        force,
        mask,
        scalar,
        *[jnp.asarray(tables[name]) for name in TABLES],
    )
    return pl.pallas_call(
        place_kernel,
        out_shape=(
            jax.ShapeDtypeStruct((3, 8, 64, 512), BF),
            jax.ShapeDtypeStruct((8, 64, 512), BF),
        ),
        in_specs=[any_spec] * 2,
        out_specs=(any_spec, any_spec),
        scratch_shapes=[vm((4, 8, 64, 512), BF), dma((8,)), dma((8,))],
        name="place",
    )(velocity, conc)


def solution(mesh):
    placed = (P(None, "col", "row", None), P("col", "row", None), P("col", "row", None))
    return jax.shard_map(
        local,
        mesh=mesh,
        in_specs=placed,
        out_specs=(P(None, "col", "row", None), P("col", "row", None)),
        check_vma=False,
    )
```

```python
import numpy as np
import jax
import jax.numpy as jnp
import ml_dtypes
from jax import lax
from jax.experimental import pallas as pl
from jax.experimental.pallas import tpu as pltpu
from jax.sharding import PartitionSpec as P

SECTIONS = 5
MESH = pl.DeviceIdType.MESH
BF = jnp.bfloat16
F32 = jnp.float32
TWO_PI = 2.0 * np.pi
PLANE_ORDER = (
    (2, 2), (2, 1), (1, 2), (2, 3), (3, 2), (2, 0), (0, 2), (1, 1), (3, 3), (1, 3), (3, 1),
    (1, 0), (3, 0), (0, 1), (0, 3),
)


def numpy_tables():
    def half(values):
        return values.astype(np.float32).astype(ml_dtypes.bfloat16)

    x = np.arange(512)
    ri, d, k = (v.reshape(-1) for v in np.meshgrid(np.arange(2), np.arange(8), np.arange(16), indexing="ij"))
    e1, ri1, k1 = (v.reshape(-1) for v in np.meshgrid(np.arange(16), np.arange(2), np.arange(8), indexing="ij"))
    m = np.concatenate([d * 32 + k, (e1 // 2) * 32 + 16 + (e1 % 2) * 8 + k1])
    ri = np.concatenate([ri, ri1])
    angle = (np.outer(x, m) % 512) * (TWO_PI / 512)
    fx = np.where(ri == 0, np.cos(angle), -np.sin(angle)) / np.sqrt(512.0)
    bx = (fx * np.where(m == 0, 1.0, 2.0)).T
    y = np.arange(256)
    angle = (np.outer(y, y) % 256) * (TWO_PI / 256)
    c, s = np.cos(angle) / 16.0, np.sin(angle) / 16.0
    real = np.concatenate([c, s], 1).reshape(16, 1, 16, 512)
    imag = np.concatenate([-s, c], 1).reshape(16, 1, 16, 512)
    ty = np.concatenate([real, imag], 1).reshape(512, 512)
    uy = np.concatenate([c, s], 1)
    uyi = np.concatenate([c, -s], 1)
    n = np.arange(16)
    angle = (np.outer(n, n) % 16) * (TWO_PI / 16)
    c, s = np.cos(angle) / 4.0, np.sin(angle) / 4.0
    cs = np.zeros((8, 256, 512))
    csi = np.zeros((8, 256, 512))
    tw = np.zeros((8, 2, 16, 256))
    k = np.arange(16)
    for d in range(8):
        for low in range(2):
            for p in range(8):
                zp = low * 8 + (p - d) % 8
                at = low * 128 + p * 16
                for k2 in range(16):
                    cs[d, at + k, k2 * 16 + k] = c[zp, k2]
                    cs[d, at + k, 256 + k2 * 16 + k] = s[zp, k2]
                    csi[d, k2 * 16 + k, at + k] = c[zp, k2]
                    csi[d, k2 * 16 + k, 256 + at + k] = s[zp, k2]
                tw[d, 0, :, at : at + 16] = np.cos(TWO_PI * zp * n / 256)[:, None] / 4.0
                tw[d, 1, :, at : at + 16] = np.sin(TWO_PI * zp * n / 256)[:, None] / 4.0
    utw = np.zeros((16, 2, 16, 128))
    uz = np.zeros((8, 256, 256))
    k = np.arange(8)
    for turn in range(8):
        for low in range(2):
            for p in range(8):
                zp = low * 8 + (p - turn) % 8
                utw[low * 8 + turn, 0, :, p * 16 : p * 16 + 16] = np.cos(TWO_PI * zp * n / 256)[:, None] / 4.0
                utw[low * 8 + turn, 1, :, p * 16 : p * 16 + 16] = np.sin(TWO_PI * zp * n / 256)[:, None] / 4.0
                at = low * 128 + p * 16
                for k2 in range(16):
                    to = k2 * 16
                    uz[turn, at + k, to + k] = c[zp, k2]
                    uz[turn, at + 8 + k, to + k] = s[zp, k2]
                    uz[turn, at + k, to + 8 + k] = -s[zp, k2]
                    uz[turn, at + 8 + k, to + 8 + k] = c[zp, k2]
    return dict(
        uy=half(uy), uyi=half(uyi), uz=half(uz), uzi=half(uz.transpose(0, 2, 1)), utw=utw.astype(np.float32),
        fx=half(fx), bx=half(bx), ty=half(ty), tyi=half(ty.T), cs=half(cs), csi=half(csi),
        tw=tw.astype(np.float32),
    )


TABLES = ("fx", "ty", "utw", "tw", "cs", "uy", "uz", "csi", "uzi", "tyi", "uyi", "bx")
BY_D = ("cs", "tw", "csi")
BY_E = ("uz", "uzi")
VARIED = BY_D + BY_E + ("utw",)


def radix4(a, sign):
    def add(u, v):
        return u[0] + v[0], u[1] + v[1]

    def sub(u, v):
        return u[0] - v[0], u[1] - v[1]

    t0, t1 = add(a[0], a[2]), sub(a[0], a[2])
    t2, t3 = add(a[1], a[3]), sub(a[1], a[3])
    t3 = (t3[1], -t3[0]) if sign > 0 else (-t3[1], t3[0])
    return add(t0, t2), add(t1, t3), sub(t0, t2), sub(t1, t3)


def turned_by(value, j, sign):
    if j == 0:
        return value
    c, s = float(np.cos(TWO_PI * j / 16)), float(np.sin(TWO_PI * j / 16)) * sign
    re, im = value
    return re * c + im * s, im * c - re * s


def times_minus_i(value):
    imag = (lax.broadcasted_iota(jnp.int32, value.shape, 1) & 8) != 0
    return jnp.where(imag, -pltpu.roll(value, 8, 1), pltpu.roll(value, 120, 1))


def packed_radix4(a, sign):
    t0, t1, t2 = a[0] + a[2], a[0] - a[2], a[1] + a[3]
    t3 = times_minus_i(a[1] - a[3])
    if sign < 0:
        t3 = -t3
    return t0 + t2, t1 + t3, t0 - t2, t1 - t3


def packed_turned(value, j, sign):
    if j == 0:
        return value
    c, s = float(np.cos(TWO_PI * j / 16)), float(np.sin(TWO_PI * j / 16)) * sign
    return value * c + times_minus_i(value) * s


def packed_dft16(values, sign):
    parts = [packed_radix4(values[low::4], sign) for low in range(4)]
    parts = [[packed_turned(v, low * k, sign) for k, v in enumerate(parts[low])] for low in range(4)]
    out = [None] * 16
    for k in range(4):
        out[k::4] = packed_radix4([parts[low][k] for low in range(4)], sign)
    return out


def merge(tiles, place):
    for bit in (1, 2, 4):
        take = (place & bit) != 0
        tiles = [jnp.where(take, tiles[(m + bit) % 8], tiles[m]) for m in range(8)]
    return tiles


def dot(a, b):
    return jnp.dot(a, b, preferred_element_type=F32)


def mixer_kernel(*refs):
    force_h, mask_h, scalar_h = refs[:3]
    count = len(TABLES)
    tables_h = dict(zip(TABLES, refs[3 : 3 + count]))
    velocity_h, conc_h = refs[3 + count : 5 + count]
    (field, mask, scalar, *rest) = refs[5 + count :]
    tab = dict(zip(TABLES, rest[:count]))
    (gain, inv, sa, ra, sb, rb, sbi, rbi, sai, rai, spec, first, second, lines, big, mid,
     gain1, inv1, su, ru, sv, rv, svi, rvi, sui, rui, spec1, first1, second1, stacked, dots, dots1, summed, big1,
     u_send, u_recv, v_send, v_recv,
     zsend, zrecv, ysend, yrecv, edge, coef, state, conc,
     in_sem, tab_sem, a_send, a_recv, b_send, b_recv, z_ssem, z_rsem, y_ssem, y_rsem, out_sem) = rest[count:]

    r = lax.axis_index("row")
    col = lax.axis_index("col")
    e = col // 2
    xl = col % 2
    d = xl * 4 + r

    def load(source, target, sem):
        copy = pltpu.make_async_copy(source, target, sem)
        copy.start()
        return copy

    def load_table(name):
        source = tables_h[name]
        sem = tab_sem.at[TABLES.index(name)]
        if name in VARIED:
            source = source.at[d if name in BY_D else (e & 7) + (8 * xl if name == "utw" else 0)]
        return load(source, tab[name], sem)

    loads = {0: load(force_h.at[0], field.at[0], in_sem.at[0]), "fx": load_table("fx")}

    def load_rest():
        for i in (1, 2):
            loads[i] = load(force_h.at[i], field.at[i], in_sem.at[i])
        for name in TABLES[1:]:
            loads[name] = load_table(name)
        loads["scalar"] = load(scalar_h, scalar, in_sem.at[4])
        loads["mask"] = load(mask_h, mask, in_sem.at[3])

    core = r & 1
    x = (r // 2) * 2 + xl
    y_at, z_at = e // 4, e & 3

    def x_peer(step, of_core):
        at = (x + step * (1 + 2 * core)) & 3
        low = at & 1
        row = (at - low) + of_core
        return low * 4 + row, (row, e * 2 + low)

    def plane_peer(dy, dz):
        to = ((y_at + dy + core * (3 * dz - dy)) & 3) * 4 + ((z_at + dz + core * (3 * dy - dz)) & 3)
        return to, (r, to * 2 + xl)

    x_peers = [
        x_peer(step, core if same else 1 - core)
        for step, same in ((2, 1), (2, 0), (1, 1), (3, 1), (1, 0), (3, 0), (0, 0))
    ]
    plane_peers = [plane_peer(dy, dz) for dy, dz in PLANE_ORDER]

    y_up = (lax.rem(r + 1, 4), col)
    y_down = (lax.rem(r + 3, 4), col)

    barrier = pltpu.get_barrier_semaphore()

    for _, device in x_peers + plane_peers:
        pl.semaphore_signal(barrier, inc=1, device_id=device, device_id_type=MESH)
    across = (r, lax.rem(col + 31 + 2 * xl, 32))
    pl.semaphore_signal(barrier, inc=1, device_id=across, device_id_type=MESH)
    pl.semaphore_wait(barrier, 23)

    def remote(source, target, ssem, rsem, device):
        return pltpu.make_async_remote_copy(
            src_ref=source, dst_ref=target, send_sem=ssem, recv_sem=rsem,
            device_id=device, device_id_type=MESH)

    my_rows = pl.ds(pl.multiple_of(r * 64, 64), 64)
    my_slab = pl.ds(pl.multiple_of(e * 32, 32), 32)

    def send_a(t, i):
        target = ra.at[t, i, :, xl, my_rows]
        recv = a_recv.at[2 * t, i]

        for to, device in x_peers:
            remote(sa.at[i, to], target, a_send.at[2 * t, i], recv, device).start()
        pltpu.make_async_copy(sa.at[i, d], target, recv).start()

    def send_ai(t, i):
        target = rai.at[t, i, d]
        recv = a_recv.at[2 * t + 1, i]

        def piece(to):
            rows = pl.ds(pl.multiple_of((to & 3) * 64, 64), 64)
            return sai.at[i, :, to // 4, rows]

        for to, device in x_peers:
            remote(piece(to), target, a_send.at[2 * t + 1, i], recv, device).start()
        pltpu.make_async_copy(piece(d), target, recv).start()

    def send_b(source, into, k, t, i):
        target = into.at[t, i, my_slab]
        recv = b_recv.at[k, i]

        for to, device in plane_peers:
            slab = source.at[i, pl.ds(pl.multiple_of(to * 32, 32), 32)]
            remote(slab, target, b_send.at[k, i], recv, device).start()
        pltpu.make_async_copy(source.at[i, my_slab], target, recv).start()

    def send_u(source, into, k, t, c):
        target = into.at[t, c, e]
        recv = u_recv.at[k, c]
        for to, device in plane_peers:
            remote(source.at[c, to], target, u_send.at[k, c], recv, device).start()
        pltpu.make_async_copy(source.at[c, e], target, recv).start()

    def send_v(t, c):
        target = rv.at[t, c, :, xl, my_rows]
        recv = v_recv.at[2 * t, c]
        for to, device in x_peers:
            remote(sv.at[c, pl.ds(2 * to, 2)], target, v_send.at[2 * t, c], recv, device).start()
        pltpu.make_async_copy(sv.at[c, pl.ds(2 * d, 2)], target, recv).start()

    def send_vi(t, c):
        target = rvi.at[t, c, pl.ds(2 * d, 2)]
        recv = v_recv.at[2 * t + 1, c]

        def piece(to):
            rows = pl.ds(pl.multiple_of((to & 3) * 64, 64), 64)
            return svi.at[c, :, to // 4, rows]

        for to, device in x_peers:
            remote(piece(to), target, v_send.at[2 * t + 1, c], recv, device).start()
        pltpu.make_async_copy(piece(d), target, recv).start()

    def arrived(buffer, sem):
        pltpu.make_async_copy(buffer, buffer, sem).wait()

    def sent_a(k, i):
        arrived(sa.at[i, pl.ds(0, 7)], a_send.at[k, i])

    def sent_b(k, i):
        arrived(sb.at[i, pl.ds(0, 480)], b_send.at[k, i])

    def sent_u(k, i):
        arrived(su.at[i, pl.ds(0, 15)], u_send.at[k, i])

    def sent_v(k, i):
        arrived(sv.at[i, pl.ds(0, 14)], v_send.at[k, i])

    near, far = 1 - xl, xl

    def send_z(s, side, q):
        rows = pl.ds(16 * q, 16)
        remote(zsend.at[s, side, rows], zrecv.at[s, 1 - side, rows], z_ssem.at[s, side],
               z_rsem.at[s, 1 - side, q], (r, (col + 2 * side + 31) & 31)).start()

    def pack_edge(s, side):
        value = edge[...]
        ysend[s, side] = jnp.concatenate([value[:, 0:256], value[:, 256:512]], axis=0).astype(BF)

    def send_y(s, side):
        remote(ysend.at[s, side], yrecv.at[s, 1 - side], y_ssem.at[s, side], y_rsem.at[s, 1 - side],
               (y_down, y_up)[side]).start()

    place = lax.broadcasted_iota(jnp.int32, (64, 128), 1) // 16

    def x_forward(t, c):
        spread = dot(field[c].reshape(512, 512), tab["fx"][:, 0:256])
        for ri in range(2):
            tiles = []
            for z in range(8):
                tile = spread[z * 64 : z * 64 + 64, ri * 128 : ri * 128 + 128]
                tiles.append(pltpu.roll(tile, 16 * z, 1) if z else tile)
            tiles = merge(tiles, place)
            for to in range(8):
                sa[c, to, ri] = tiles[-to % 8].astype(BF)
        send_a(t, c)

    def x_forward1(t, c):
        spread = dot(field[c].reshape(512, 512), tab["fx"][:, 256:512])
        for j in range(2):
            tiles = []
            for z in range(8):
                tile = spread[z * 64 : z * 64 + 64, j * 128 : j * 128 + 128]
                tiles.append(pltpu.roll(tile, 16 * z, 1) if z else tile)
            tiles = merge(tiles, place)
            for to in range(8):
                su[c, 8 * j + to] = tiles[-to % 8].astype(BF)
        send_u(su, ru, 2 * t, t, c)

    def x_inverse(t, c):
        def gather(j):
            if j < 2:
                tiles = [rai[t, c, source, j].astype(F32) for source in range(8)]
            else:
                tiles = [rui[t, c, 8 * (j - 2) + source].astype(F32) for source in range(8)]
            tiles = merge(tiles, place)
            for z in range(8):
                tile = tiles[-z % 8]
                tile = pltpu.roll(tile, 128 - 16 * z, 1) if z else tile
                lines[z * 64 : z * 64 + 64, j * 128 : j * 128 + 128] = tile.astype(BF)

        arrived(rai.at[t, c], a_recv.at[2 * t + 1, c])
        gather(0)
        gather(1)
        summed[...] = dot(lines[:, 0:256], tab["bx"][0:256, :])
        arrived(rui.at[t, c], u_recv.at[2 * t + 1, c])
        gather(2)
        gather(3)
        values = (summed[...] + dot(lines[:, 256:512], tab["bx"][256:512, :])).astype(BF).reshape(8, 64, 512)
        if t == 0:
            values = (values.astype(F32) * mask[...].astype(F32)).astype(BF)
        field[c] = values

    def y_forward(t, i):
        arrived(ra.at[t, i], a_recv.at[2 * t, i])
        sides = [ra[t, i, :, side].reshape(512, 128) for side in range(2)]
        sb[i] = dot(tab["ty"][...], jnp.concatenate(sides, axis=1)).astype(BF)
        send_b(sb, rb, 2 * t, t, i)

    def y_inverse(t, i):
        arrived(rbi.at[t, i], b_recv.at[2 * t + 1, i])
        out = dot(tab["tyi"][...], rbi[t, i]).astype(BF)
        for side in range(2):
            sai[i, :, side] = out[:, side * 128 : side * 128 + 128].reshape(2, 256, 128)
        send_ai(t, i)

    def z_forward(t, i):
        for half in range(2):
            lanes = slice(half * 128, half * 128 + 128)

            def source(e_from, ri):
                return rb[t, i, e_from * 32 + ri * 16 : e_from * 32 + ri * 16 + 16, lanes].astype(F32)

            for low in range(4):
                out = radix4([(source(low + 4 * j, 0), source(low + 4 * j, 1)) for j in range(4)], 1)
                for k, value in enumerate(out):
                    mid[low, k, 0, :, lanes], mid[low, k, 1, :, lanes] = turned_by(value, low * k, 1)
            for k in range(4):
                out = radix4([(mid[low, k, 0, :, lanes], mid[low, k, 1, :, lanes]) for low in range(4)], 1)
                for high, (re, im) in enumerate(out):
                    k1 = k + 4 * high
                    wc, ws = tab["tw"][0, k1 : k1 + 1, lanes], tab["tw"][1, k1 : k1 + 1, lanes]
                    big[k1 * 16 : k1 * 16 + 16, lanes] = (re * wc + im * ws).astype(BF)
                    big[256 + k1 * 16 : 256 + k1 * 16 + 16, lanes] = (im * wc - re * ws).astype(BF)
        both = dot(big[...], tab["cs"][...])
        spec[i, 0] = both[:256, :256] + both[256:, 256:]
        spec[i, 1] = both[256:, :256] - both[:256, 256:]

    def z_inverse(source, t, i):
        both = dot(source[i].reshape(512, 256), tab["csi"][...])
        for half in range(2):
            lanes = slice(half * 128, half * 128 + 128)
            other = slice(256 + half * 128, 256 + half * 128 + 128)

            def value(k1):
                upper, lower = slice(k1 * 16, k1 * 16 + 16), slice(256 + k1 * 16, 256 + k1 * 16 + 16)
                re = both[upper, lanes] - both[lower, other]
                im = both[lower, lanes] + both[upper, other]
                wc, ws = tab["tw"][0, k1 : k1 + 1, lanes], tab["tw"][1, k1 : k1 + 1, lanes]
                return re * wc - im * ws, im * wc + re * ws

            for low in range(4):
                out = radix4([value(low + 4 * j) for j in range(4)], -1)
                for k, turned in enumerate(out):
                    mid[low, k, 0, :, lanes], mid[low, k, 1, :, lanes] = turned_by(turned, low * k, -1)
            for k in range(4):
                out = radix4([(mid[low, k, 0, :, lanes], mid[low, k, 1, :, lanes]) for low in range(4)], -1)
                for high, (re, im) in enumerate(out):
                    to = (k + 4 * high) * 32
                    sbi[i, to : to + 16, lanes] = re.astype(BF)
                    sbi[i, to + 16 : to + 32, lanes] = im.astype(BF)
        send_b(sbi, rbi, 2 * t + 1, t, i)

    def v_forward(t, c):
        arrived(ru.at[t, c], u_recv.at[2 * t, c])

        def some(n, carry):
            rows = pl.ds(pl.multiple_of(n * 16, 16), 16)
            out = packed_dft16([ru[t, c, j, rows].astype(F32) for j in range(16)], 1)
            for k1, value in enumerate(out):
                wc, ws = tab["utw"][0, k1 : k1 + 1], tab["utw"][1, k1 : k1 + 1]
                sv[c, k1, rows] = (value * wc + times_minus_i(value) * ws).astype(BF)
            return carry

        lax.fori_loop(0, 4, some, 0)
        send_v(t, c)

    def v_inverse(t, c):
        arrived(rvi.at[t, c], v_recv.at[2 * t + 1, c])

        def some(n, carry):
            rows = pl.ds(pl.multiple_of(n * 16, 16), 16)
            values = []
            for k1 in range(16):
                value = rvi[t, c, k1, rows].astype(F32)
                wc, ws = tab["utw"][0, k1 : k1 + 1], tab["utw"][1, k1 : k1 + 1]
                values.append(value * wc - times_minus_i(value) * ws)
            for j, value in enumerate(packed_dft16(values, -1)):
                sui[c, j, rows] = value.astype(BF)
            return carry

        lax.fori_loop(0, 4, some, 0)
        send_u(sui, rui, 2 * t + 1, t, c)

    def y_product(table, values, wide):
        for half in range(2):
            lanes = slice(half * 128, half * 128 + 128)
            stacked[256:512, lanes] = times_minus_i(wide[:, lanes]).astype(BF)
        stacked[0:256, :] = values
        return dot(table, stacked[...]).astype(BF)

    def w_forward(t, c):
        for k1 in range(2):
            values = jnp.concatenate([rv[t, c, k1, 0], rv[t, c, k1, 1]], axis=1)
            big1[k1 * 256 : k1 * 256 + 256, :] = y_product(tab["uy"][...], values, values.astype(F32))
        spec1[c] = dot(big1[...], tab["uz"][...])

    def w_inverse(source, t, c):
        wide = dot(source[c], tab["uzi"][...])
        for k1 in range(2):
            part = wide[k1 * 256 : k1 * 256 + 256]
            out = y_product(tab["uyi"][...], part.astype(BF), part)
            for side in range(2):
                svi[c, k1, side] = out[:, side * 128 : side * 128 + 128]
        send_vi(t, c)

    lane = lax.broadcasted_iota(jnp.int32, (16, 256), 1)
    unit_long, unit = np.float32(TWO_PI / 512), np.float32(TWO_PI / 256)
    index_y = e * 16 + lax.broadcasted_iota(jnp.int32, (16, 256), 0)
    wave_y = jnp.where(index_y < 128, index_y, index_y - 256).astype(F32) * unit

    wave_x = (d * 32 + (lane & 15)).astype(F32) * unit_long
    wave_x1 = ((e // 2) * 32 + 16 + (e & 1) * 8 + (lane & 7)).astype(F32) * unit_long

    def along_z(k1):
        index_z = k1 + 16 * (lane // 16)
        return index_z, jnp.where(index_z < 128, index_z, index_z - 256).astype(F32) * unit

    def at_rows(n):
        return pl.ds(pl.multiple_of(n * 16, 16), 16)

    def along_y1(n):
        index = (n & 15) * 16 + lax.broadcasted_iota(jnp.int32, (16, 256), 0)
        return index, jnp.where(index < 128, index, index - 256).astype(F32) * unit

    def scales(kx, ky, kz, edge):
        ksq = kx * kx + ky * ky + kz * kz
        return (
            jnp.where(edge, 0.0, 1.0 / (0.05 * ksq + 0.5)),
            jnp.where(ksq > 0.0, 1.0 / jnp.where(ksq > 0.0, ksq, 1.0), 0.0),
        )

    def factors(n, carry):
        index_z, wave_z = along_z(n)
        gain[at_rows(n)], inv[at_rows(n)] = scales(wave_x, wave_y, wave_z, (index_y == 128) | (index_z == 128))
        return carry

    def factors1(n, carry):
        index_z, wave_z = along_z(2 * d + n // 16)
        index, wave = along_y1(n)
        gain1[at_rows(n)], inv1[at_rows(n)] = scales(wave_x1, wave, wave_z, (index == 128) | (index_z == 128))
        return carry

    def parts():
        def one(n, carry):
            rows = at_rows(n)
            for ri in range(2):
                dots[ri, rows] = wave_x * spec[0, ri, rows] + wave_y * spec[1, ri, rows]
            return carry

        lax.fori_loop(0, 16, one, 0)

    def keep(t, kept, result, at, value):
        if t == 0:
            kept[at] = value.astype(BF)
        else:
            result[at] = (kept[at].astype(F32) - value).astype(BF)

    def project_x(t):
        def one(n, carry):
            rows = at_rows(n)
            wave_z = along_z(n)[1]
            for ri in range(2):
                along = (dots[ri, rows] + wave_z * spec[2, ri, rows]) * inv[rows]
                dots[ri, rows] = along
                keep(t, first, second, (0, ri, rows), gain[rows] * (spec[0, ri, rows] - wave_x * along))
            return carry

        lax.fori_loop(0, 16, one, 0)

    def project_yz(t):
        def one(n, carry):
            rows = at_rows(n)
            waves = (wave_x, wave_y, along_z(n)[1])
            for ri in range(2):
                along = dots[ri, rows]
                for c in (1, 2):
                    keep(t, first, second, (c, ri, rows), gain[rows] * (spec[c, ri, rows] - waves[c] * along))
            return carry

        lax.fori_loop(0, 16, one, 0)

    def parts1():
        def one(n, carry):
            rows = at_rows(n)
            dots1[rows] = wave_x1 * spec1[0, rows] + along_y1(n)[1] * spec1[1, rows]
            return carry

        lax.fori_loop(0, 32, one, 0)

    def project1_x(t):
        def one(n, carry):
            rows = at_rows(n)
            along = (dots1[rows] + along_z(2 * d + n // 16)[1] * spec1[2, rows]) * inv1[rows]
            dots1[rows] = along
            keep(t, first1, second1, (0, rows), gain1[rows] * (spec1[0, rows] - wave_x1 * along))
            return carry

        lax.fori_loop(0, 32, one, 0)

    def project1_yz(t):
        def one(n, carry):
            rows = at_rows(n)
            waves = (wave_x1, along_y1(n)[1], along_z(2 * d + n // 16)[1])
            along = dots1[rows]
            for c in (1, 2):
                keep(t, first1, second1, (c, rows), gain1[rows] * (spec1[c, rows] - waves[c] * along))
            return carry

        lax.fori_loop(0, 32, one, 0)

    def each(count, step):
        def body(i, _):
            step(i)
            return _

        lax.fori_loop(0, count, body, 0)

    def spectral(t, source, source1):
        def out(c):
            y_forward(t, c)
            v_forward(t, c)

        def inner_arrived(c):
            arrived(rv.at[t, c], v_recv.at[2 * t, c])
            arrived(rb.at[t, c], b_recv.at[2 * t, c])

        def inner(c):
            inner_arrived(c)
            w_forward(t, c)
            z_forward(t, c)

        def outer(c):
            w_inverse(source1, t, c + 1)
            z_inverse(source, t, c + 1)

        def back(c):
            v_inverse(t, c)
            y_inverse(t, c)

        each(3, out)
        each(2, inner)
        parts1()
        parts()
        inner_arrived(2)
        w_forward(t, 2)
        z_forward(t, 2)
        project1_x(t)
        w_inverse(source1, t, 0)
        project_x(t)
        z_inverse(source, t, 0)
        project1_yz(t)
        project_yz(t)
        each(2, outer)
        each(3, back)

    def start(c):
        @pl.when(c > 0)
        def _():
            arrived(field.at[c], in_sem.at[c])

        x_forward(0, c)
        x_forward1(0, c)

    loads["fx"].wait()
    loads[0].wait()
    load_rest()
    each(3, start)
    lax.fori_loop(0, 16, factors, 0)
    lax.fori_loop(0, 32, factors1, 0)
    loads["scalar"].wait()
    for z in range(8):
        state[0, z + 1, pl.ds(8, 64), :] = scalar[z].astype(F32)
    zsend[0, 0] = scalar[0]
    zsend[0, 1] = scalar[7]
    for side in (far, near):
        for q in range(4):
            send_z(0, side, q)
    for side in range(2):
        for z in range(8):
            edge[pl.ds(z, 1), :] = state[0, z + 1, pl.ds(8 + 63 * side, 1), :]
        pack_edge(0, side)
        send_y(0, side)
    for name in TABLES[1:]:
        loads[name].wait()
    loads["mask"].wait()
    spectral(0, first, first1)

    def sent(t, c):
        for k in (2 * t, 2 * t + 1):
            sent_a(k, c)
            sent_b(k, c)
            sent_u(k, c)
            sent_v(k, c)

    def middle(c):
        x_inverse(0, c)
        sent(0, c)
        x_forward(1, c)
        x_forward1(1, c)

    each(3, middle)
    spectral(1, second, second1)

    def coefficients(z, c):
        fluid = 0.25 * (1.0 - mask[z].astype(F32))
        u = field[c, z].astype(F32)
        below = fluid * (0.25 + jnp.maximum(u, 0.0))
        above = fluid * (0.25 - jnp.minimum(u, 0.0))
        coef[2 * c, z] = below
        coef[2 * c + 1, z] = above
        start = jnp.where(c == 0, jnp.ones_like(u), coef[6, z])
        coef[6, z] = start - (below + above)
        return c

    def last(c):
        x_inverse(1, c)
        pltpu.make_async_copy(field.at[c], velocity_h.at[c], out_sem.at[c]).start()

        @pl.when(c < 2)
        def _():
            lax.fori_loop(0, 8, coefficients, c)

    each(3, last)

    def block(s, z, q):
        now, later = s & 1, (s + 1) & 1
        at = 8 + 16 * q
        rows, cells = pl.ds(at, 16), pl.ds(16 * q, 16)
        center = state[now, z, rows]
        new = coef[6, z - 1, cells] * center
        new = new + coef[0, z - 1, cells] * pltpu.roll(center, 1, 1)
        new = new + coef[1, z - 1, cells] * pltpu.roll(center, 511, 1)
        new = new + coef[2, z - 1, cells] * state[now, z, pl.ds(at - 1, 16)]
        new = new + coef[3, z - 1, cells] * state[now, z, pl.ds(at + 1, 16)]
        new = new + coef[4, z - 1, cells] * state[now, z - 1, rows]
        new = new + coef[5, z - 1, cells] * state[now, z + 1, rows]
        state[later, z, rows] = new
        return new

    def outer_block(s, side, q):
        cells = pl.ds(16 * q, 16)
        arrived(zrecv.at[s, side, cells], z_rsem.at[s, side, q])
        state[s & 1, 9 * side, pl.ds(8 + 16 * q, 16)] = zrecv[s, side, cells].astype(F32)
        face = block(s, 1 + 7 * side, q)

        @pl.when(s < SECTIONS - 1)
        def _():
            zsend[s + 1, side, cells] = face.astype(BF)
            send_z(s + 1, side, q)

    def y_halo(s):
        for side in range(2):
            arrived(yrecv.at[s, side], y_rsem.at[s, side])
            halo = yrecv[s, side].astype(F32)
            for z in range(8):
                for half in range(2):
                    lanes = slice(half * 256, half * 256 + 256)
                    state[s & 1, z + 1, pl.ds(7 + 65 * side, 1), lanes] = halo[8 * half + z : 8 * half + z + 1]

    def section(s, carry):
        @pl.when(s == SECTIONS - 1)
        def _():
            y_halo(s)

        for q in (0, 3, 1, 2):
            outer_block(s, near, q)
            for z in range(2, 8):
                block(s, z, q)
            if q in (0, 3):
                side = q // 3

                @pl.when(s < SECTIONS - 1)
                def _():
                    for z in range(8):
                        edge[pl.ds(z, 1), :] = state[(s + 1) & 1, z + 1, pl.ds(8 + 63 * side, 1), :]
                    pack_edge(s + 1, side)
                    send_y(s + 1, side)

        following = jnp.minimum(s + 1, SECTIONS - 1)

        @pl.when(s != SECTIONS - 2)
        def _():
            for q in (1, 2):
                outer_block(following, far, q)

        @pl.when(s < SECTIONS - 2)
        def _():
            y_halo(s + 1)

        @pl.when(s != SECTIONS - 2)
        def _():
            for q in (0, 3):
                outer_block(following, far, q)

        return carry

    y_halo(0)
    coefficients(7 * far, 2)
    for q in (1, 2, 0, 3):
        outer_block(0, far, q)
    lax.fori_loop(0, 7, lambda n, carry: coefficients(n + near, carry), 2)
    lax.fori_loop(0, SECTIONS, section, 0)
    for half in range(2):
        planes = pl.ds(4 * half, 4)
        conc[planes] = state[SECTIONS % 2, pl.ds(1 + 4 * half, 4), pl.ds(8, 64), :].astype(BF)
        pltpu.make_async_copy(conc.at[planes], conc_h.at[planes], out_sem.at[3 + half]).start()

    each(3, lambda c: sent(1, c))
    for s in range(SECTIONS):
        for i in range(2):
            arrived(zsend.at[s, i], z_ssem.at[s, i])
            arrived(ysend.at[s, i], y_ssem.at[s, i])
    for c in range(3):
        pltpu.make_async_copy(field.at[c], velocity_h.at[c], out_sem.at[c]).wait()
    for half in range(2):
        planes = pl.ds(4 * half, 4)
        pltpu.make_async_copy(conc.at[planes], conc_h.at[planes], out_sem.at[3 + half]).wait()


def place_kernel(velocity_in, conc_in, velocity, conc, held, in_sem, out_sem):
    pairs = []
    for half in range(2):
        planes = pl.ds(4 * half, 4)
        pairs += [(velocity_in.at[c, planes], held.at[c, planes], velocity.at[c, planes]) for c in range(3)]
        pairs.append((conc_in.at[planes], held.at[3, planes], conc.at[planes]))
    loads = [pltpu.make_async_copy(a, b, in_sem.at[i]) for i, (a, b, _) in enumerate(pairs)]
    stores = [pltpu.make_async_copy(b, c, out_sem.at[i]) for i, (_, b, c) in enumerate(pairs)]
    for copy in loads:
        copy.start()
    for load, store in zip(loads, stores):
        load.wait()
        store.start()
    for copy in stores:
        copy.wait()


def local(force, mask, scalar):
    tables = numpy_tables()
    vm = pltpu.VMEM
    dma = pltpu.SemaphoreType.DMA
    scratch = [vm((3, 8, 64, 512), BF), vm((8, 64, 512), jnp.int32), vm((8, 64, 512), BF)]
    for name in TABLES:
        value = tables[name]
        shape = value.shape[1:] if name in VARIED else value.shape
        scratch.append(vm(shape, value.dtype))
    scratch += [
        vm((256, 256), F32), vm((256, 256), F32),
        vm((3, 8, 2, 64, 128), BF), vm((2, 3, 2, 2, 256, 128), BF),
        vm((3, 512, 256), BF), vm((2, 3, 512, 256), BF),
        vm((3, 512, 256), BF), vm((2, 3, 512, 256), BF),
        vm((3, 2, 2, 256, 128), BF), vm((2, 3, 8, 2, 64, 128), BF),
        vm((3, 2, 256, 256), F32), vm((3, 2, 256, 256), BF), vm((3, 2, 256, 256), BF),
        vm((512, 512), BF), vm((512, 256), BF), vm((4, 4, 2, 16, 256), F32),
        vm((512, 256), F32), vm((512, 256), F32),
        vm((3, 16, 64, 128), BF), vm((2, 3, 16, 64, 128), BF),
        vm((3, 16, 64, 128), BF), vm((2, 3, 2, 2, 256, 128), BF),
        vm((3, 2, 2, 256, 128), BF), vm((2, 3, 16, 64, 128), BF),
        vm((3, 16, 64, 128), BF), vm((2, 3, 16, 64, 128), BF),
        vm((3, 512, 256), F32), vm((3, 512, 256), BF), vm((3, 512, 256), BF),
        vm((512, 256), BF), vm((2, 256, 256), F32), vm((512, 256), F32),
        vm((512, 512), F32), vm((512, 256), BF),
        dma((4, 3)), dma((4, 3)), dma((4, 3)), dma((4, 3)),
        vm((SECTIONS, 2, 64, 512), BF), vm((SECTIONS, 2, 64, 512), BF),
        vm((SECTIONS, 2, 16, 256), BF), vm((SECTIONS, 2, 16, 256), BF), vm((8, 512), F32),
        vm((7, 8, 64, 512), F32), vm((2, 10, 80, 512), F32), vm((8, 64, 512), BF),
        dma((5,)), dma((len(TABLES),)),
        dma((4, 3)), dma((4, 3)), dma((4, 3)), dma((4, 3)),
        dma((SECTIONS, 2)), dma((SECTIONS, 2, 4)), dma((SECTIONS, 2)), dma((SECTIONS, 2)),
        dma((5,)),
    ]
    any_spec = pl.BlockSpec(memory_space=pl.ANY)
    velocity, conc = pl.pallas_call(
        mixer_kernel,
        out_shape=(
            jax.ShapeDtypeStruct((3, 8, 64, 512), BF),
            jax.ShapeDtypeStruct((8, 64, 512), BF),
        ),
        in_specs=[any_spec] * (3 + len(TABLES)),
        out_specs=(any_spec, any_spec),
        scratch_shapes=scratch,
        compiler_params=pltpu.CompilerParams(
            collective_id=0, has_side_effects=True, vmem_limit_bytes=62 * 1024 * 1024
        ),
        name="mixer",
    )(
        force,
        mask,
        scalar,
        *[jnp.asarray(tables[name]) for name in TABLES],
    )
    return pl.pallas_call(
        place_kernel,
        out_shape=(
            jax.ShapeDtypeStruct((3, 8, 64, 512), BF),
            jax.ShapeDtypeStruct((8, 64, 512), BF),
        ),
        in_specs=[any_spec] * 2,
        out_specs=(any_spec, any_spec),
        scratch_shapes=[vm((4, 8, 64, 512), BF), dma((8,)), dma((8,))],
        name="place",
    )(velocity, conc)


def solution(mesh):
    placed = (P(None, "col", "row", None), P("col", "row", None), P("col", "row", None))
    return jax.shard_map(
        local,
        mesh=mesh,
        in_specs=placed,
        out_specs=(P(None, "col", "row", None), P("col", "row", None)),
        check_vma=False,
    )
```

```python
import numpy as np
import jax
import jax.numpy as jnp
import ml_dtypes
from jax import lax
from jax.experimental import pallas as pl
from jax.experimental.pallas import tpu as pltpu
from jax.sharding import PartitionSpec as P

SECTIONS = 5
MESH = pl.DeviceIdType.MESH
BF = jnp.bfloat16
F32 = jnp.float32
TWO_PI = 2.0 * np.pi
PLANE_ORDER = (
    (2, 2), (2, 1), (1, 2), (2, 3), (3, 2), (2, 0), (0, 2), (1, 1), (3, 3), (1, 3), (3, 1),
    (1, 0), (3, 0), (0, 1), (0, 3),
)


def numpy_tables():
    def half(values):
        return values.astype(np.float32).astype(ml_dtypes.bfloat16)

    x = np.arange(512)
    ri, d, k = (v.reshape(-1) for v in np.meshgrid(np.arange(2), np.arange(8), np.arange(16), indexing="ij"))
    e1, ri1, k1 = (v.reshape(-1) for v in np.meshgrid(np.arange(16), np.arange(2), np.arange(8), indexing="ij"))
    m = np.concatenate([d * 32 + k, (e1 // 2) * 32 + 16 + (e1 % 2) * 8 + k1])
    ri = np.concatenate([ri, ri1])
    angle = (np.outer(x, m) % 512) * (TWO_PI / 512)
    fx = np.where(ri == 0, np.cos(angle), -np.sin(angle)) / np.sqrt(512.0)
    bx = (fx * np.where(m == 0, 1.0, 2.0)).T
    y = np.arange(256)
    angle = (np.outer(y, y) % 256) * (TWO_PI / 256)
    c, s = np.cos(angle) / 16.0, np.sin(angle) / 16.0
    real = np.concatenate([c, s], 1).reshape(16, 1, 16, 512)
    imag = np.concatenate([-s, c], 1).reshape(16, 1, 16, 512)
    ty = np.concatenate([real, imag], 1).reshape(512, 512)
    uy = np.concatenate([c, s], 1)
    uyi = np.concatenate([c, -s], 1)
    n = np.arange(16)
    angle = (np.outer(n, n) % 16) * (TWO_PI / 16)
    c, s = np.cos(angle) / 4.0, np.sin(angle) / 4.0
    cs = np.zeros((8, 256, 512))
    csi = np.zeros((8, 256, 512))
    tw = np.zeros((8, 2, 16, 256))
    k = np.arange(16)
    for d in range(8):
        for low in range(2):
            for p in range(8):
                zp = low * 8 + (p - d) % 8
                at = low * 128 + p * 16
                for k2 in range(16):
                    cs[d, at + k, k2 * 16 + k] = c[zp, k2]
                    cs[d, at + k, 256 + k2 * 16 + k] = s[zp, k2]
                    csi[d, k2 * 16 + k, at + k] = c[zp, k2]
                    csi[d, k2 * 16 + k, 256 + at + k] = s[zp, k2]
                tw[d, 0, :, at : at + 16] = np.cos(TWO_PI * zp * n / 256)[:, None] / 4.0
                tw[d, 1, :, at : at + 16] = np.sin(TWO_PI * zp * n / 256)[:, None] / 4.0
    utw = np.zeros((16, 2, 16, 128))
    uz = np.zeros((8, 256, 256))
    k = np.arange(8)
    for turn in range(8):
        for low in range(2):
            for p in range(8):
                zp = low * 8 + (p - turn) % 8
                utw[low * 8 + turn, 0, :, p * 16 : p * 16 + 16] = np.cos(TWO_PI * zp * n / 256)[:, None] / 4.0
                utw[low * 8 + turn, 1, :, p * 16 : p * 16 + 16] = np.sin(TWO_PI * zp * n / 256)[:, None] / 4.0
                at = low * 128 + p * 16
                for k2 in range(16):
                    to = k2 * 16
                    uz[turn, at + k, to + k] = c[zp, k2]
                    uz[turn, at + 8 + k, to + k] = s[zp, k2]
                    uz[turn, at + k, to + 8 + k] = -s[zp, k2]
                    uz[turn, at + 8 + k, to + 8 + k] = c[zp, k2]
    return dict(
        uy=half(uy), uyi=half(uyi), uz=half(uz), uzi=half(uz.transpose(0, 2, 1)), utw=utw.astype(np.float32),
        fx=half(fx), bx=half(bx), ty=half(ty), tyi=half(ty.T), cs=half(cs), csi=half(csi),
        tw=tw.astype(np.float32),
    )


TABLES = ("fx", "ty", "utw", "tw", "cs", "uy", "uz", "csi", "uzi", "tyi", "uyi", "bx")
BY_D = ("cs", "tw", "csi")
BY_E = ("uz", "uzi")
VARIED = BY_D + BY_E + ("utw",)


def radix4(a, sign):
    def add(u, v):
        return u[0] + v[0], u[1] + v[1]

    def sub(u, v):
        return u[0] - v[0], u[1] - v[1]

    t0, t1 = add(a[0], a[2]), sub(a[0], a[2])
    t2, t3 = add(a[1], a[3]), sub(a[1], a[3])
    t3 = (t3[1], -t3[0]) if sign > 0 else (-t3[1], t3[0])
    return add(t0, t2), add(t1, t3), sub(t0, t2), sub(t1, t3)


def turned_by(value, j, sign):
    if j == 0:
        return value
    c, s = float(np.cos(TWO_PI * j / 16)), float(np.sin(TWO_PI * j / 16)) * sign
    re, im = value
    return re * c + im * s, im * c - re * s


def times_minus_i(value):
    imag = (lax.broadcasted_iota(jnp.int32, value.shape, 1) & 8) != 0
    return jnp.where(imag, -pltpu.roll(value, 8, 1), pltpu.roll(value, 120, 1))


def packed_radix4(a, sign):
    t0, t1, t2 = a[0] + a[2], a[0] - a[2], a[1] + a[3]
    t3 = times_minus_i(a[1] - a[3])
    if sign < 0:
        t3 = -t3
    return t0 + t2, t1 + t3, t0 - t2, t1 - t3


def packed_turned(value, j, sign):
    if j == 0:
        return value
    c, s = float(np.cos(TWO_PI * j / 16)), float(np.sin(TWO_PI * j / 16)) * sign
    return value * c + times_minus_i(value) * s


def packed_dft16(values, sign):
    parts = [packed_radix4(values[low::4], sign) for low in range(4)]
    parts = [[packed_turned(v, low * k, sign) for k, v in enumerate(parts[low])] for low in range(4)]
    out = [None] * 16
    for k in range(4):
        out[k::4] = packed_radix4([parts[low][k] for low in range(4)], sign)
    return out


def merge(tiles, place):
    for bit in (1, 2, 4):
        take = (place & bit) != 0
        tiles = [jnp.where(take, tiles[(m + bit) % 8], tiles[m]) for m in range(8)]
    return tiles


def dot(a, b):
    return jnp.dot(a, b, preferred_element_type=F32)


def mixer_kernel(*refs):
    force_h, mask_h, scalar_h = refs[:3]
    count = len(TABLES)
    tables_h = dict(zip(TABLES, refs[3 : 3 + count]))
    velocity_h, conc_h = refs[3 + count : 5 + count]
    (field, mask, scalar, *rest) = refs[5 + count :]
    tab = dict(zip(TABLES, rest[:count]))
    (gain, inv, sa, ra, sb, rb, sbi, rbi, sai, rai, spec, first, second, lines, big, mid,
     gain1, inv1, su, ru, sv, rv, svi, rvi, sui, rui, spec1, first1, second1, stacked, dots, dots1, summed, big1,
     u_send, u_recv, v_send, v_recv,
     zsend, zrecv, ysend, yrecv, edge, coef, state, conc,
     in_sem, tab_sem, a_send, a_recv, b_send, b_recv, z_ssem, z_rsem, y_ssem, y_rsem, out_sem) = rest[count:]

    r = lax.axis_index("row")
    col = lax.axis_index("col")
    e = col // 2
    xl = col % 2
    d = xl * 4 + r

    def load(source, target, sem):
        copy = pltpu.make_async_copy(source, target, sem)
        copy.start()
        return copy

    def load_table(name):
        source = tables_h[name]
        sem = tab_sem.at[TABLES.index(name)]
        if name in VARIED:
            source = source.at[d if name in BY_D else (e & 7) + (8 * xl if name == "utw" else 0)]
        return load(source, tab[name], sem)

    loads = {0: load(force_h.at[0], field.at[0], in_sem.at[0]), "fx": load_table("fx")}

    def load_rest():
        for i in (1, 2):
            loads[i] = load(force_h.at[i], field.at[i], in_sem.at[i])
        for name in TABLES[1:]:
            loads[name] = load_table(name)
        loads["scalar"] = load(scalar_h, scalar, in_sem.at[4])
        loads["mask"] = load(mask_h, mask, in_sem.at[3])

    core = r & 1
    x = (r // 2) * 2 + xl
    y_at, z_at = e // 4, e & 3

    def x_peer(step, of_core):
        at = (x + step * (1 + 2 * core)) & 3
        low = at & 1
        row = (at - low) + of_core
        return low * 4 + row, (row, e * 2 + low)

    def plane_peer(dy, dz):
        to = ((y_at + dy + core * (3 * dz - dy)) & 3) * 4 + ((z_at + dz + core * (3 * dy - dz)) & 3)
        return to, (r, to * 2 + xl)

    x_peers = [
        x_peer(step, core if same else 1 - core)
        for step, same in ((2, 1), (2, 0), (1, 1), (3, 1), (1, 0), (3, 0), (0, 0))
    ]
    plane_peers = [plane_peer(dy, dz) for dy, dz in PLANE_ORDER]

    y_up = (lax.rem(r + 1, 4), col)
    y_down = (lax.rem(r + 3, 4), col)

    barrier = pltpu.get_barrier_semaphore()

    for _, device in x_peers + plane_peers:
        pl.semaphore_signal(barrier, inc=1, device_id=device, device_id_type=MESH)
    across = (r, lax.rem(col + 31 + 2 * xl, 32))
    pl.semaphore_signal(barrier, inc=1, device_id=across, device_id_type=MESH)
    pl.semaphore_wait(barrier, 23)

    def remote(source, target, ssem, rsem, device):
        return pltpu.make_async_remote_copy(
            src_ref=source, dst_ref=target, send_sem=ssem, recv_sem=rsem,
            device_id=device, device_id_type=MESH)

    my_rows = pl.ds(pl.multiple_of(r * 64, 64), 64)
    my_slab = pl.ds(pl.multiple_of(e * 32, 32), 32)

    def send_a(t, i):
        target = ra.at[t, i, :, xl, my_rows]
        recv = a_recv.at[2 * t, i]

        for to, device in x_peers:
            remote(sa.at[i, to], target, a_send.at[2 * t, i], recv, device).start()
        pltpu.make_async_copy(sa.at[i, d], target, recv).start()

    def send_ai(t, i):
        target = rai.at[t, i, d]
        recv = a_recv.at[2 * t + 1, i]

        def piece(to):
            rows = pl.ds(pl.multiple_of((to & 3) * 64, 64), 64)
            return sai.at[i, :, to // 4, rows]

        for to, device in x_peers:
            remote(piece(to), target, a_send.at[2 * t + 1, i], recv, device).start()
        pltpu.make_async_copy(piece(d), target, recv).start()

    def send_b(source, into, k, t, i):
        target = into.at[t, i, my_slab]
        recv = b_recv.at[k, i]

        for to, device in plane_peers:
            slab = source.at[i, pl.ds(pl.multiple_of(to * 32, 32), 32)]
            remote(slab, target, b_send.at[k, i], recv, device).start()
        pltpu.make_async_copy(source.at[i, my_slab], target, recv).start()

    def send_u(source, into, k, t, c):
        target = into.at[t, c, e]
        recv = u_recv.at[k, c]
        for to, device in plane_peers:
            remote(source.at[c, to], target, u_send.at[k, c], recv, device).start()
        pltpu.make_async_copy(source.at[c, e], target, recv).start()

    def send_v(t, c):
        target = rv.at[t, c, :, xl, my_rows]
        recv = v_recv.at[2 * t, c]
        for to, device in x_peers:
            remote(sv.at[c, pl.ds(2 * to, 2)], target, v_send.at[2 * t, c], recv, device).start()
        pltpu.make_async_copy(sv.at[c, pl.ds(2 * d, 2)], target, recv).start()

    def send_vi(t, c):
        target = rvi.at[t, c, pl.ds(2 * d, 2)]
        recv = v_recv.at[2 * t + 1, c]

        def piece(to):
            rows = pl.ds(pl.multiple_of((to & 3) * 64, 64), 64)
            return svi.at[c, :, to // 4, rows]

        for to, device in x_peers:
            remote(piece(to), target, v_send.at[2 * t + 1, c], recv, device).start()
        pltpu.make_async_copy(piece(d), target, recv).start()

    def arrived(buffer, sem):
        pltpu.make_async_copy(buffer, buffer, sem).wait()

    def sent_a(k, i):
        arrived(sa.at[i, pl.ds(0, 7)], a_send.at[k, i])

    def sent_b(k, i):
        arrived(sb.at[i, pl.ds(0, 480)], b_send.at[k, i])

    def sent_u(k, i):
        arrived(su.at[i, pl.ds(0, 15)], u_send.at[k, i])

    def sent_v(k, i):
        arrived(sv.at[i, pl.ds(0, 14)], v_send.at[k, i])

    near, far = 1 - xl, xl

    def send_z(s, side, q):
        rows = pl.ds(16 * q, 16)
        remote(zsend.at[s, side, rows], zrecv.at[s, 1 - side, rows], z_ssem.at[s, side],
               z_rsem.at[s, 1 - side, q], (r, (col + 2 * side + 31) & 31)).start()

    def pack_edge(s, side):
        value = edge[...]
        ysend[s, side] = jnp.concatenate([value[:, 0:256], value[:, 256:512]], axis=0).astype(BF)

    def send_y(s, side):
        remote(ysend.at[s, side], yrecv.at[s, 1 - side], y_ssem.at[s, side], y_rsem.at[s, 1 - side],
               (y_down, y_up)[side]).start()

    place = lax.broadcasted_iota(jnp.int32, (64, 128), 1) // 16

    def x_forward(t, c):
        spread = dot(field[c].reshape(512, 512), tab["fx"][:, 0:256])
        for ri in range(2):
            tiles = []
            for z in range(8):
                tile = spread[z * 64 : z * 64 + 64, ri * 128 : ri * 128 + 128]
                tiles.append(pltpu.roll(tile, 16 * z, 1) if z else tile)
            tiles = merge(tiles, place)
            for to in range(8):
                sa[c, to, ri] = tiles[-to % 8].astype(BF)
        send_a(t, c)

    def x_forward1(t, c):
        spread = dot(field[c].reshape(512, 512), tab["fx"][:, 256:512])
        for j in range(2):
            tiles = []
            for z in range(8):
                tile = spread[z * 64 : z * 64 + 64, j * 128 : j * 128 + 128]
                tiles.append(pltpu.roll(tile, 16 * z, 1) if z else tile)
            tiles = merge(tiles, place)
            for to in range(8):
                su[c, 8 * j + to] = tiles[-to % 8].astype(BF)
        send_u(su, ru, 2 * t, t, c)

    def x_inverse(t, c):
        def gather(j):
            if j < 2:
                tiles = [rai[t, c, source, j].astype(F32) for source in range(8)]
            else:
                tiles = [rui[t, c, 8 * (j - 2) + source].astype(F32) for source in range(8)]
            tiles = merge(tiles, place)
            for z in range(8):
                tile = tiles[-z % 8]
                tile = pltpu.roll(tile, 128 - 16 * z, 1) if z else tile
                lines[z * 64 : z * 64 + 64, j * 128 : j * 128 + 128] = tile.astype(BF)

        arrived(rai.at[t, c], a_recv.at[2 * t + 1, c])
        gather(0)
        gather(1)
        summed[...] = dot(lines[:, 0:256], tab["bx"][0:256, :])
        arrived(rui.at[t, c], u_recv.at[2 * t + 1, c])
        gather(2)
        gather(3)
        values = (summed[...] + dot(lines[:, 256:512], tab["bx"][256:512, :])).astype(BF).reshape(8, 64, 512)
        if t == 0:
            values = (values.astype(F32) * mask[...].astype(F32)).astype(BF)
        field[c] = values

    def y_forward(t, i):
        arrived(ra.at[t, i], a_recv.at[2 * t, i])
        sides = [ra[t, i, :, side].reshape(512, 128) for side in range(2)]
        sb[i] = dot(tab["ty"][...], jnp.concatenate(sides, axis=1)).astype(BF)
        send_b(sb, rb, 2 * t, t, i)

    def y_inverse(t, i):
        arrived(rbi.at[t, i], b_recv.at[2 * t + 1, i])
        out = dot(tab["tyi"][...], rbi[t, i]).astype(BF)
        for side in range(2):
            sai[i, :, side] = out[:, side * 128 : side * 128 + 128].reshape(2, 256, 128)
        send_ai(t, i)

    def z_forward(t, i):
        for half in range(2):
            lanes = slice(half * 128, half * 128 + 128)

            def source(e_from, ri):
                return rb[t, i, e_from * 32 + ri * 16 : e_from * 32 + ri * 16 + 16, lanes].astype(F32)

            for low in range(4):
                out = radix4([(source(low + 4 * j, 0), source(low + 4 * j, 1)) for j in range(4)], 1)
                for k, value in enumerate(out):
                    mid[low, k, 0, :, lanes], mid[low, k, 1, :, lanes] = turned_by(value, low * k, 1)
            for k in range(4):
                out = radix4([(mid[low, k, 0, :, lanes], mid[low, k, 1, :, lanes]) for low in range(4)], 1)
                for high, (re, im) in enumerate(out):
                    k1 = k + 4 * high
                    wc, ws = tab["tw"][0, k1 : k1 + 1, lanes], tab["tw"][1, k1 : k1 + 1, lanes]
                    big[k1 * 16 : k1 * 16 + 16, lanes] = (re * wc + im * ws).astype(BF)
                    big[256 + k1 * 16 : 256 + k1 * 16 + 16, lanes] = (im * wc - re * ws).astype(BF)
        both = dot(big[...], tab["cs"][...])
        spec[i, 0] = both[:256, :256] + both[256:, 256:]
        spec[i, 1] = both[256:, :256] - both[:256, 256:]

    def z_inverse(source, t, i):
        both = dot(source[i].reshape(512, 256), tab["csi"][...])
        for half in range(2):
            lanes = slice(half * 128, half * 128 + 128)
            other = slice(256 + half * 128, 256 + half * 128 + 128)

            def value(k1):
                upper, lower = slice(k1 * 16, k1 * 16 + 16), slice(256 + k1 * 16, 256 + k1 * 16 + 16)
                re = both[upper, lanes] - both[lower, other]
                im = both[lower, lanes] + both[upper, other]
                wc, ws = tab["tw"][0, k1 : k1 + 1, lanes], tab["tw"][1, k1 : k1 + 1, lanes]
                return re * wc - im * ws, im * wc + re * ws

            for low in range(4):
                out = radix4([value(low + 4 * j) for j in range(4)], -1)
                for k, turned in enumerate(out):
                    mid[low, k, 0, :, lanes], mid[low, k, 1, :, lanes] = turned_by(turned, low * k, -1)
            for k in range(4):
                out = radix4([(mid[low, k, 0, :, lanes], mid[low, k, 1, :, lanes]) for low in range(4)], -1)
                for high, (re, im) in enumerate(out):
                    to = (k + 4 * high) * 32
                    sbi[i, to : to + 16, lanes] = re.astype(BF)
                    sbi[i, to + 16 : to + 32, lanes] = im.astype(BF)
        send_b(sbi, rbi, 2 * t + 1, t, i)

    def v_forward(t, c):
        arrived(ru.at[t, c], u_recv.at[2 * t, c])

        def some(n, carry):
            rows = pl.ds(pl.multiple_of(n * 16, 16), 16)
            out = packed_dft16([ru[t, c, j, rows].astype(F32) for j in range(16)], 1)
            for k1, value in enumerate(out):
                wc, ws = tab["utw"][0, k1 : k1 + 1], tab["utw"][1, k1 : k1 + 1]
                sv[c, k1, rows] = (value * wc + times_minus_i(value) * ws).astype(BF)
            return carry

        lax.fori_loop(0, 4, some, 0)
        send_v(t, c)

    def v_inverse(t, c):
        arrived(rvi.at[t, c], v_recv.at[2 * t + 1, c])

        def some(n, carry):
            rows = pl.ds(pl.multiple_of(n * 16, 16), 16)
            values = []
            for k1 in range(16):
                value = rvi[t, c, k1, rows].astype(F32)
                wc, ws = tab["utw"][0, k1 : k1 + 1], tab["utw"][1, k1 : k1 + 1]
                values.append(value * wc - times_minus_i(value) * ws)
            for j, value in enumerate(packed_dft16(values, -1)):
                sui[c, j, rows] = value.astype(BF)
            return carry

        lax.fori_loop(0, 4, some, 0)
        send_u(sui, rui, 2 * t + 1, t, c)

    def y_product(table, values, wide):
        for half in range(2):
            lanes = slice(half * 128, half * 128 + 128)
            stacked[256:512, lanes] = times_minus_i(wide[:, lanes]).astype(BF)
        stacked[0:256, :] = values
        return dot(table, stacked[...]).astype(BF)

    def w_forward(t, c):
        for k1 in range(2):
            values = jnp.concatenate([rv[t, c, k1, 0], rv[t, c, k1, 1]], axis=1)
            big1[k1 * 256 : k1 * 256 + 256, :] = y_product(tab["uy"][...], values, values.astype(F32))
        spec1[c] = dot(big1[...], tab["uz"][...])

    def w_inverse(source, t, c):
        wide = dot(source[c], tab["uzi"][...])
        for k1 in range(2):
            part = wide[k1 * 256 : k1 * 256 + 256]
            out = y_product(tab["uyi"][...], part.astype(BF), part)
            for side in range(2):
                svi[c, k1, side] = out[:, side * 128 : side * 128 + 128]
        send_vi(t, c)

    lane = lax.broadcasted_iota(jnp.int32, (16, 256), 1)
    unit_long, unit = np.float32(TWO_PI / 512), np.float32(TWO_PI / 256)
    index_y = e * 16 + lax.broadcasted_iota(jnp.int32, (16, 256), 0)
    wave_y = jnp.where(index_y < 128, index_y, index_y - 256).astype(F32) * unit

    wave_x = (d * 32 + (lane & 15)).astype(F32) * unit_long
    wave_x1 = ((e // 2) * 32 + 16 + (e & 1) * 8 + (lane & 7)).astype(F32) * unit_long

    def along_z(k1):
        index_z = k1 + 16 * (lane // 16)
        return index_z, jnp.where(index_z < 128, index_z, index_z - 256).astype(F32) * unit

    def at_rows(n):
        return pl.ds(pl.multiple_of(n * 16, 16), 16)

    def along_y1(n):
        index = (n & 15) * 16 + lax.broadcasted_iota(jnp.int32, (16, 256), 0)
        return index, jnp.where(index < 128, index, index - 256).astype(F32) * unit

    def scales(kx, ky, kz, edge):
        ksq = kx * kx + ky * ky + kz * kz
        return (
            jnp.where(edge, 0.0, 1.0 / (0.05 * ksq + 0.5)),
            jnp.where(ksq > 0.0, 1.0 / jnp.where(ksq > 0.0, ksq, 1.0), 0.0),
        )

    def factors(n, carry):
        index_z, wave_z = along_z(n)
        gain[at_rows(n)], inv[at_rows(n)] = scales(wave_x, wave_y, wave_z, (index_y == 128) | (index_z == 128))
        return carry

    def factors1(n, carry):
        index_z, wave_z = along_z(2 * d + n // 16)
        index, wave = along_y1(n)
        gain1[at_rows(n)], inv1[at_rows(n)] = scales(wave_x1, wave, wave_z, (index == 128) | (index_z == 128))
        return carry

    def parts():
        def one(n, carry):
            rows = at_rows(n)
            for ri in range(2):
                dots[ri, rows] = wave_x * spec[0, ri, rows] + wave_y * spec[1, ri, rows]
            return carry

        lax.fori_loop(0, 16, one, 0)

    def keep(t, kept, result, at, value):
        if t == 0:
            kept[at] = value.astype(BF)
        else:
            result[at] = (kept[at].astype(F32) - value).astype(BF)

    def project_x(t):
        def one(n, carry):
            rows = at_rows(n)
            wave_z = along_z(n)[1]
            for ri in range(2):
                along = (dots[ri, rows] + wave_z * spec[2, ri, rows]) * inv[rows]
                dots[ri, rows] = along
                keep(t, first, second, (0, ri, rows), gain[rows] * (spec[0, ri, rows] - wave_x * along))
            return carry

        lax.fori_loop(0, 16, one, 0)

    def project_yz(t):
        def one(n, carry):
            rows = at_rows(n)
            waves = (wave_x, wave_y, along_z(n)[1])
            for ri in range(2):
                along = dots[ri, rows]
                for c in (1, 2):
                    keep(t, first, second, (c, ri, rows), gain[rows] * (spec[c, ri, rows] - waves[c] * along))
            return carry

        lax.fori_loop(0, 16, one, 0)

    def parts1():
        def one(n, carry):
            rows = at_rows(n)
            dots1[rows] = wave_x1 * spec1[0, rows] + along_y1(n)[1] * spec1[1, rows]
            return carry

        lax.fori_loop(0, 32, one, 0)

    def project1_x(t):
        def one(n, carry):
            rows = at_rows(n)
            along = (dots1[rows] + along_z(2 * d + n // 16)[1] * spec1[2, rows]) * inv1[rows]
            dots1[rows] = along
            keep(t, first1, second1, (0, rows), gain1[rows] * (spec1[0, rows] - wave_x1 * along))
            return carry

        lax.fori_loop(0, 32, one, 0)

    def project1_yz(t):
        def one(n, carry):
            rows = at_rows(n)
            waves = (wave_x1, along_y1(n)[1], along_z(2 * d + n // 16)[1])
            along = dots1[rows]
            for c in (1, 2):
                keep(t, first1, second1, (c, rows), gain1[rows] * (spec1[c, rows] - waves[c] * along))
            return carry

        lax.fori_loop(0, 32, one, 0)

    def each(count, step):
        def body(i, _):
            step(i)
            return _

        lax.fori_loop(0, count, body, 0)

    def spectral(t, source, source1):
        def out(c):
            y_forward(t, c)
            v_forward(t, c)

        def inner_arrived(c):
            arrived(rv.at[t, c], v_recv.at[2 * t, c])
            arrived(rb.at[t, c], b_recv.at[2 * t, c])

        def inner(c):
            inner_arrived(c)
            w_forward(t, c)
            z_forward(t, c)

        def outer(c):
            w_inverse(source1, t, c + 1)
            z_inverse(source, t, c + 1)

        def back(c):
            v_inverse(t, c)
            y_inverse(t, c)

        each(3, out)
        each(2, inner)
        parts1()
        parts()
        inner_arrived(2)
        w_forward(t, 2)
        z_forward(t, 2)
        project1_x(t)
        w_inverse(source1, t, 0)
        project_x(t)
        z_inverse(source, t, 0)
        project1_yz(t)
        project_yz(t)
        each(2, outer)
        each(3, back)

    def start(c):
        @pl.when(c > 0)
        def _():
            arrived(field.at[c], in_sem.at[c])

        x_forward(0, c)
        x_forward1(0, c)

    loads["fx"].wait()
    loads[0].wait()
    load_rest()
    each(3, start)
    lax.fori_loop(0, 16, factors, 0)
    lax.fori_loop(0, 32, factors1, 0)
    loads["scalar"].wait()
    for z in range(8):
        state[0, z + 1, pl.ds(8, 64), :] = scalar[z].astype(F32)
    zsend[0, 0] = scalar[0]
    zsend[0, 1] = scalar[7]
    for side in (far, near):
        for q in range(4):
            send_z(0, side, q)
    for side in range(2):
        for z in range(8):
            edge[pl.ds(z, 1), :] = state[0, z + 1, pl.ds(8 + 63 * side, 1), :]
        pack_edge(0, side)
        send_y(0, side)
    for name in TABLES[1:]:
        loads[name].wait()
    loads["mask"].wait()
    spectral(0, first, first1)

    def sent(t, c):
        for k in (2 * t, 2 * t + 1):
            sent_a(k, c)
            sent_b(k, c)
            sent_u(k, c)
            sent_v(k, c)

    def middle(c):
        x_inverse(0, c)
        sent(0, c)
        x_forward(1, c)
        x_forward1(1, c)

    each(3, middle)
    spectral(1, second, second1)

    def coefficients(z, c):
        fluid = 0.25 * (1.0 - mask[z].astype(F32))
        u = field[c, z].astype(F32)
        below = fluid * (0.25 + jnp.maximum(u, 0.0))
        above = fluid * (0.25 - jnp.minimum(u, 0.0))
        coef[2 * c, z] = below
        coef[2 * c + 1, z] = above
        start = jnp.where(c == 0, jnp.ones_like(u), coef[6, z])
        coef[6, z] = start - (below + above)
        return c

    def last(c):
        x_inverse(1, c)
        pltpu.make_async_copy(field.at[c], velocity_h.at[c], out_sem.at[c]).start()

        @pl.when(c < 2)
        def _():
            lax.fori_loop(0, 8, coefficients, c)

    each(3, last)

    def block(s, z, q):
        now, later = s & 1, (s + 1) & 1
        at = 8 + 16 * q
        rows, cells = pl.ds(at, 16), pl.ds(16 * q, 16)
        center = state[now, z, rows]
        new = coef[6, z - 1, cells] * center
        new = new + coef[0, z - 1, cells] * pltpu.roll(center, 1, 1)
        new = new + coef[1, z - 1, cells] * pltpu.roll(center, 511, 1)
        new = new + coef[2, z - 1, cells] * state[now, z, pl.ds(at - 1, 16)]
        new = new + coef[3, z - 1, cells] * state[now, z, pl.ds(at + 1, 16)]
        new = new + coef[4, z - 1, cells] * state[now, z - 1, rows]
        new = new + coef[5, z - 1, cells] * state[now, z + 1, rows]
        state[later, z, rows] = new
        return new

    def outer_block(s, side, q):
        cells = pl.ds(16 * q, 16)
        arrived(zrecv.at[s, side, cells], z_rsem.at[s, side, q])
        state[s & 1, 9 * side, pl.ds(8 + 16 * q, 16)] = zrecv[s, side, cells].astype(F32)
        face = block(s, 1 + 7 * side, q)

        @pl.when(s < SECTIONS - 1)
        def _():
            zsend[s + 1, side, cells] = face.astype(BF)
            send_z(s + 1, side, q)

    def y_halo(s):
        for side in range(2):
            arrived(yrecv.at[s, side], y_rsem.at[s, side])
            halo = yrecv[s, side].astype(F32)
            for z in range(8):
                for half in range(2):
                    lanes = slice(half * 256, half * 256 + 256)
                    state[s & 1, z + 1, pl.ds(7 + 65 * side, 1), lanes] = halo[8 * half + z : 8 * half + z + 1]

    def store_planes(z, count):
        planes = pl.ds(z, count)
        return pltpu.make_async_copy(conc.at[planes], conc_h.at[planes], out_sem.at[3 + (0, 1, 0, 0, 0, 0, 0, 2)[z]])

    def section(s, carry):
        @pl.when(s == SECTIONS - 1)
        def _():
            y_halo(s)

        for q in (0, 3, 1, 2):
            outer_block(s, near, q)
            for z in range(2, 8):
                block(s, z, q)
            if q in (0, 3):
                side = q // 3

                @pl.when(s < SECTIONS - 1)
                def _():
                    for z in range(8):
                        edge[pl.ds(z, 1), :] = state[(s + 1) & 1, z + 1, pl.ds(8 + 63 * side, 1), :]
                    pack_edge(s + 1, side)
                    send_y(s + 1, side)

        @pl.when(s == SECTIONS - 1)
        def _():
            conc[pl.ds(1, 6)] = state[SECTIONS % 2, pl.ds(2, 6), pl.ds(8, 64), :].astype(BF)
            store_planes(1, 6).start()

        following = jnp.minimum(s + 1, SECTIONS - 1)

        @pl.when(s != SECTIONS - 2)
        def _():
            for q in (1, 2):
                outer_block(following, far, q)

        @pl.when(s < SECTIONS - 2)
        def _():
            y_halo(s + 1)

        @pl.when(s != SECTIONS - 2)
        def _():
            for q in (0, 3):
                outer_block(following, far, q)

        return carry

    y_halo(0)
    coefficients(7 * far, 2)
    for q in (1, 2, 0, 3):
        outer_block(0, far, q)
    lax.fori_loop(0, 7, lambda n, carry: coefficients(n + near, carry), 2)
    lax.fori_loop(0, SECTIONS, section, 0)
    for z in (0, 7):
        conc[z] = state[SECTIONS % 2, z + 1, pl.ds(8, 64), :].astype(BF)
        store_planes(z, 1).start()

    each(3, lambda c: sent(1, c))
    for s in range(SECTIONS):
        for i in range(2):
            arrived(zsend.at[s, i], z_ssem.at[s, i])
            arrived(ysend.at[s, i], y_ssem.at[s, i])
    for c in range(3):
        pltpu.make_async_copy(field.at[c], velocity_h.at[c], out_sem.at[c]).wait()
    for z, count in ((0, 1), (1, 6), (7, 1)):
        store_planes(z, count).wait()


def place_kernel(velocity_in, conc_in, velocity, conc, held, in_sem, out_sem):
    pairs = []
    for half in range(2):
        planes = pl.ds(4 * half, 4)
        pairs += [(velocity_in.at[c, planes], held.at[c, planes], velocity.at[c, planes]) for c in range(3)]
        pairs.append((conc_in.at[planes], held.at[3, planes], conc.at[planes]))
    loads = [pltpu.make_async_copy(a, b, in_sem.at[i]) for i, (a, b, _) in enumerate(pairs)]
    stores = [pltpu.make_async_copy(b, c, out_sem.at[i]) for i, (_, b, c) in enumerate(pairs)]
    for copy in loads:
        copy.start()
    for load, store in zip(loads, stores):
        load.wait()
        store.start()
    for copy in stores:
        copy.wait()


def local(force, mask, scalar):
    tables = numpy_tables()
    vm = pltpu.VMEM
    dma = pltpu.SemaphoreType.DMA
    scratch = [vm((3, 8, 64, 512), BF), vm((8, 64, 512), jnp.int32), vm((8, 64, 512), BF)]
    for name in TABLES:
        value = tables[name]
        shape = value.shape[1:] if name in VARIED else value.shape
        scratch.append(vm(shape, value.dtype))
    scratch += [
        vm((256, 256), F32), vm((256, 256), F32),
        vm((3, 8, 2, 64, 128), BF), vm((2, 3, 2, 2, 256, 128), BF),
        vm((3, 512, 256), BF), vm((2, 3, 512, 256), BF),
        vm((3, 512, 256), BF), vm((2, 3, 512, 256), BF),
        vm((3, 2, 2, 256, 128), BF), vm((2, 3, 8, 2, 64, 128), BF),
        vm((3, 2, 256, 256), F32), vm((3, 2, 256, 256), BF), vm((3, 2, 256, 256), BF),
        vm((512, 512), BF), vm((512, 256), BF), vm((4, 4, 2, 16, 256), F32),
        vm((512, 256), F32), vm((512, 256), F32),
        vm((3, 16, 64, 128), BF), vm((2, 3, 16, 64, 128), BF),
        vm((3, 16, 64, 128), BF), vm((2, 3, 2, 2, 256, 128), BF),
        vm((3, 2, 2, 256, 128), BF), vm((2, 3, 16, 64, 128), BF),
        vm((3, 16, 64, 128), BF), vm((2, 3, 16, 64, 128), BF),
        vm((3, 512, 256), F32), vm((3, 512, 256), BF), vm((3, 512, 256), BF),
        vm((512, 256), BF), vm((2, 256, 256), F32), vm((512, 256), F32),
        vm((512, 512), F32), vm((512, 256), BF),
        dma((4, 3)), dma((4, 3)), dma((4, 3)), dma((4, 3)),
        vm((SECTIONS, 2, 64, 512), BF), vm((SECTIONS, 2, 64, 512), BF),
        vm((SECTIONS, 2, 16, 256), BF), vm((SECTIONS, 2, 16, 256), BF), vm((8, 512), F32),
        vm((7, 8, 64, 512), F32), vm((2, 10, 80, 512), F32), vm((8, 64, 512), BF),
        dma((5,)), dma((len(TABLES),)),
        dma((4, 3)), dma((4, 3)), dma((4, 3)), dma((4, 3)),
        dma((SECTIONS, 2)), dma((SECTIONS, 2, 4)), dma((SECTIONS, 2)), dma((SECTIONS, 2)),
        dma((6,)),
    ]
    any_spec = pl.BlockSpec(memory_space=pl.ANY)
    velocity, conc = pl.pallas_call(
        mixer_kernel,
        out_shape=(
            jax.ShapeDtypeStruct((3, 8, 64, 512), BF),
            jax.ShapeDtypeStruct((8, 64, 512), BF),
        ),
        in_specs=[any_spec] * (3 + len(TABLES)),
        out_specs=(any_spec, any_spec),
        scratch_shapes=scratch,
        compiler_params=pltpu.CompilerParams(
            collective_id=0, has_side_effects=True, vmem_limit_bytes=52 * 1024 * 1024
        ),
        name="mixer",
    )(
        force,
        mask,
        scalar,
        *[jnp.asarray(tables[name]) for name in TABLES],
    )
    return pl.pallas_call(
        place_kernel,
        out_shape=(
            jax.ShapeDtypeStruct((3, 8, 64, 512), BF),
            jax.ShapeDtypeStruct((8, 64, 512), BF),
        ),
        in_specs=[any_spec] * 2,
        out_specs=(any_spec, any_spec),
        scratch_shapes=[vm((4, 8, 64, 512), BF), dma((8,)), dma((8,))],
        name="place",
    )(velocity, conc)


def solution(mesh):
    placed = (P(None, "col", "row", None), P("col", "row", None), P("col", "row", None))
    return jax.shard_map(
        local,
        mesh=mesh,
        in_specs=placed,
        out_specs=(P(None, "col", "row", None), P("col", "row", None)),
        check_vma=False,
    )
```

```python
import numpy as np
import jax
import jax.numpy as jnp
import ml_dtypes
from jax import lax
from jax.experimental import pallas as pl
from jax.experimental.pallas import tpu as pltpu
from jax.sharding import PartitionSpec as P

SECTIONS = 5
MESH = pl.DeviceIdType.MESH
BF = jnp.bfloat16
F32 = jnp.float32
TWO_PI = 2.0 * np.pi
PLANE_ORDER = (
    (2, 2), (2, 1), (1, 2), (2, 3), (3, 2), (2, 0), (0, 2), (1, 1), (3, 3), (1, 3), (3, 1),
    (1, 0), (3, 0), (0, 1), (0, 3),
)


def numpy_tables():
    def half(values):
        return values.astype(np.float32).astype(ml_dtypes.bfloat16)

    x = np.arange(512)
    ri, d, k = (v.reshape(-1) for v in np.meshgrid(np.arange(2), np.arange(8), np.arange(16), indexing="ij"))
    e1, ri1, k1 = (v.reshape(-1) for v in np.meshgrid(np.arange(16), np.arange(2), np.arange(8), indexing="ij"))
    m = np.concatenate([d * 32 + k, (e1 // 2) * 32 + 16 + (e1 % 2) * 8 + k1])
    ri = np.concatenate([ri, ri1])
    angle = (np.outer(x, m) % 512) * (TWO_PI / 512)
    fx = np.where(ri == 0, np.cos(angle), -np.sin(angle)) / np.sqrt(512.0)
    bx = (fx * np.where(m == 0, 1.0, 2.0)).T
    y = np.arange(256)
    angle = (np.outer(y, y) % 256) * (TWO_PI / 256)
    c, s = np.cos(angle) / 16.0, np.sin(angle) / 16.0
    real = np.concatenate([c, s], 1).reshape(16, 1, 16, 512)
    imag = np.concatenate([-s, c], 1).reshape(16, 1, 16, 512)
    ty = np.concatenate([real, imag], 1).reshape(512, 512)
    uy = np.concatenate([c, s], 1)
    uyi = np.concatenate([c, -s], 1)
    n = np.arange(16)
    angle = (np.outer(n, n) % 16) * (TWO_PI / 16)
    c, s = np.cos(angle) / 4.0, np.sin(angle) / 4.0
    cs = np.zeros((8, 256, 512))
    csi = np.zeros((8, 256, 512))
    tw = np.zeros((8, 2, 16, 256))
    k = np.arange(16)
    for d in range(8):
        for low in range(2):
            for p in range(8):
                zp = low * 8 + (p - d) % 8
                at = low * 128 + p * 16
                for k2 in range(16):
                    cs[d, at + k, k2 * 16 + k] = c[zp, k2]
                    cs[d, at + k, 256 + k2 * 16 + k] = s[zp, k2]
                    csi[d, k2 * 16 + k, at + k] = c[zp, k2]
                    csi[d, k2 * 16 + k, 256 + at + k] = s[zp, k2]
                tw[d, 0, :, at : at + 16] = np.cos(TWO_PI * zp * n / 256)[:, None] / 4.0
                tw[d, 1, :, at : at + 16] = np.sin(TWO_PI * zp * n / 256)[:, None] / 4.0
    utw = np.zeros((16, 2, 16, 128))
    uz = np.zeros((8, 256, 256))
    k = np.arange(8)
    for turn in range(8):
        for low in range(2):
            for p in range(8):
                zp = low * 8 + (p - turn) % 8
                utw[low * 8 + turn, 0, :, p * 16 : p * 16 + 16] = np.cos(TWO_PI * zp * n / 256)[:, None] / 4.0
                utw[low * 8 + turn, 1, :, p * 16 : p * 16 + 16] = np.sin(TWO_PI * zp * n / 256)[:, None] / 4.0
                at = low * 128 + p * 16
                for k2 in range(16):
                    to = k2 * 16
                    uz[turn, at + k, to + k] = c[zp, k2]
                    uz[turn, at + 8 + k, to + k] = s[zp, k2]
                    uz[turn, at + k, to + 8 + k] = -s[zp, k2]
                    uz[turn, at + 8 + k, to + 8 + k] = c[zp, k2]
    return dict(
        uy=half(uy), uyi=half(uyi), uz=half(uz), uzi=half(uz.transpose(0, 2, 1)), utw=utw.astype(np.float32),
        fx=half(fx), bx=half(bx), ty=half(ty), tyi=half(ty.T), cs=half(cs), csi=half(csi),
        tw=tw.astype(np.float32),
    )


TABLES = ("fx", "ty", "utw", "tw", "cs", "uy", "uz", "csi", "uzi", "tyi", "uyi", "bx")
BY_D = ("cs", "tw", "csi")
BY_E = ("uz", "uzi")
VARIED = BY_D + BY_E + ("utw",)


def radix4(a, sign):
    def add(u, v):
        return u[0] + v[0], u[1] + v[1]

    def sub(u, v):
        return u[0] - v[0], u[1] - v[1]

    t0, t1 = add(a[0], a[2]), sub(a[0], a[2])
    t2, t3 = add(a[1], a[3]), sub(a[1], a[3])
    t3 = (t3[1], -t3[0]) if sign > 0 else (-t3[1], t3[0])
    return add(t0, t2), add(t1, t3), sub(t0, t2), sub(t1, t3)


def turned_by(value, j, sign):
    if j == 0:
        return value
    c, s = float(np.cos(TWO_PI * j / 16)), float(np.sin(TWO_PI * j / 16)) * sign
    re, im = value
    return re * c + im * s, im * c - re * s


def times_minus_i(value):
    imag = (lax.broadcasted_iota(jnp.int32, value.shape, 1) & 8) != 0
    return jnp.where(imag, -pltpu.roll(value, 8, 1), pltpu.roll(value, 120, 1))


def packed_radix4(a, sign):
    t0, t1, t2 = a[0] + a[2], a[0] - a[2], a[1] + a[3]
    t3 = times_minus_i(a[1] - a[3])
    if sign < 0:
        t3 = -t3
    return t0 + t2, t1 + t3, t0 - t2, t1 - t3


def packed_turned(value, j, sign):
    if j == 0:
        return value
    c, s = float(np.cos(TWO_PI * j / 16)), float(np.sin(TWO_PI * j / 16)) * sign
    return value * c + times_minus_i(value) * s


def packed_dft16(values, sign):
    parts = [packed_radix4(values[low::4], sign) for low in range(4)]
    parts = [[packed_turned(v, low * k, sign) for k, v in enumerate(parts[low])] for low in range(4)]
    out = [None] * 16
    for k in range(4):
        out[k::4] = packed_radix4([parts[low][k] for low in range(4)], sign)
    return out


def merge(tiles, place):
    for bit in (1, 2, 4):
        take = (place & bit) != 0
        tiles = [jnp.where(take, tiles[(m + bit) % 8], tiles[m]) for m in range(8)]
    return tiles


def dot(a, b):
    return jnp.dot(a, b, preferred_element_type=F32)


def mixer_kernel(*refs):
    force_h, mask_h, scalar_h = refs[:3]
    count = len(TABLES)
    tables_h = dict(zip(TABLES, refs[3 : 3 + count]))
    velocity_h, conc_h = refs[3 + count : 5 + count]
    (field, mask, scalar, *rest) = refs[5 + count :]
    tab = dict(zip(TABLES, rest[:count]))
    (gain, inv, sa, ra, sb, rb, sbi, rbi, sai, rai, spec, first, second, lines, big, mid,
     gain1, inv1, su, ru, sv, rv, svi, rvi, sui, rui, spec1, first1, second1, stacked, dots, dots1, summed, big1,
     u_send, u_recv, v_send, v_recv,
     zsend, zrecv, ysend, yrecv, edge, coef, state, conc,
     in_sem, tab_sem, a_send, a_recv, b_send, b_recv, z_ssem, z_rsem, y_ssem, y_rsem, out_sem) = rest[count:]

    r = lax.axis_index("row")
    col = lax.axis_index("col")
    e = col // 2
    xl = col % 2
    d = xl * 4 + r

    def load(source, target, sem):
        copy = pltpu.make_async_copy(source, target, sem)
        copy.start()
        return copy

    def load_table(name):
        source = tables_h[name]
        sem = tab_sem.at[TABLES.index(name)]
        if name in VARIED:
            source = source.at[d if name in BY_D else (e & 7) + (8 * xl if name == "utw" else 0)]
        return load(source, tab[name], sem)

    loads = {0: load(force_h.at[0], field.at[0], in_sem.at[0]), "fx": load_table("fx")}

    def load_rest():
        for i in (1, 2):
            loads[i] = load(force_h.at[i], field.at[i], in_sem.at[i])
        for name in TABLES[1:]:
            loads[name] = load_table(name)
        loads["scalar"] = load(scalar_h, scalar, in_sem.at[4])
        loads["mask"] = load(mask_h, mask, in_sem.at[3])

    core = r & 1
    x = (r // 2) * 2 + xl
    y_at, z_at = e // 4, e & 3

    def x_peer(step, of_core):
        at = (x + step * (1 + 2 * core)) & 3
        low = at & 1
        row = (at - low) + of_core
        return low * 4 + row, (row, e * 2 + low)

    def plane_peer(dy, dz):
        to = ((y_at + dy + core * (3 * dz - dy)) & 3) * 4 + ((z_at + dz + core * (3 * dy - dz)) & 3)
        return to, (r, to * 2 + xl)

    x_peers = [
        x_peer(step, core if same else 1 - core)
        for step, same in ((2, 1), (2, 0), (1, 1), (3, 1), (1, 0), (3, 0), (0, 0))
    ]
    plane_peers = [plane_peer(dy, dz) for dy, dz in PLANE_ORDER]

    y_up = (lax.rem(r + 1, 4), col)
    y_down = (lax.rem(r + 3, 4), col)

    barrier = pltpu.get_barrier_semaphore()

    for _, device in x_peers + plane_peers:
        pl.semaphore_signal(barrier, inc=1, device_id=device, device_id_type=MESH)
    across = (r, lax.rem(col + 31 + 2 * xl, 32))
    pl.semaphore_signal(barrier, inc=1, device_id=across, device_id_type=MESH)
    pl.semaphore_wait(barrier, 23)

    def remote(source, target, ssem, rsem, device):
        return pltpu.make_async_remote_copy(
            src_ref=source, dst_ref=target, send_sem=ssem, recv_sem=rsem,
            device_id=device, device_id_type=MESH)

    my_rows = pl.ds(pl.multiple_of(r * 64, 64), 64)
    my_slab = pl.ds(pl.multiple_of(e * 32, 32), 32)

    def send_a(t, i):
        target = ra.at[t, i, :, xl, my_rows]
        recv = a_recv.at[2 * t, i]

        for to, device in x_peers:
            remote(sa.at[i, to], target, a_send.at[2 * t, i], recv, device).start()
        pltpu.make_async_copy(sa.at[i, d], target, recv).start()

    def send_ai(t, i):
        target = rai.at[t, i, d]
        recv = a_recv.at[2 * t + 1, i]

        def piece(to):
            rows = pl.ds(pl.multiple_of((to & 3) * 64, 64), 64)
            return sai.at[i, :, to // 4, rows]

        for to, device in x_peers:
            remote(piece(to), target, a_send.at[2 * t + 1, i], recv, device).start()
        pltpu.make_async_copy(piece(d), target, recv).start()

    def send_b(source, into, k, t, i):
        target = into.at[t, i, my_slab]
        recv = b_recv.at[k, i]

        for to, device in plane_peers:
            slab = source.at[i, pl.ds(pl.multiple_of(to * 32, 32), 32)]
            remote(slab, target, b_send.at[k, i], recv, device).start()
        pltpu.make_async_copy(source.at[i, my_slab], target, recv).start()

    def send_u(source, into, k, t, c):
        target = into.at[t, c, e]
        recv = u_recv.at[k, c]
        for to, device in plane_peers:
            remote(source.at[c, to], target, u_send.at[k, c], recv, device).start()
        pltpu.make_async_copy(source.at[c, e], target, recv).start()

    def send_v(t, c):
        target = rv.at[t, c, :, xl, my_rows]
        recv = v_recv.at[2 * t, c]
        for to, device in x_peers:
            remote(sv.at[c, pl.ds(2 * to, 2)], target, v_send.at[2 * t, c], recv, device).start()
        pltpu.make_async_copy(sv.at[c, pl.ds(2 * d, 2)], target, recv).start()

    def send_vi(t, c):
        target = rvi.at[t, c, pl.ds(2 * d, 2)]
        recv = v_recv.at[2 * t + 1, c]

        def piece(to):
            rows = pl.ds(pl.multiple_of((to & 3) * 64, 64), 64)
            return svi.at[c, :, to // 4, rows]

        for to, device in x_peers:
            remote(piece(to), target, v_send.at[2 * t + 1, c], recv, device).start()
        pltpu.make_async_copy(piece(d), target, recv).start()

    def arrived(buffer, sem):
        pltpu.make_async_copy(buffer, buffer, sem).wait()

    def sent_a(k, i):
        arrived(sa.at[i, pl.ds(0, 7)], a_send.at[k, i])

    def sent_b(k, i):
        arrived(sb.at[i, pl.ds(0, 480)], b_send.at[k, i])

    def sent_u(k, i):
        arrived(su.at[i, pl.ds(0, 15)], u_send.at[k, i])

    def sent_v(k, i):
        arrived(sv.at[i, pl.ds(0, 14)], v_send.at[k, i])

    near, far = 1 - xl, xl

    def send_z(s, side, q):
        rows = pl.ds(16 * q, 16)
        remote(zsend.at[s, side, rows], zrecv.at[s, 1 - side, rows], z_ssem.at[s, side],
               z_rsem.at[s, 1 - side, q], (r, (col + 2 * side + 31) & 31)).start()

    def pack_edge(s, side):
        value = edge[...]
        ysend[s, side] = jnp.concatenate([value[:, 0:256], value[:, 256:512]], axis=0).astype(BF)

    def send_y(s, side):
        remote(ysend.at[s, side], yrecv.at[s, 1 - side], y_ssem.at[s, side], y_rsem.at[s, 1 - side],
               (y_down, y_up)[side]).start()

    place = lax.broadcasted_iota(jnp.int32, (64, 128), 1) // 16

    def x_forward(t, c):
        spread = dot(field[c].reshape(512, 512), tab["fx"][:, 0:256])
        for ri in range(2):
            tiles = []
            for z in range(8):
                tile = spread[z * 64 : z * 64 + 64, ri * 128 : ri * 128 + 128]
                tiles.append(pltpu.roll(tile, 16 * z, 1) if z else tile)
            tiles = merge(tiles, place)
            for to in range(8):
                sa[c, to, ri] = tiles[-to % 8].astype(BF)
        send_a(t, c)

    def x_forward1(t, c):
        spread = dot(field[c].reshape(512, 512), tab["fx"][:, 256:512])
        for j in range(2):
            tiles = []
            for z in range(8):
                tile = spread[z * 64 : z * 64 + 64, j * 128 : j * 128 + 128]
                tiles.append(pltpu.roll(tile, 16 * z, 1) if z else tile)
            tiles = merge(tiles, place)
            for to in range(8):
                su[c, 8 * j + to] = tiles[-to % 8].astype(BF)
        send_u(su, ru, 2 * t, t, c)

    def x_inverse(t, c):
        def gather(j):
            if j < 2:
                tiles = [rai[t, c, source, j].astype(F32) for source in range(8)]
            else:
                tiles = [rui[t, c, 8 * (j - 2) + source].astype(F32) for source in range(8)]
            tiles = merge(tiles, place)
            for z in range(8):
                tile = tiles[-z % 8]
                tile = pltpu.roll(tile, 128 - 16 * z, 1) if z else tile
                lines[z * 64 : z * 64 + 64, j * 128 : j * 128 + 128] = tile.astype(BF)

        arrived(rai.at[t, c], a_recv.at[2 * t + 1, c])
        gather(0)
        gather(1)
        summed[...] = dot(lines[:, 0:256], tab["bx"][0:256, :])
        arrived(rui.at[t, c], u_recv.at[2 * t + 1, c])
        gather(2)
        gather(3)
        values = (summed[...] + dot(lines[:, 256:512], tab["bx"][256:512, :])).astype(BF).reshape(8, 64, 512)
        if t == 0:
            values = (values.astype(F32) * mask[...].astype(F32)).astype(BF)
        field[c] = values

    def y_forward(t, i):
        arrived(ra.at[t, i], a_recv.at[2 * t, i])
        sides = [ra[t, i, :, side].reshape(512, 128) for side in range(2)]
        sb[i] = dot(tab["ty"][...], jnp.concatenate(sides, axis=1)).astype(BF)
        send_b(sb, rb, 2 * t, t, i)

    def y_inverse(t, i):
        arrived(rbi.at[t, i], b_recv.at[2 * t + 1, i])
        out = dot(tab["tyi"][...], rbi[t, i]).astype(BF)
        for side in range(2):
            sai[i, :, side] = out[:, side * 128 : side * 128 + 128].reshape(2, 256, 128)
        send_ai(t, i)

    def z_forward(t, i):
        arrived(rb.at[t, i], b_recv.at[2 * t, i])
        for half in range(2):
            lanes = slice(half * 128, half * 128 + 128)

            def source(e_from, ri):
                return rb[t, i, e_from * 32 + ri * 16 : e_from * 32 + ri * 16 + 16, lanes].astype(F32)

            for low in range(4):
                out = radix4([(source(low + 4 * j, 0), source(low + 4 * j, 1)) for j in range(4)], 1)
                for k, value in enumerate(out):
                    mid[low, k, 0, :, lanes], mid[low, k, 1, :, lanes] = turned_by(value, low * k, 1)
            for k in range(4):
                out = radix4([(mid[low, k, 0, :, lanes], mid[low, k, 1, :, lanes]) for low in range(4)], 1)
                for high, (re, im) in enumerate(out):
                    k1 = k + 4 * high
                    wc, ws = tab["tw"][0, k1 : k1 + 1, lanes], tab["tw"][1, k1 : k1 + 1, lanes]
                    big[k1 * 16 : k1 * 16 + 16, lanes] = (re * wc + im * ws).astype(BF)
                    big[256 + k1 * 16 : 256 + k1 * 16 + 16, lanes] = (im * wc - re * ws).astype(BF)
        both = dot(big[...], tab["cs"][...])
        spec[i, 0] = both[:256, :256] + both[256:, 256:]
        spec[i, 1] = both[256:, :256] - both[:256, 256:]

    def z_inverse(source, t, i):
        both = dot(source[i].reshape(512, 256), tab["csi"][...])
        for half in range(2):
            lanes = slice(half * 128, half * 128 + 128)
            other = slice(256 + half * 128, 256 + half * 128 + 128)

            def value(k1):
                upper, lower = slice(k1 * 16, k1 * 16 + 16), slice(256 + k1 * 16, 256 + k1 * 16 + 16)
                re = both[upper, lanes] - both[lower, other]
                im = both[lower, lanes] + both[upper, other]
                wc, ws = tab["tw"][0, k1 : k1 + 1, lanes], tab["tw"][1, k1 : k1 + 1, lanes]
                return re * wc - im * ws, im * wc + re * ws

            for low in range(4):
                out = radix4([value(low + 4 * j) for j in range(4)], -1)
                for k, turned in enumerate(out):
                    mid[low, k, 0, :, lanes], mid[low, k, 1, :, lanes] = turned_by(turned, low * k, -1)
            for k in range(4):
                out = radix4([(mid[low, k, 0, :, lanes], mid[low, k, 1, :, lanes]) for low in range(4)], -1)
                for high, (re, im) in enumerate(out):
                    to = (k + 4 * high) * 32
                    sbi[i, to : to + 16, lanes] = re.astype(BF)
                    sbi[i, to + 16 : to + 32, lanes] = im.astype(BF)
        send_b(sbi, rbi, 2 * t + 1, t, i)

    def v_forward(t, c):
        arrived(ru.at[t, c], u_recv.at[2 * t, c])

        def some(n, carry):
            rows = pl.ds(pl.multiple_of(n * 16, 16), 16)
            out = packed_dft16([ru[t, c, j, rows].astype(F32) for j in range(16)], 1)
            for k1, value in enumerate(out):
                wc, ws = tab["utw"][0, k1 : k1 + 1], tab["utw"][1, k1 : k1 + 1]
                sv[c, k1, rows] = (value * wc + times_minus_i(value) * ws).astype(BF)
            return carry

        lax.fori_loop(0, 4, some, 0)
        send_v(t, c)

    def v_inverse(t, c):
        arrived(rvi.at[t, c], v_recv.at[2 * t + 1, c])

        def some(n, carry):
            rows = pl.ds(pl.multiple_of(n * 16, 16), 16)
            values = []
            for k1 in range(16):
                value = rvi[t, c, k1, rows].astype(F32)
                wc, ws = tab["utw"][0, k1 : k1 + 1], tab["utw"][1, k1 : k1 + 1]
                values.append(value * wc - times_minus_i(value) * ws)
            for j, value in enumerate(packed_dft16(values, -1)):
                sui[c, j, rows] = value.astype(BF)
            return carry

        lax.fori_loop(0, 4, some, 0)
        send_u(sui, rui, 2 * t + 1, t, c)

    def y_product(table, values, wide):
        for half in range(2):
            lanes = slice(half * 128, half * 128 + 128)
            stacked[256:512, lanes] = times_minus_i(wide[:, lanes]).astype(BF)
        stacked[0:256, :] = values
        return dot(table, stacked[...]).astype(BF)

    def w_forward(t, c):
        arrived(rv.at[t, c], v_recv.at[2 * t, c])
        for k1 in range(2):
            values = jnp.concatenate([rv[t, c, k1, 0], rv[t, c, k1, 1]], axis=1)
            big1[k1 * 256 : k1 * 256 + 256, :] = y_product(tab["uy"][...], values, values.astype(F32))
        spec1[c] = dot(big1[...], tab["uz"][...])

    def w_inverse(source, t, c):
        wide = dot(source[c], tab["uzi"][...])
        for k1 in range(2):
            part = wide[k1 * 256 : k1 * 256 + 256]
            out = y_product(tab["uyi"][...], part.astype(BF), part)
            for side in range(2):
                svi[c, k1, side] = out[:, side * 128 : side * 128 + 128]
        send_vi(t, c)

    lane = lax.broadcasted_iota(jnp.int32, (16, 256), 1)
    unit_long, unit = np.float32(TWO_PI / 512), np.float32(TWO_PI / 256)
    index_y = e * 16 + lax.broadcasted_iota(jnp.int32, (16, 256), 0)
    wave_y = jnp.where(index_y < 128, index_y, index_y - 256).astype(F32) * unit

    wave_x = (d * 32 + (lane & 15)).astype(F32) * unit_long
    wave_x1 = ((e // 2) * 32 + 16 + (e & 1) * 8 + (lane & 7)).astype(F32) * unit_long

    def along_z(k1):
        index_z = k1 + 16 * (lane // 16)
        return index_z, jnp.where(index_z < 128, index_z, index_z - 256).astype(F32) * unit

    def at_rows(n):
        return pl.ds(pl.multiple_of(n * 16, 16), 16)

    def along_y1(n):
        index = (n & 15) * 16 + lax.broadcasted_iota(jnp.int32, (16, 256), 0)
        return index, jnp.where(index < 128, index, index - 256).astype(F32) * unit

    def scales(kx, ky, kz, edge):
        ksq = kx * kx + ky * ky + kz * kz
        return (
            jnp.where(edge, 0.0, 1.0 / (0.05 * ksq + 0.5)),
            jnp.where(ksq > 0.0, 1.0 / jnp.where(ksq > 0.0, ksq, 1.0), 0.0),
        )

    def factors(n, carry):
        index_z, wave_z = along_z(n)
        gain[at_rows(n)], inv[at_rows(n)] = scales(wave_x, wave_y, wave_z, (index_y == 128) | (index_z == 128))
        return carry

    def factors1(n, carry):
        index_z, wave_z = along_z(2 * d + n // 16)
        index, wave = along_y1(n)
        gain1[at_rows(n)], inv1[at_rows(n)] = scales(wave_x1, wave, wave_z, (index == 128) | (index_z == 128))
        return carry

    def parts():
        def one(n, carry):
            rows = at_rows(n)
            for ri in range(2):
                dots[ri, rows] = wave_x * spec[0, ri, rows] + wave_y * spec[1, ri, rows]
            return carry

        lax.fori_loop(0, 16, one, 0)

    def keep(t, kept, result, at, value):
        if t == 0:
            kept[at] = value.astype(BF)
        else:
            result[at] = (kept[at].astype(F32) - value).astype(BF)

    def project_x(t):
        def one(n, carry):
            rows = at_rows(n)
            wave_z = along_z(n)[1]
            for ri in range(2):
                along = (dots[ri, rows] + wave_z * spec[2, ri, rows]) * inv[rows]
                dots[ri, rows] = along
                keep(t, first, second, (0, ri, rows), gain[rows] * (spec[0, ri, rows] - wave_x * along))
            return carry

        lax.fori_loop(0, 16, one, 0)

    def project_yz(t):
        def one(n, carry):
            rows = at_rows(n)
            waves = (wave_x, wave_y, along_z(n)[1])
            for ri in range(2):
                along = dots[ri, rows]
                for c in (1, 2):
                    keep(t, first, second, (c, ri, rows), gain[rows] * (spec[c, ri, rows] - waves[c] * along))
            return carry

        lax.fori_loop(0, 16, one, 0)

    def parts1():
        def one(n, carry):
            rows = at_rows(n)
            dots1[rows] = wave_x1 * spec1[0, rows] + along_y1(n)[1] * spec1[1, rows]
            return carry

        lax.fori_loop(0, 32, one, 0)

    def project1_x(t):
        def one(n, carry):
            rows = at_rows(n)
            along = (dots1[rows] + along_z(2 * d + n // 16)[1] * spec1[2, rows]) * inv1[rows]
            dots1[rows] = along
            keep(t, first1, second1, (0, rows), gain1[rows] * (spec1[0, rows] - wave_x1 * along))
            return carry

        lax.fori_loop(0, 32, one, 0)

    def project1_yz(t):
        def one(n, carry):
            rows = at_rows(n)
            waves = (wave_x1, along_y1(n)[1], along_z(2 * d + n // 16)[1])
            along = dots1[rows]
            for c in (1, 2):
                keep(t, first1, second1, (c, rows), gain1[rows] * (spec1[c, rows] - waves[c] * along))
            return carry

        lax.fori_loop(0, 32, one, 0)

    def each(count, step):
        def body(i, _):
            step(i)
            return _

        lax.fori_loop(0, count, body, 0)

    def spectral(t, source, source1):
        def out(c):
            y_forward(t, c)
            v_forward(t, c)

        def inner(c):
            w_forward(t, c)
            z_forward(t, c)

        def outer(c):
            w_inverse(source1, t, c + 1)
            z_inverse(source, t, c + 1)

        def back(c):
            v_inverse(t, c)
            y_inverse(t, c)

        each(3, out)
        each(2, inner)
        parts1()
        parts()
        w_forward(t, 2)
        project1_x(t)
        w_inverse(source1, t, 0)
        z_forward(t, 2)
        project_x(t)
        z_inverse(source, t, 0)
        project1_yz(t)
        project_yz(t)
        each(2, outer)
        each(3, back)

    def start(c):
        @pl.when(c > 0)
        def _():
            arrived(field.at[c], in_sem.at[c])

        x_forward(0, c)
        x_forward1(0, c)

    loads["fx"].wait()
    loads[0].wait()
    load_rest()
    each(3, start)
    lax.fori_loop(0, 16, factors, 0)
    lax.fori_loop(0, 32, factors1, 0)
    loads["scalar"].wait()
    for z in range(8):
        state[0, z + 1, pl.ds(8, 64), :] = scalar[z].astype(F32)
    zsend[0, 0] = scalar[0]
    zsend[0, 1] = scalar[7]
    for side in (far, near):
        for q in range(4):
            send_z(0, side, q)
    for side in range(2):
        for z in range(8):
            edge[pl.ds(z, 1), :] = state[0, z + 1, pl.ds(8 + 63 * side, 1), :]
        pack_edge(0, side)
        send_y(0, side)
    for name in TABLES[1:]:
        loads[name].wait()
    loads["mask"].wait()
    spectral(0, first, first1)

    def sent(t, c):
        for k in (2 * t, 2 * t + 1):
            sent_a(k, c)
            sent_b(k, c)
            sent_u(k, c)
            sent_v(k, c)

    def middle(c):
        x_inverse(0, c)
        sent(0, c)
        x_forward(1, c)
        x_forward1(1, c)

    each(3, middle)
    spectral(1, second, second1)

    def coefficients(z, c):
        fluid = 0.25 * (1.0 - mask[z].astype(F32))
        u = field[c, z].astype(F32)
        below = fluid * (0.25 + jnp.maximum(u, 0.0))
        above = fluid * (0.25 - jnp.minimum(u, 0.0))
        coef[2 * c, z] = below
        coef[2 * c + 1, z] = above
        start = jnp.where(c == 0, jnp.ones_like(u), coef[6, z])
        coef[6, z] = start - (below + above)
        return c

    def last(c):
        x_inverse(1, c)
        pltpu.make_async_copy(field.at[c], velocity_h.at[c], out_sem.at[c]).start()

        @pl.when(c < 2)
        def _():
            lax.fori_loop(0, 8, coefficients, c)

    each(3, last)

    def block(s, z, q):
        now, later = s & 1, (s + 1) & 1
        at = 8 + 16 * q
        rows, cells = pl.ds(at, 16), pl.ds(16 * q, 16)
        center = state[now, z, rows]
        new = coef[6, z - 1, cells] * center
        new = new + coef[0, z - 1, cells] * pltpu.roll(center, 1, 1)
        new = new + coef[1, z - 1, cells] * pltpu.roll(center, 511, 1)
        new = new + coef[2, z - 1, cells] * state[now, z, pl.ds(at - 1, 16)]
        new = new + coef[3, z - 1, cells] * state[now, z, pl.ds(at + 1, 16)]
        new = new + coef[4, z - 1, cells] * state[now, z - 1, rows]
        new = new + coef[5, z - 1, cells] * state[now, z + 1, rows]
        state[later, z, rows] = new
        return new

    def outer_block(s, side, q):
        cells = pl.ds(16 * q, 16)
        arrived(zrecv.at[s, side, cells], z_rsem.at[s, side, q])
        state[s & 1, 9 * side, pl.ds(8 + 16 * q, 16)] = zrecv[s, side, cells].astype(F32)
        face = block(s, 1 + 7 * side, q)

        @pl.when(s < SECTIONS - 1)
        def _():
            zsend[s + 1, side, cells] = face.astype(BF)
            send_z(s + 1, side, q)

    def y_halo(s):
        for side in range(2):
            arrived(yrecv.at[s, side], y_rsem.at[s, side])
            halo = yrecv[s, side].astype(F32)
            for z in range(8):
                for half in range(2):
                    lanes = slice(half * 256, half * 256 + 256)
                    state[s & 1, z + 1, pl.ds(7 + 65 * side, 1), lanes] = halo[8 * half + z : 8 * half + z + 1]

    def store_planes(z, count):
        planes = pl.ds(z, count)
        return pltpu.make_async_copy(conc.at[planes], conc_h.at[planes], out_sem.at[3 + (0, 1, 0, 0, 0, 0, 0, 2)[z]])

    def section(s, carry):
        @pl.when(s == SECTIONS - 1)
        def _():
            y_halo(s)

        for q in (0, 3, 1, 2):
            outer_block(s, near, q)
            for z in range(2, 8):
                block(s, z, q)
            if q in (0, 3):
                side = q // 3

                @pl.when(s < SECTIONS - 1)
                def _():
                    for z in range(8):
                        edge[pl.ds(z, 1), :] = state[(s + 1) & 1, z + 1, pl.ds(8 + 63 * side, 1), :]
                    pack_edge(s + 1, side)
                    send_y(s + 1, side)

        @pl.when(s == SECTIONS - 1)
        def _():
            conc[pl.ds(1, 6)] = state[SECTIONS % 2, pl.ds(2, 6), pl.ds(8, 64), :].astype(BF)
            store_planes(1, 6).start()

        following = jnp.minimum(s + 1, SECTIONS - 1)

        @pl.when(s != SECTIONS - 2)
        def _():
            for q in (1, 2):
                outer_block(following, far, q)

        @pl.when(s < SECTIONS - 2)
        def _():
            y_halo(s + 1)

        @pl.when(s != SECTIONS - 2)
        def _():
            for q in (0, 3):
                outer_block(following, far, q)

        return carry

    y_halo(0)
    coefficients(7 * far, 2)
    for q in (1, 2, 0, 3):
        outer_block(0, far, q)
    lax.fori_loop(0, 7, lambda n, carry: coefficients(n + near, carry), 2)
    lax.fori_loop(0, SECTIONS, section, 0)
    for z in (0, 7):
        conc[z] = state[SECTIONS % 2, z + 1, pl.ds(8, 64), :].astype(BF)
        store_planes(z, 1).start()

    each(3, lambda c: sent(1, c))
    for s in range(SECTIONS):
        for i in range(2):
            arrived(zsend.at[s, i], z_ssem.at[s, i])
            arrived(ysend.at[s, i], y_ssem.at[s, i])
    for c in range(3):
        pltpu.make_async_copy(field.at[c], velocity_h.at[c], out_sem.at[c]).wait()
    for z, count in ((0, 1), (1, 6), (7, 1)):
        store_planes(z, count).wait()


def place_kernel(velocity_in, conc_in, velocity, conc, held, in_sem, out_sem):
    pairs = []
    for half in range(2):
        planes = pl.ds(4 * half, 4)
        pairs += [(velocity_in.at[c, planes], held.at[c, planes], velocity.at[c, planes]) for c in range(3)]
        pairs.append((conc_in.at[planes], held.at[3, planes], conc.at[planes]))
    loads = [pltpu.make_async_copy(a, b, in_sem.at[i]) for i, (a, b, _) in enumerate(pairs)]
    stores = [pltpu.make_async_copy(b, c, out_sem.at[i]) for i, (_, b, c) in enumerate(pairs)]
    for copy in loads:
        copy.start()
    for load, store in zip(loads, stores):
        load.wait()
        store.start()
    for copy in stores:
        copy.wait()


def local(force, mask, scalar):
    tables = numpy_tables()
    vm = pltpu.VMEM
    dma = pltpu.SemaphoreType.DMA
    scratch = [vm((3, 8, 64, 512), BF), vm((8, 64, 512), jnp.int32), vm((8, 64, 512), BF)]
    for name in TABLES:
        value = tables[name]
        shape = value.shape[1:] if name in VARIED else value.shape
        scratch.append(vm(shape, value.dtype))
    scratch += [
        vm((256, 256), F32), vm((256, 256), F32),
        vm((3, 8, 2, 64, 128), BF), vm((2, 3, 2, 2, 256, 128), BF),
        vm((3, 512, 256), BF), vm((2, 3, 512, 256), BF),
        vm((3, 512, 256), BF), vm((2, 3, 512, 256), BF),
        vm((3, 2, 2, 256, 128), BF), vm((2, 3, 8, 2, 64, 128), BF),
        vm((3, 2, 256, 256), F32), vm((3, 2, 256, 256), BF), vm((3, 2, 256, 256), BF),
        vm((512, 512), BF), vm((512, 256), BF), vm((4, 4, 2, 16, 256), F32),
        vm((512, 256), F32), vm((512, 256), F32),
        vm((3, 16, 64, 128), BF), vm((2, 3, 16, 64, 128), BF),
        vm((3, 16, 64, 128), BF), vm((2, 3, 2, 2, 256, 128), BF),
        vm((3, 2, 2, 256, 128), BF), vm((2, 3, 16, 64, 128), BF),
        vm((3, 16, 64, 128), BF), vm((2, 3, 16, 64, 128), BF),
        vm((3, 512, 256), F32), vm((3, 512, 256), BF), vm((3, 512, 256), BF),
        vm((512, 256), BF), vm((2, 256, 256), F32), vm((512, 256), F32),
        vm((512, 512), F32), vm((512, 256), BF),
        dma((4, 3)), dma((4, 3)), dma((4, 3)), dma((4, 3)),
        vm((SECTIONS, 2, 64, 512), BF), vm((SECTIONS, 2, 64, 512), BF),
        vm((SECTIONS, 2, 16, 256), BF), vm((SECTIONS, 2, 16, 256), BF), vm((8, 512), F32),
        vm((7, 8, 64, 512), F32), vm((2, 10, 80, 512), F32), vm((8, 64, 512), BF),
        dma((5,)), dma((len(TABLES),)),
        dma((4, 3)), dma((4, 3)), dma((4, 3)), dma((4, 3)),
        dma((SECTIONS, 2)), dma((SECTIONS, 2, 4)), dma((SECTIONS, 2)), dma((SECTIONS, 2)),
        dma((6,)),
    ]
    any_spec = pl.BlockSpec(memory_space=pl.ANY)
    velocity, conc = pl.pallas_call(
        mixer_kernel,
        out_shape=(
            jax.ShapeDtypeStruct((3, 8, 64, 512), BF),
            jax.ShapeDtypeStruct((8, 64, 512), BF),
        ),
        in_specs=[any_spec] * (3 + len(TABLES)),
        out_specs=(any_spec, any_spec),
        scratch_shapes=scratch,
        compiler_params=pltpu.CompilerParams(
            collective_id=0, has_side_effects=True, vmem_limit_bytes=62 * 1024 * 1024
        ),
        name="mixer",
    )(
        force,
        mask,
        scalar,
        *[jnp.asarray(tables[name]) for name in TABLES],
    )
    return pl.pallas_call(
        place_kernel,
        out_shape=(
            jax.ShapeDtypeStruct((3, 8, 64, 512), BF),
            jax.ShapeDtypeStruct((8, 64, 512), BF),
        ),
        in_specs=[any_spec] * 2,
        out_specs=(any_spec, any_spec),
        scratch_shapes=[vm((4, 8, 64, 512), BF), dma((8,)), dma((8,))],
        name="place",
    )(velocity, conc)


def solution(mesh):
    placed = (P(None, "col", "row", None), P("col", "row", None), P("col", "row", None))
    return jax.shard_map(
        local,
        mesh=mesh,
        in_specs=placed,
        out_specs=(P(None, "col", "row", None), P("col", "row", None)),
        check_vma=False,
    )
```

```python
import numpy as np
import jax
import jax.numpy as jnp
import ml_dtypes
from jax import lax
from jax.experimental import pallas as pl
from jax.experimental.pallas import tpu as pltpu
from jax.sharding import PartitionSpec as P

SECTIONS = 5
MESH = pl.DeviceIdType.MESH
BF = jnp.bfloat16
F32 = jnp.float32
TWO_PI = 2.0 * np.pi
PLANE_ORDER = (
    (2, 2), (2, 1), (1, 2), (2, 3), (3, 2), (2, 0), (0, 2), (1, 1), (3, 3), (1, 3), (3, 1),
    (1, 0), (3, 0), (0, 1), (0, 3),
)


def numpy_tables():
    def half(values):
        return values.astype(np.float32).astype(ml_dtypes.bfloat16)

    x = np.arange(512)
    ri, d, k = (v.reshape(-1) for v in np.meshgrid(np.arange(2), np.arange(8), np.arange(16), indexing="ij"))
    e1, ri1, k1 = (v.reshape(-1) for v in np.meshgrid(np.arange(16), np.arange(2), np.arange(8), indexing="ij"))
    m = np.concatenate([d * 32 + k, (e1 // 2) * 32 + 16 + (e1 % 2) * 8 + k1])
    ri = np.concatenate([ri, ri1])
    angle = (np.outer(x, m) % 512) * (TWO_PI / 512)
    fx = np.where(ri == 0, np.cos(angle), -np.sin(angle)) / np.sqrt(512.0)
    bx = (fx * np.where(m == 0, 1.0, 2.0)).T
    y = np.arange(256)
    angle = (np.outer(y, y) % 256) * (TWO_PI / 256)
    c, s = np.cos(angle) / 16.0, np.sin(angle) / 16.0
    real = np.concatenate([c, s], 1).reshape(16, 1, 16, 512)
    imag = np.concatenate([-s, c], 1).reshape(16, 1, 16, 512)
    ty = np.concatenate([real, imag], 1).reshape(512, 512)
    uy = np.concatenate([c, s], 1)
    uyi = np.concatenate([c, -s], 1)
    n = np.arange(16)
    angle = (np.outer(n, n) % 16) * (TWO_PI / 16)
    c, s = np.cos(angle) / 4.0, np.sin(angle) / 4.0
    cs = np.zeros((8, 256, 512))
    csi = np.zeros((8, 256, 512))
    tw = np.zeros((8, 2, 16, 256))
    k = np.arange(16)
    for d in range(8):
        for low in range(2):
            for p in range(8):
                zp = low * 8 + (p - d) % 8
                at = low * 128 + p * 16
                for k2 in range(16):
                    cs[d, at + k, k2 * 16 + k] = c[zp, k2]
                    cs[d, at + k, 256 + k2 * 16 + k] = s[zp, k2]
                    csi[d, k2 * 16 + k, at + k] = c[zp, k2]
                    csi[d, k2 * 16 + k, 256 + at + k] = s[zp, k2]
                tw[d, 0, :, at : at + 16] = np.cos(TWO_PI * zp * n / 256)[:, None] / 4.0
                tw[d, 1, :, at : at + 16] = np.sin(TWO_PI * zp * n / 256)[:, None] / 4.0
    utw = np.zeros((16, 2, 16, 128))
    uz = np.zeros((8, 256, 256))
    k = np.arange(8)
    for turn in range(8):
        for low in range(2):
            for p in range(8):
                zp = low * 8 + (p - turn) % 8
                utw[low * 8 + turn, 0, :, p * 16 : p * 16 + 16] = np.cos(TWO_PI * zp * n / 256)[:, None] / 4.0
                utw[low * 8 + turn, 1, :, p * 16 : p * 16 + 16] = np.sin(TWO_PI * zp * n / 256)[:, None] / 4.0
                at = low * 128 + p * 16
                for k2 in range(16):
                    to = k2 * 16
                    uz[turn, at + k, to + k] = c[zp, k2]
                    uz[turn, at + 8 + k, to + k] = s[zp, k2]
                    uz[turn, at + k, to + 8 + k] = -s[zp, k2]
                    uz[turn, at + 8 + k, to + 8 + k] = c[zp, k2]
    return dict(
        uy=half(uy), uyi=half(uyi), uz=half(uz), uzi=half(uz.transpose(0, 2, 1)), utw=utw.astype(np.float32),
        fx=half(fx), bx=half(bx), ty=half(ty), tyi=half(ty.T), cs=half(cs), csi=half(csi),
        tw=tw.astype(np.float32),
    )


TABLES = ("fx", "ty", "utw", "tw", "cs", "uy", "uz", "csi", "uzi", "tyi", "uyi", "bx")
BY_D = ("cs", "tw", "csi")
BY_E = ("uz", "uzi")
VARIED = BY_D + BY_E + ("utw",)


def radix4(a, sign):
    def add(u, v):
        return u[0] + v[0], u[1] + v[1]

    def sub(u, v):
        return u[0] - v[0], u[1] - v[1]

    t0, t1 = add(a[0], a[2]), sub(a[0], a[2])
    t2, t3 = add(a[1], a[3]), sub(a[1], a[3])
    t3 = (t3[1], -t3[0]) if sign > 0 else (-t3[1], t3[0])
    return add(t0, t2), add(t1, t3), sub(t0, t2), sub(t1, t3)


def turned_by(value, j, sign):
    if j == 0:
        return value
    c, s = float(np.cos(TWO_PI * j / 16)), float(np.sin(TWO_PI * j / 16)) * sign
    re, im = value
    return re * c + im * s, im * c - re * s


def times_minus_i(value):
    imag = (lax.broadcasted_iota(jnp.int32, value.shape, 1) & 8) != 0
    return jnp.where(imag, -pltpu.roll(value, 8, 1), pltpu.roll(value, 120, 1))


def packed_radix4(a, sign):
    t0, t1, t2 = a[0] + a[2], a[0] - a[2], a[1] + a[3]
    t3 = times_minus_i(a[1] - a[3])
    if sign < 0:
        t3 = -t3
    return t0 + t2, t1 + t3, t0 - t2, t1 - t3


def packed_turned(value, j, sign):
    if j == 0:
        return value
    c, s = float(np.cos(TWO_PI * j / 16)), float(np.sin(TWO_PI * j / 16)) * sign
    return value * c + times_minus_i(value) * s


def packed_dft16(values, sign):
    parts = [packed_radix4(values[low::4], sign) for low in range(4)]
    parts = [[packed_turned(v, low * k, sign) for k, v in enumerate(parts[low])] for low in range(4)]
    out = [None] * 16
    for k in range(4):
        out[k::4] = packed_radix4([parts[low][k] for low in range(4)], sign)
    return out


def merge(tiles, place):
    for bit in (1, 2, 4):
        take = (place & bit) != 0
        tiles = [jnp.where(take, tiles[(m + bit) % 8], tiles[m]) for m in range(8)]
    return tiles


def dot(a, b):
    return jnp.dot(a, b, preferred_element_type=F32)


def mixer_kernel(*refs):
    force_h, mask_h, scalar_h = refs[:3]
    count = len(TABLES)
    tables_h = dict(zip(TABLES, refs[3 : 3 + count]))
    velocity_h, conc_h = refs[3 + count : 5 + count]
    (field, mask, scalar, *rest) = refs[5 + count :]
    tab = dict(zip(TABLES, rest[:count]))
    (gain, inv, sa, ra, sb, rb, sbi, rbi, sai, rai, spec, first, second, lines, big, mid,
     gain1, inv1, su, ru, sv, rv, svi, rvi, sui, rui, spec1, first1, second1, stacked, dots, dots1, summed, big1,
     u_send, u_recv, v_send, v_recv,
     zsend, zrecv, ysend, yrecv, edge, coef, state, conc,
     in_sem, tab_sem, a_send, a_recv, b_send, b_recv, z_ssem, z_rsem, y_ssem, y_rsem, out_sem) = rest[count:]

    r = lax.axis_index("row")
    col = lax.axis_index("col")
    e = col // 2
    xl = col % 2
    d = xl * 4 + r

    def load(source, target, sem):
        copy = pltpu.make_async_copy(source, target, sem)
        copy.start()
        return copy

    def load_table(name):
        source = tables_h[name]
        sem = tab_sem.at[TABLES.index(name)]
        if name in VARIED:
            source = source.at[d if name in BY_D else (e & 7) + (8 * xl if name == "utw" else 0)]
        return load(source, tab[name], sem)

    for i in range(4):
        planes, rows = pl.ds(2 * i, 2), pl.ds(128 * i, 128)
        load(force_h.at[0, planes], field.at[0, planes], in_sem.at[0])
        load(tables_h["fx"].at[rows], tab["fx"].at[rows], tab_sem.at[0])
    loads = {}

    def load_rest():
        for i in (1, 2):
            loads[i] = load(force_h.at[i], field.at[i], in_sem.at[i])
        for name in TABLES[1:]:
            loads[name] = load_table(name)
        loads["scalar"] = load(scalar_h, scalar, in_sem.at[4])
        loads["mask"] = load(mask_h, mask, in_sem.at[3])

    core = r & 1
    x = (r // 2) * 2 + xl
    y_at, z_at = e // 4, e & 3

    def x_peer(step, of_core):
        at = (x + step * (1 + 2 * core)) & 3
        low = at & 1
        row = (at - low) + of_core
        return low * 4 + row, (row, e * 2 + low)

    def plane_peer(dy, dz):
        to = ((y_at + dy + core * (3 * dz - dy)) & 3) * 4 + ((z_at + dz + core * (3 * dy - dz)) & 3)
        return to, (r, to * 2 + xl)

    x_peers = [
        x_peer(step, core if same else 1 - core)
        for step, same in ((2, 1), (2, 0), (1, 1), (3, 1), (1, 0), (3, 0), (0, 0))
    ]
    plane_peers = [plane_peer(dy, dz) for dy, dz in PLANE_ORDER]

    y_up = (lax.rem(r + 1, 4), col)
    y_down = (lax.rem(r + 3, 4), col)

    barrier = pltpu.get_barrier_semaphore()

    for _, device in x_peers + plane_peers:
        pl.semaphore_signal(barrier, inc=1, device_id=device, device_id_type=MESH)
    across = (r, lax.rem(col + 31 + 2 * xl, 32))
    pl.semaphore_signal(barrier, inc=1, device_id=across, device_id_type=MESH)
    pl.semaphore_wait(barrier, 23)

    def remote(source, target, ssem, rsem, device):
        return pltpu.make_async_remote_copy(
            src_ref=source, dst_ref=target, send_sem=ssem, recv_sem=rsem,
            device_id=device, device_id_type=MESH)

    my_rows = pl.ds(pl.multiple_of(r * 64, 64), 64)
    my_slab = pl.ds(pl.multiple_of(e * 32, 32), 32)

    def send_a(t, i):
        target = ra.at[t, i, :, xl, my_rows]
        recv = a_recv.at[2 * t, i]

        for to, device in x_peers:
            remote(sa.at[i, to], target, a_send.at[2 * t, i], recv, device).start()
        pltpu.make_async_copy(sa.at[i, d], target, recv).start()

    def send_ai(t, i):
        target = rai.at[t, i, d]
        recv = a_recv.at[2 * t + 1, i]

        def piece(to):
            rows = pl.ds(pl.multiple_of((to & 3) * 64, 64), 64)
            return sai.at[i, :, to // 4, rows]

        for to, device in x_peers:
            remote(piece(to), target, a_send.at[2 * t + 1, i], recv, device).start()
        pltpu.make_async_copy(piece(d), target, recv).start()

    def send_b(source, into, k, t, i):
        target = into.at[t, i, my_slab]
        recv = b_recv.at[k, i]

        for to, device in plane_peers:
            slab = source.at[i, pl.ds(pl.multiple_of(to * 32, 32), 32)]
            remote(slab, target, b_send.at[k, i], recv, device).start()
        pltpu.make_async_copy(source.at[i, my_slab], target, recv).start()

    def send_u(source, into, k, t, c):
        target = into.at[t, c, e]
        recv = u_recv.at[k, c]
        for to, device in plane_peers:
            remote(source.at[c, to], target, u_send.at[k, c], recv, device).start()
        pltpu.make_async_copy(source.at[c, e], target, recv).start()

    def send_v(t, c):
        target = rv.at[t, c, :, xl, my_rows]
        recv = v_recv.at[2 * t, c]
        for to, device in x_peers:
            remote(sv.at[c, pl.ds(2 * to, 2)], target, v_send.at[2 * t, c], recv, device).start()
        pltpu.make_async_copy(sv.at[c, pl.ds(2 * d, 2)], target, recv).start()

    def send_vi(t, c):
        target = rvi.at[t, c, pl.ds(2 * d, 2)]
        recv = v_recv.at[2 * t + 1, c]

        def piece(to):
            rows = pl.ds(pl.multiple_of((to & 3) * 64, 64), 64)
            return svi.at[c, :, to // 4, rows]

        for to, device in x_peers:
            remote(piece(to), target, v_send.at[2 * t + 1, c], recv, device).start()
        pltpu.make_async_copy(piece(d), target, recv).start()

    def arrived(buffer, sem):
        pltpu.make_async_copy(buffer, buffer, sem).wait()

    def sent_a(k, i):
        arrived(sa.at[i, pl.ds(0, 7)], a_send.at[k, i])

    def sent_b(k, i):
        arrived(sb.at[i, pl.ds(0, 480)], b_send.at[k, i])

    def sent_u(k, i):
        arrived(su.at[i, pl.ds(0, 15)], u_send.at[k, i])

    def sent_v(k, i):
        arrived(sv.at[i, pl.ds(0, 14)], v_send.at[k, i])

    near, far = 1 - xl, xl

    def send_z(s, side, q):
        rows = pl.ds(16 * q, 16)
        remote(zsend.at[s, side, rows], zrecv.at[s, 1 - side, rows], z_ssem.at[s, side],
               z_rsem.at[s, 1 - side, q], (r, (col + 2 * side + 31) & 31)).start()

    def pack_edge(s, side):
        value = edge[...]
        ysend[s, side] = jnp.concatenate([value[:, 0:256], value[:, 256:512]], axis=0).astype(BF)

    def send_y(s, side):
        remote(ysend.at[s, side], yrecv.at[s, 1 - side], y_ssem.at[s, side], y_rsem.at[s, 1 - side],
               (y_down, y_up)[side]).start()

    place = lax.broadcasted_iota(jnp.int32, (64, 128), 1) // 16

    def x_forward(t, c):
        spread = dot(field[c].reshape(512, 512), tab["fx"][:, 0:256])
        for ri in range(2):
            tiles = []
            for z in range(8):
                tile = spread[z * 64 : z * 64 + 64, ri * 128 : ri * 128 + 128]
                tiles.append(pltpu.roll(tile, 16 * z, 1) if z else tile)
            tiles = merge(tiles, place)
            for to in range(8):
                sa[c, to, ri] = tiles[-to % 8].astype(BF)
        send_a(t, c)

    def x_forward1(t, c):
        spread = dot(field[c].reshape(512, 512), tab["fx"][:, 256:512])
        for j in range(2):
            tiles = []
            for z in range(8):
                tile = spread[z * 64 : z * 64 + 64, j * 128 : j * 128 + 128]
                tiles.append(pltpu.roll(tile, 16 * z, 1) if z else tile)
            tiles = merge(tiles, place)
            for to in range(8):
                su[c, 8 * j + to] = tiles[-to % 8].astype(BF)
        send_u(su, ru, 2 * t, t, c)

    def x_inverse(t, c):
        def gather(j):
            if j < 2:
                tiles = [rai[t, c, source, j].astype(F32) for source in range(8)]
            else:
                tiles = [rui[t, c, 8 * (j - 2) + source].astype(F32) for source in range(8)]
            tiles = merge(tiles, place)
            for z in range(8):
                tile = tiles[-z % 8]
                tile = pltpu.roll(tile, 128 - 16 * z, 1) if z else tile
                lines[z * 64 : z * 64 + 64, j * 128 : j * 128 + 128] = tile.astype(BF)

        arrived(rai.at[t, c], a_recv.at[2 * t + 1, c])
        gather(0)
        gather(1)
        summed[...] = dot(lines[:, 0:256], tab["bx"][0:256, :])
        arrived(rui.at[t, c], u_recv.at[2 * t + 1, c])
        gather(2)
        gather(3)
        values = (summed[...] + dot(lines[:, 256:512], tab["bx"][256:512, :])).astype(BF).reshape(8, 64, 512)
        if t == 0:
            values = (values.astype(F32) * mask[...].astype(F32)).astype(BF)
        field[c] = values

    def y_forward(t, i):
        arrived(ra.at[t, i], a_recv.at[2 * t, i])
        sides = [ra[t, i, :, side].reshape(512, 128) for side in range(2)]
        sb[i] = dot(tab["ty"][...], jnp.concatenate(sides, axis=1)).astype(BF)
        send_b(sb, rb, 2 * t, t, i)

    def y_inverse(t, i):
        arrived(rbi.at[t, i], b_recv.at[2 * t + 1, i])
        out = dot(tab["tyi"][...], rbi[t, i]).astype(BF)
        for side in range(2):
            sai[i, :, side] = out[:, side * 128 : side * 128 + 128].reshape(2, 256, 128)
        send_ai(t, i)

    def z_forward(t, i):
        arrived(rb.at[t, i], b_recv.at[2 * t, i])
        for half in range(2):
            lanes = slice(half * 128, half * 128 + 128)

            def source(e_from, ri):
                return rb[t, i, e_from * 32 + ri * 16 : e_from * 32 + ri * 16 + 16, lanes].astype(F32)

            for low in range(4):
                out = radix4([(source(low + 4 * j, 0), source(low + 4 * j, 1)) for j in range(4)], 1)
                for k, value in enumerate(out):
                    mid[low, k, 0, :, lanes], mid[low, k, 1, :, lanes] = turned_by(value, low * k, 1)
            for k in range(4):
                out = radix4([(mid[low, k, 0, :, lanes], mid[low, k, 1, :, lanes]) for low in range(4)], 1)
                for high, (re, im) in enumerate(out):
                    k1 = k + 4 * high
                    wc, ws = tab["tw"][0, k1 : k1 + 1, lanes], tab["tw"][1, k1 : k1 + 1, lanes]
                    big[k1 * 16 : k1 * 16 + 16, lanes] = (re * wc + im * ws).astype(BF)
                    big[256 + k1 * 16 : 256 + k1 * 16 + 16, lanes] = (im * wc - re * ws).astype(BF)
        both = dot(big[...], tab["cs"][...])
        spec[i, 0] = both[:256, :256] + both[256:, 256:]
        spec[i, 1] = both[256:, :256] - both[:256, 256:]

    def z_inverse(source, t, i):
        both = dot(source[i].reshape(512, 256), tab["csi"][...])
        for half in range(2):
            lanes = slice(half * 128, half * 128 + 128)
            other = slice(256 + half * 128, 256 + half * 128 + 128)

            def value(k1):
                upper, lower = slice(k1 * 16, k1 * 16 + 16), slice(256 + k1 * 16, 256 + k1 * 16 + 16)
                re = both[upper, lanes] - both[lower, other]
                im = both[lower, lanes] + both[upper, other]
                wc, ws = tab["tw"][0, k1 : k1 + 1, lanes], tab["tw"][1, k1 : k1 + 1, lanes]
                return re * wc - im * ws, im * wc + re * ws

            for low in range(4):
                out = radix4([value(low + 4 * j) for j in range(4)], -1)
                for k, turned in enumerate(out):
                    mid[low, k, 0, :, lanes], mid[low, k, 1, :, lanes] = turned_by(turned, low * k, -1)
            for k in range(4):
                out = radix4([(mid[low, k, 0, :, lanes], mid[low, k, 1, :, lanes]) for low in range(4)], -1)
                for high, (re, im) in enumerate(out):
                    to = (k + 4 * high) * 32
                    sbi[i, to : to + 16, lanes] = re.astype(BF)
                    sbi[i, to + 16 : to + 32, lanes] = im.astype(BF)
        send_b(sbi, rbi, 2 * t + 1, t, i)

    def v_forward(t, c):
        arrived(ru.at[t, c], u_recv.at[2 * t, c])

        def some(n, carry):
            rows = pl.ds(pl.multiple_of(n * 16, 16), 16)
            out = packed_dft16([ru[t, c, j, rows].astype(F32) for j in range(16)], 1)
            for k1, value in enumerate(out):
                wc, ws = tab["utw"][0, k1 : k1 + 1], tab["utw"][1, k1 : k1 + 1]
                sv[c, k1, rows] = (value * wc + times_minus_i(value) * ws).astype(BF)
            return carry

        lax.fori_loop(0, 4, some, 0)
        send_v(t, c)

    def v_inverse(t, c):
        arrived(rvi.at[t, c], v_recv.at[2 * t + 1, c])

        def some(n, carry):
            rows = pl.ds(pl.multiple_of(n * 16, 16), 16)
            values = []
            for k1 in range(16):
                value = rvi[t, c, k1, rows].astype(F32)
                wc, ws = tab["utw"][0, k1 : k1 + 1], tab["utw"][1, k1 : k1 + 1]
                values.append(value * wc - times_minus_i(value) * ws)
            for j, value in enumerate(packed_dft16(values, -1)):
                sui[c, j, rows] = value.astype(BF)
            return carry

        lax.fori_loop(0, 4, some, 0)
        send_u(sui, rui, 2 * t + 1, t, c)

    def y_product(table, values, wide):
        for half in range(2):
            lanes = slice(half * 128, half * 128 + 128)
            stacked[256:512, lanes] = times_minus_i(wide[:, lanes]).astype(BF)
        stacked[0:256, :] = values
        return dot(table, stacked[...]).astype(BF)

    def first_faces(t):
        for q in range(4):
            send_z(0, near if t else far, q)
        send_y(0, t)

    def w_forward(t, c, last=False):
        arrived(rv.at[t, c], v_recv.at[2 * t, c])
        if last:
            first_faces(t)
        for k1 in range(2):
            values = jnp.concatenate([rv[t, c, k1, 0], rv[t, c, k1, 1]], axis=1)
            big1[k1 * 256 : k1 * 256 + 256, :] = y_product(tab["uy"][...], values, values.astype(F32))
        spec1[c] = dot(big1[...], tab["uz"][...])

    def w_inverse(source, t, c):
        wide = dot(source[c], tab["uzi"][...])
        for k1 in range(2):
            part = wide[k1 * 256 : k1 * 256 + 256]
            out = y_product(tab["uyi"][...], part.astype(BF), part)
            for side in range(2):
                svi[c, k1, side] = out[:, side * 128 : side * 128 + 128]
        send_vi(t, c)

    lane = lax.broadcasted_iota(jnp.int32, (16, 256), 1)
    unit_long, unit = np.float32(TWO_PI / 512), np.float32(TWO_PI / 256)
    index_y = e * 16 + lax.broadcasted_iota(jnp.int32, (16, 256), 0)
    wave_y = jnp.where(index_y < 128, index_y, index_y - 256).astype(F32) * unit

    wave_x = (d * 32 + (lane & 15)).astype(F32) * unit_long
    wave_x1 = ((e // 2) * 32 + 16 + (e & 1) * 8 + (lane & 7)).astype(F32) * unit_long

    def along_z(k1):
        index_z = k1 + 16 * (lane // 16)
        return index_z, jnp.where(index_z < 128, index_z, index_z - 256).astype(F32) * unit

    def at_rows(n):
        return pl.ds(pl.multiple_of(n * 16, 16), 16)

    def along_y1(n):
        index = (n & 15) * 16 + lax.broadcasted_iota(jnp.int32, (16, 256), 0)
        return index, jnp.where(index < 128, index, index - 256).astype(F32) * unit

    def scales(kx, ky, kz, edge):
        ksq = kx * kx + ky * ky + kz * kz
        return (
            jnp.where(edge, 0.0, 1.0 / (0.05 * ksq + 0.5)),
            jnp.where(ksq > 0.0, 1.0 / jnp.where(ksq > 0.0, ksq, 1.0), 0.0),
        )

    def factors(n, carry):
        index_z, wave_z = along_z(n)
        gain[at_rows(n)], inv[at_rows(n)] = scales(wave_x, wave_y, wave_z, (index_y == 128) | (index_z == 128))
        return carry

    def factors1(n, carry):
        index_z, wave_z = along_z(2 * d + n // 16)
        index, wave = along_y1(n)
        gain1[at_rows(n)], inv1[at_rows(n)] = scales(wave_x1, wave, wave_z, (index == 128) | (index_z == 128))
        return carry

    def parts():
        def one(n, carry):
            rows = at_rows(n)
            for ri in range(2):
                dots[ri, rows] = wave_x * spec[0, ri, rows] + wave_y * spec[1, ri, rows]
            return carry

        lax.fori_loop(0, 16, one, 0)

    def keep(t, kept, result, at, value):
        if t == 0:
            kept[at] = value.astype(BF)
        else:
            result[at] = (kept[at].astype(F32) - value).astype(BF)

    def project_x(t):
        def one(n, carry):
            rows = at_rows(n)
            wave_z = along_z(n)[1]
            for ri in range(2):
                along = (dots[ri, rows] + wave_z * spec[2, ri, rows]) * inv[rows]
                dots[ri, rows] = along
                keep(t, first, second, (0, ri, rows), gain[rows] * (spec[0, ri, rows] - wave_x * along))
            return carry

        lax.fori_loop(0, 16, one, 0)

    def project_yz(t):
        def one(n, carry):
            rows = at_rows(n)
            waves = (wave_x, wave_y, along_z(n)[1])
            for ri in range(2):
                along = dots[ri, rows]
                for c in (1, 2):
                    keep(t, first, second, (c, ri, rows), gain[rows] * (spec[c, ri, rows] - waves[c] * along))
            return carry

        lax.fori_loop(0, 16, one, 0)

    def parts1():
        def one(n, carry):
            rows = at_rows(n)
            dots1[rows] = wave_x1 * spec1[0, rows] + along_y1(n)[1] * spec1[1, rows]
            return carry

        lax.fori_loop(0, 32, one, 0)

    def project1_x(t):
        def one(n, carry):
            rows = at_rows(n)
            along = (dots1[rows] + along_z(2 * d + n // 16)[1] * spec1[2, rows]) * inv1[rows]
            dots1[rows] = along
            keep(t, first1, second1, (0, rows), gain1[rows] * (spec1[0, rows] - wave_x1 * along))
            return carry

        lax.fori_loop(0, 32, one, 0)

    def project1_yz(t):
        def one(n, carry):
            rows = at_rows(n)
            waves = (wave_x1, along_y1(n)[1], along_z(2 * d + n // 16)[1])
            along = dots1[rows]
            for c in (1, 2):
                keep(t, first1, second1, (c, rows), gain1[rows] * (spec1[c, rows] - waves[c] * along))
            return carry

        lax.fori_loop(0, 32, one, 0)

    def each(count, step):
        def body(i, _):
            step(i)
            return _

        lax.fori_loop(0, count, body, 0)

    def spectral(t, source, source1):
        def out(c):
            y_forward(t, c)
            v_forward(t, c)

        def inner(c):
            w_forward(t, c)
            z_forward(t, c)

        def outer(c):
            w_inverse(source1, t, c + 1)
            z_inverse(source, t, c + 1)

        def back(c):
            v_inverse(t, c)
            y_inverse(t, c)

        each(3, out)
        each(2, inner)
        parts1()
        parts()
        w_forward(t, 2, True)
        project1_x(t)
        w_inverse(source1, t, 0)
        z_forward(t, 2)
        project_x(t)
        z_inverse(source, t, 0)
        project1_yz(t)
        project_yz(t)
        each(2, outer)
        each(3, back)

    def start(c):
        @pl.when(c > 0)
        def _():
            arrived(field.at[c], in_sem.at[c])

        x_forward(0, c)
        x_forward1(0, c)

    arrived(tab["fx"], tab_sem.at[0])
    arrived(field.at[0], in_sem.at[0])
    load_rest()
    each(3, start)
    lax.fori_loop(0, 16, factors, 0)
    lax.fori_loop(0, 32, factors1, 0)
    loads["scalar"].wait()
    for z in range(8):
        state[0, z + 1, pl.ds(8, 64), :] = scalar[z].astype(F32)
    zsend[0, 0] = scalar[0]
    zsend[0, 1] = scalar[7]
    for side in range(2):
        for z in range(8):
            edge[pl.ds(z, 1), :] = state[0, z + 1, pl.ds(8 + 63 * side, 1), :]
        pack_edge(0, side)
    for name in TABLES[1:]:
        loads[name].wait()
    loads["mask"].wait()
    spectral(0, first, first1)

    def sent(t, c):
        for k in (2 * t, 2 * t + 1):
            sent_a(k, c)
            sent_b(k, c)
            sent_u(k, c)
            sent_v(k, c)

    def middle(c):
        x_inverse(0, c)
        sent(0, c)
        x_forward(1, c)
        x_forward1(1, c)

    each(3, middle)
    spectral(1, second, second1)

    def coefficients(z, c):
        fluid = 0.25 * (1.0 - mask[z].astype(F32))
        u = field[c, z].astype(F32)
        below = fluid * (0.25 + jnp.maximum(u, 0.0))
        above = fluid * (0.25 - jnp.minimum(u, 0.0))
        coef[2 * c, z] = below
        coef[2 * c + 1, z] = above
        start = jnp.where(c == 0, jnp.ones_like(u), coef[6, z])
        coef[6, z] = start - (below + above)
        return c

    def last(c):
        x_inverse(1, c)
        pltpu.make_async_copy(field.at[c], velocity_h.at[c], out_sem.at[c]).start()

        @pl.when(c < 2)
        def _():
            lax.fori_loop(0, 8, coefficients, c)

    each(3, last)

    def block(s, z, q):
        now, later = s & 1, (s + 1) & 1
        at = 8 + 16 * q
        rows, cells = pl.ds(at, 16), pl.ds(16 * q, 16)
        center = state[now, z, rows]
        new = coef[6, z - 1, cells] * center
        new = new + coef[0, z - 1, cells] * pltpu.roll(center, 1, 1)
        new = new + coef[1, z - 1, cells] * pltpu.roll(center, 511, 1)
        new = new + coef[2, z - 1, cells] * state[now, z, pl.ds(at - 1, 16)]
        new = new + coef[3, z - 1, cells] * state[now, z, pl.ds(at + 1, 16)]
        new = new + coef[4, z - 1, cells] * state[now, z - 1, rows]
        new = new + coef[5, z - 1, cells] * state[now, z + 1, rows]
        state[later, z, rows] = new
        return new

    def outer_block(s, side, q):
        cells = pl.ds(16 * q, 16)
        arrived(zrecv.at[s, side, cells], z_rsem.at[s, side, q])
        state[s & 1, 9 * side, pl.ds(8 + 16 * q, 16)] = zrecv[s, side, cells].astype(F32)
        face = block(s, 1 + 7 * side, q)

        @pl.when(s < SECTIONS - 1)
        def _():
            zsend[s + 1, side, cells] = face.astype(BF)
            send_z(s + 1, side, q)

    def y_halo(s):
        for side in range(2):
            arrived(yrecv.at[s, side], y_rsem.at[s, side])
            halo = yrecv[s, side].astype(F32)
            for z in range(8):
                for half in range(2):
                    lanes = slice(half * 256, half * 256 + 256)
                    state[s & 1, z + 1, pl.ds(7 + 65 * side, 1), lanes] = halo[8 * half + z : 8 * half + z + 1]

    def store_planes(z, count):
        planes = pl.ds(z, count)
        return pltpu.make_async_copy(conc.at[planes], conc_h.at[planes], out_sem.at[3 + (0, 1, 0, 0, 0, 0, 0, 2)[z]])

    def section(s, carry):
        @pl.when(s == SECTIONS - 1)
        def _():
            y_halo(s)

        for q in (0, 3, 1, 2):
            outer_block(s, near, q)
            for z in range(2, 8):
                block(s, z, q)
            if q in (0, 3):
                side = q // 3

                @pl.when(s < SECTIONS - 1)
                def _():
                    for z in range(8):
                        edge[pl.ds(z, 1), :] = state[(s + 1) & 1, z + 1, pl.ds(8 + 63 * side, 1), :]
                    pack_edge(s + 1, side)
                    send_y(s + 1, side)

        @pl.when(s == SECTIONS - 1)
        def _():
            conc[pl.ds(1, 6)] = state[SECTIONS % 2, pl.ds(2, 6), pl.ds(8, 64), :].astype(BF)
            store_planes(1, 6).start()

        following = jnp.minimum(s + 1, SECTIONS - 1)

        @pl.when(s != SECTIONS - 2)
        def _():
            for q in (1, 2):
                outer_block(following, far, q)

        @pl.when(s < SECTIONS - 2)
        def _():
            y_halo(s + 1)

        @pl.when(s != SECTIONS - 2)
        def _():
            for q in (0, 3):
                outer_block(following, far, q)

        return carry

    y_halo(0)
    coefficients(7 * far, 2)
    for q in (1, 2, 0, 3):
        outer_block(0, far, q)
    lax.fori_loop(0, 7, lambda n, carry: coefficients(n + near, carry), 2)
    lax.fori_loop(0, SECTIONS, section, 0)
    for z in (0, 7):
        conc[z] = state[SECTIONS % 2, z + 1, pl.ds(8, 64), :].astype(BF)
        store_planes(z, 1).start()

    each(3, lambda c: sent(1, c))
    for s in range(SECTIONS):
        for i in range(2):
            arrived(zsend.at[s, i], z_ssem.at[s, i])
            arrived(ysend.at[s, i], y_ssem.at[s, i])
    for c in range(3):
        pltpu.make_async_copy(field.at[c], velocity_h.at[c], out_sem.at[c]).wait()
    for z, count in ((0, 1), (1, 6), (7, 1)):
        store_planes(z, count).wait()


def place_kernel(velocity_in, conc_in, velocity, conc, held, in_sem, out_sem):
    pairs = []
    for half in range(2):
        planes = pl.ds(4 * half, 4)
        pairs += [(velocity_in.at[c, planes], held.at[c, planes], velocity.at[c, planes]) for c in range(3)]
        pairs.append((conc_in.at[planes], held.at[3, planes], conc.at[planes]))
    loads = [pltpu.make_async_copy(a, b, in_sem.at[i]) for i, (a, b, _) in enumerate(pairs)]
    stores = [pltpu.make_async_copy(b, c, out_sem.at[i]) for i, (_, b, c) in enumerate(pairs)]
    for copy in loads:
        copy.start()
    for load, store in zip(loads, stores):
        load.wait()
        store.start()
    for copy in stores:
        copy.wait()


def local(force, mask, scalar):
    tables = numpy_tables()
    vm = pltpu.VMEM
    dma = pltpu.SemaphoreType.DMA
    scratch = [vm((3, 8, 64, 512), BF), vm((8, 64, 512), jnp.int32), vm((8, 64, 512), BF)]
    for name in TABLES:
        value = tables[name]
        shape = value.shape[1:] if name in VARIED else value.shape
        scratch.append(vm(shape, value.dtype))
    scratch += [
        vm((256, 256), F32), vm((256, 256), F32),
        vm((3, 8, 2, 64, 128), BF), vm((2, 3, 2, 2, 256, 128), BF),
        vm((3, 512, 256), BF), vm((2, 3, 512, 256), BF),
        vm((3, 512, 256), BF), vm((2, 3, 512, 256), BF),
        vm((3, 2, 2, 256, 128), BF), vm((2, 3, 8, 2, 64, 128), BF),
        vm((3, 2, 256, 256), F32), vm((3, 2, 256, 256), BF), vm((3, 2, 256, 256), BF),
        vm((512, 512), BF), vm((512, 256), BF), vm((4, 4, 2, 16, 256), F32),
        vm((512, 256), F32), vm((512, 256), F32),
        vm((3, 16, 64, 128), BF), vm((2, 3, 16, 64, 128), BF),
        vm((3, 16, 64, 128), BF), vm((2, 3, 2, 2, 256, 128), BF),
        vm((3, 2, 2, 256, 128), BF), vm((2, 3, 16, 64, 128), BF),
        vm((3, 16, 64, 128), BF), vm((2, 3, 16, 64, 128), BF),
        vm((3, 512, 256), F32), vm((3, 512, 256), BF), vm((3, 512, 256), BF),
        vm((512, 256), BF), vm((2, 256, 256), F32), vm((512, 256), F32),
        vm((512, 512), F32), vm((512, 256), BF),
        dma((4, 3)), dma((4, 3)), dma((4, 3)), dma((4, 3)),
        vm((SECTIONS, 2, 64, 512), BF), vm((SECTIONS, 2, 64, 512), BF),
        vm((SECTIONS, 2, 16, 256), BF), vm((SECTIONS, 2, 16, 256), BF), vm((8, 512), F32),
        vm((7, 8, 64, 512), F32), vm((2, 10, 80, 512), F32), vm((8, 64, 512), BF),
        dma((5,)), dma((len(TABLES),)),
        dma((4, 3)), dma((4, 3)), dma((4, 3)), dma((4, 3)),
        dma((SECTIONS, 2)), dma((SECTIONS, 2, 4)), dma((SECTIONS, 2)), dma((SECTIONS, 2)),
        dma((6,)),
    ]
    any_spec = pl.BlockSpec(memory_space=pl.ANY)
    velocity, conc = pl.pallas_call(
        mixer_kernel,
        out_shape=(
            jax.ShapeDtypeStruct((3, 8, 64, 512), BF),
            jax.ShapeDtypeStruct((8, 64, 512), BF),
        ),
        in_specs=[any_spec] * (3 + len(TABLES)),
        out_specs=(any_spec, any_spec),
        scratch_shapes=scratch,
        compiler_params=pltpu.CompilerParams(
            collective_id=0, has_side_effects=True, vmem_limit_bytes=62 * 1024 * 1024
        ),
        name="mixer",
    )(
        force,
        mask,
        scalar,
        *[jnp.asarray(tables[name]) for name in TABLES],
    )
    return pl.pallas_call(
        place_kernel,
        out_shape=(
            jax.ShapeDtypeStruct((3, 8, 64, 512), BF),
            jax.ShapeDtypeStruct((8, 64, 512), BF),
        ),
        in_specs=[any_spec] * 2,
        out_specs=(any_spec, any_spec),
        scratch_shapes=[vm((4, 8, 64, 512), BF), dma((8,)), dma((8,))],
        name="place",
    )(velocity, conc)


def solution(mesh):
    placed = (P(None, "col", "row", None), P("col", "row", None), P("col", "row", None))
    return jax.shard_map(
        local,
        mesh=mesh,
        in_specs=placed,
        out_specs=(P(None, "col", "row", None), P("col", "row", None)),
        check_vma=False,
    )
```

```python
import numpy as np
import jax
import jax.numpy as jnp
import ml_dtypes
from jax import lax
from jax.experimental import pallas as pl
from jax.experimental.pallas import tpu as pltpu
from jax.sharding import PartitionSpec as P

SECTIONS = 5
MESH = pl.DeviceIdType.MESH
BF = jnp.bfloat16
F32 = jnp.float32
TWO_PI = 2.0 * np.pi
PLANE_ORDER = (
    (2, 2), (2, 1), (1, 2), (2, 3), (3, 2), (2, 0), (0, 2), (1, 1), (3, 3), (1, 3), (3, 1),
    (1, 0), (3, 0), (0, 1), (0, 3),
)


def numpy_tables():
    def half(values):
        return values.astype(np.float32).astype(ml_dtypes.bfloat16)

    x = np.arange(512)
    ri, d, k = (v.reshape(-1) for v in np.meshgrid(np.arange(2), np.arange(8), np.arange(16), indexing="ij"))
    e1, ri1, k1 = (v.reshape(-1) for v in np.meshgrid(np.arange(16), np.arange(2), np.arange(8), indexing="ij"))
    m = np.concatenate([d * 32 + k, (e1 // 2) * 32 + 16 + (e1 % 2) * 8 + k1])
    ri = np.concatenate([ri, ri1])
    angle = (np.outer(x, m) % 512) * (TWO_PI / 512)
    fx = np.where(ri == 0, np.cos(angle), -np.sin(angle)) / np.sqrt(512.0)
    bx = (fx * np.where(m == 0, 1.0, 2.0)).T
    y = np.arange(256)
    angle = (np.outer(y, y) % 256) * (TWO_PI / 256)
    c, s = np.cos(angle) / 16.0, np.sin(angle) / 16.0
    real = np.concatenate([c, s], 1).reshape(16, 1, 16, 512)
    imag = np.concatenate([-s, c], 1).reshape(16, 1, 16, 512)
    ty = np.concatenate([real, imag], 1).reshape(512, 512)
    uy = np.concatenate([c, s], 1)
    uyi = np.concatenate([c, -s], 1)
    n = np.arange(16)
    angle = (np.outer(n, n) % 16) * (TWO_PI / 16)
    c, s = np.cos(angle) / 4.0, np.sin(angle) / 4.0
    cs = np.zeros((8, 256, 512))
    csi = np.zeros((8, 256, 512))
    tw = np.zeros((8, 2, 16, 256))
    k = np.arange(16)
    for d in range(8):
        for low in range(2):
            for p in range(8):
                zp = low * 8 + (p - d) % 8
                at = low * 128 + p * 16
                for k2 in range(16):
                    cs[d, at + k, k2 * 16 + k] = c[zp, k2]
                    cs[d, at + k, 256 + k2 * 16 + k] = s[zp, k2]
                    csi[d, k2 * 16 + k, at + k] = c[zp, k2]
                    csi[d, k2 * 16 + k, 256 + at + k] = s[zp, k2]
                tw[d, 0, :, at : at + 16] = np.cos(TWO_PI * zp * n / 256)[:, None] / 4.0
                tw[d, 1, :, at : at + 16] = np.sin(TWO_PI * zp * n / 256)[:, None] / 4.0
    utw = np.zeros((16, 2, 16, 128))
    uz = np.zeros((8, 256, 256))
    k = np.arange(8)
    for turn in range(8):
        for low in range(2):
            for p in range(8):
                zp = low * 8 + (p - turn) % 8
                utw[low * 8 + turn, 0, :, p * 16 : p * 16 + 16] = np.cos(TWO_PI * zp * n / 256)[:, None] / 4.0
                utw[low * 8 + turn, 1, :, p * 16 : p * 16 + 16] = np.sin(TWO_PI * zp * n / 256)[:, None] / 4.0
                at = low * 128 + p * 16
                for k2 in range(16):
                    to = k2 * 16
                    uz[turn, at + k, to + k] = c[zp, k2]
                    uz[turn, at + 8 + k, to + k] = s[zp, k2]
                    uz[turn, at + k, to + 8 + k] = -s[zp, k2]
                    uz[turn, at + 8 + k, to + 8 + k] = c[zp, k2]
    return dict(
        uy=half(uy), uyi=half(uyi), uz=half(uz), uzi=half(uz.transpose(0, 2, 1)), utw=utw.astype(np.float32),
        fx=half(fx), bx=half(bx), ty=half(ty), tyi=half(ty.T), cs=half(cs), csi=half(csi),
        tw=tw.astype(np.float32),
    )


TABLES = ("fx", "ty", "utw", "tw", "cs", "uy", "uz", "csi", "uzi", "tyi", "uyi", "bx")
BY_D = ("cs", "tw", "csi")
BY_E = ("uz", "uzi")
VARIED = BY_D + BY_E + ("utw",)


def radix4(a, sign):
    def add(u, v):
        return u[0] + v[0], u[1] + v[1]

    def sub(u, v):
        return u[0] - v[0], u[1] - v[1]

    t0, t1 = add(a[0], a[2]), sub(a[0], a[2])
    t2, t3 = add(a[1], a[3]), sub(a[1], a[3])
    t3 = (t3[1], -t3[0]) if sign > 0 else (-t3[1], t3[0])
    return add(t0, t2), add(t1, t3), sub(t0, t2), sub(t1, t3)


def turned_by(value, j, sign):
    if j == 0:
        return value
    c, s = float(np.cos(TWO_PI * j / 16)), float(np.sin(TWO_PI * j / 16)) * sign
    re, im = value
    return re * c + im * s, im * c - re * s


def times_minus_i(value):
    imag = (lax.broadcasted_iota(jnp.int32, value.shape, 1) & 8) != 0
    return jnp.where(imag, -pltpu.roll(value, 8, 1), pltpu.roll(value, 120, 1))


def packed_radix4(a, sign):
    t0, t1, t2 = a[0] + a[2], a[0] - a[2], a[1] + a[3]
    t3 = times_minus_i(a[1] - a[3])
    if sign < 0:
        t3 = -t3
    return t0 + t2, t1 + t3, t0 - t2, t1 - t3


def packed_turned(value, j, sign):
    if j == 0:
        return value
    c, s = float(np.cos(TWO_PI * j / 16)), float(np.sin(TWO_PI * j / 16)) * sign
    return value * c + times_minus_i(value) * s


def packed_dft16(values, sign):
    parts = [packed_radix4(values[low::4], sign) for low in range(4)]
    parts = [[packed_turned(v, low * k, sign) for k, v in enumerate(parts[low])] for low in range(4)]
    out = [None] * 16
    for k in range(4):
        out[k::4] = packed_radix4([parts[low][k] for low in range(4)], sign)
    return out


def merge(tiles, place):
    for bit in (1, 2, 4):
        take = (place & bit) != 0
        tiles = [jnp.where(take, tiles[(m + bit) % 8], tiles[m]) for m in range(8)]
    return tiles


def dot(a, b):
    return jnp.dot(a, b, preferred_element_type=F32)


def mixer_kernel(*refs):
    force_h, mask_h, scalar_h = refs[:3]
    count = len(TABLES)
    tables_h = dict(zip(TABLES, refs[3 : 3 + count]))
    velocity_h, conc_h = refs[3 + count : 5 + count]
    (field, mask, scalar, *rest) = refs[5 + count :]
    tab = dict(zip(TABLES, rest[:count]))
    (gain, inv, sa, ra, sb, rb, sbi, rbi, sai, rai, spec, first, second, lines, big, mid,
     gain1, inv1, su, ru, sv, rv, svi, rvi, sui, rui, spec1, first1, second1, stacked, dots, dots1, summed, big1,
     u_send, u_recv, v_send, v_recv,
     zsend, zrecv, ysend, yrecv, edge, coef, state, conc,
     in_sem, tab_sem, a_send, a_recv, b_send, b_recv, z_ssem, z_rsem, y_ssem, y_rsem, out_sem) = rest[count:]

    r = lax.axis_index("row")
    col = lax.axis_index("col")
    e = col // 2
    xl = col % 2
    d = xl * 4 + r

    def load(source, target, sem):
        copy = pltpu.make_async_copy(source, target, sem)
        copy.start()
        return copy

    def load_table(name):
        source = tables_h[name]
        sem = tab_sem.at[TABLES.index(name)]
        if name in VARIED:
            source = source.at[d if name in BY_D else (e & 7) + (8 * xl if name == "utw" else 0)]
        return load(source, tab[name], sem)

    for i in range(4):
        planes, rows = pl.ds(2 * i, 2), pl.ds(128 * i, 128)
        load(force_h.at[0, planes], field.at[0, planes], in_sem.at[0])
        load(tables_h["fx"].at[rows], tab["fx"].at[rows], tab_sem.at[0])
    loads = {}

    def load_rest():
        for i in (1, 2):
            loads[i] = load(force_h.at[i], field.at[i], in_sem.at[i])
        for name in TABLES[1:]:
            loads[name] = load_table(name)
        loads["scalar"] = load(scalar_h, scalar, in_sem.at[4])
        loads["mask"] = load(mask_h, mask, in_sem.at[3])

    core = r & 1
    x = (r // 2) * 2 + xl
    y_at, z_at = e // 4, e & 3

    def x_peer(step, of_core):
        at = (x + step * (1 + 2 * core)) & 3
        low = at & 1
        row = (at - low) + of_core
        return low * 4 + row, (row, e * 2 + low)

    def plane_peer(dy, dz):
        to = ((y_at + dy + core * (3 * dz - dy)) & 3) * 4 + ((z_at + dz + core * (3 * dy - dz)) & 3)
        return to, (r, to * 2 + xl)

    x_peers = [
        x_peer(step, core if same else 1 - core)
        for step, same in ((2, 1), (2, 0), (1, 1), (3, 1), (1, 0), (3, 0), (0, 0))
    ]
    plane_peers = [plane_peer(dy, dz) for dy, dz in PLANE_ORDER]

    y_up = (lax.rem(r + 1, 4), col)
    y_down = (lax.rem(r + 3, 4), col)

    barrier = pltpu.get_barrier_semaphore()

    for _, device in x_peers + plane_peers:
        pl.semaphore_signal(barrier, inc=1, device_id=device, device_id_type=MESH)
    across = (r, lax.rem(col + 31 + 2 * xl, 32))
    pl.semaphore_signal(barrier, inc=1, device_id=across, device_id_type=MESH)
    pl.semaphore_wait(barrier, 23)

    def remote(source, target, ssem, rsem, device):
        return pltpu.make_async_remote_copy(
            src_ref=source, dst_ref=target, send_sem=ssem, recv_sem=rsem,
            device_id=device, device_id_type=MESH)

    my_rows = pl.ds(pl.multiple_of(r * 64, 64), 64)
    my_slab = pl.ds(pl.multiple_of(e * 32, 32), 32)

    def send_a(t, i):
        target = ra.at[t, i, :, xl, my_rows]
        recv = a_recv.at[2 * t, i]

        for to, device in x_peers:
            remote(sa.at[i, to], target, a_send.at[2 * t, i], recv, device).start()
        pltpu.make_async_copy(sa.at[i, d], target, recv).start()

    def send_ai(t, i):
        target = rai.at[t, i, d]
        recv = a_recv.at[2 * t + 1, i]

        def piece(to):
            rows = pl.ds(pl.multiple_of((to & 3) * 64, 64), 64)
            return sai.at[i, :, to // 4, rows]

        for to, device in x_peers:
            remote(piece(to), target, a_send.at[2 * t + 1, i], recv, device).start()
        pltpu.make_async_copy(piece(d), target, recv).start()

    def send_b(source, into, k, t, i):
        target = into.at[t, i, my_slab]
        recv = b_recv.at[k, i]

        for to, device in plane_peers:
            slab = source.at[i, pl.ds(pl.multiple_of(to * 32, 32), 32)]
            remote(slab, target, b_send.at[k, i], recv, device).start()
        pltpu.make_async_copy(source.at[i, my_slab], target, recv).start()

    def send_u(source, into, k, t, c):
        target = into.at[t, c, e]
        recv = u_recv.at[k, c]
        for to, device in plane_peers:
            remote(source.at[c, to], target, u_send.at[k, c], recv, device).start()
        pltpu.make_async_copy(source.at[c, e], target, recv).start()

    def send_v(t, c):
        target = rv.at[t, c, :, xl, my_rows]
        recv = v_recv.at[2 * t, c]
        for to, device in x_peers:
            remote(sv.at[c, pl.ds(2 * to, 2)], target, v_send.at[2 * t, c], recv, device).start()
        pltpu.make_async_copy(sv.at[c, pl.ds(2 * d, 2)], target, recv).start()

    def send_vi(t, c):
        target = rvi.at[t, c, pl.ds(2 * d, 2)]
        recv = v_recv.at[2 * t + 1, c]

        def piece(to):
            rows = pl.ds(pl.multiple_of((to & 3) * 64, 64), 64)
            return svi.at[c, :, to // 4, rows]

        for to, device in x_peers:
            remote(piece(to), target, v_send.at[2 * t + 1, c], recv, device).start()
        pltpu.make_async_copy(piece(d), target, recv).start()

    def arrived(buffer, sem):
        pltpu.make_async_copy(buffer, buffer, sem).wait()

    def sent_a(k, i):
        arrived(sa.at[i, pl.ds(0, 7)], a_send.at[k, i])

    def sent_b(k, i):
        arrived(sb.at[i, pl.ds(0, 480)], b_send.at[k, i])

    def sent_u(k, i):
        arrived(su.at[i, pl.ds(0, 15)], u_send.at[k, i])

    def sent_v(k, i):
        arrived(sv.at[i, pl.ds(0, 14)], v_send.at[k, i])

    near, far = 1 - xl, xl

    def send_z(s, side, q):
        rows = pl.ds(16 * q, 16)
        remote(zsend.at[s, side, rows], zrecv.at[s, 1 - side, rows], z_ssem.at[s, side],
               z_rsem.at[s, 1 - side, q], (r, (col + 2 * side + 31) & 31)).start()

    def pack_edge(s, side):
        value = edge[...]
        ysend[s, side] = jnp.concatenate([value[:, 0:256], value[:, 256:512]], axis=0).astype(BF)

    def send_y(s, side):
        remote(ysend.at[s, side], yrecv.at[s, 1 - side], y_ssem.at[s, side], y_rsem.at[s, 1 - side],
               (y_down, y_up)[side]).start()

    place = lax.broadcasted_iota(jnp.int32, (64, 128), 1) // 16

    def x_forward(t, c):
        spread = dot(field[c].reshape(512, 512), tab["fx"][:, 0:256])
        for ri in range(2):
            tiles = []
            for z in range(8):
                tile = spread[z * 64 : z * 64 + 64, ri * 128 : ri * 128 + 128]
                tiles.append(pltpu.roll(tile, 16 * z, 1) if z else tile)
            tiles = merge(tiles, place)
            for to in range(8):
                sa[c, to, ri] = tiles[-to % 8].astype(BF)
        send_a(t, c)

    def x_forward1(t, c):
        spread = dot(field[c].reshape(512, 512), tab["fx"][:, 256:512])
        for j in range(2):
            tiles = []
            for z in range(8):
                tile = spread[z * 64 : z * 64 + 64, j * 128 : j * 128 + 128]
                tiles.append(pltpu.roll(tile, 16 * z, 1) if z else tile)
            tiles = merge(tiles, place)
            for to in range(8):
                su[c, 8 * j + to] = tiles[-to % 8].astype(BF)
        send_u(su, ru, 2 * t, t, c)

    def x_inverse(t, c):
        def gather(j):
            if j < 2:
                tiles = [rai[t, c, source, j].astype(F32) for source in range(8)]
            else:
                tiles = [rui[t, c, 8 * (j - 2) + source].astype(F32) for source in range(8)]
            tiles = merge(tiles, place)
            for z in range(8):
                tile = tiles[-z % 8]
                tile = pltpu.roll(tile, 128 - 16 * z, 1) if z else tile
                lines[z * 64 : z * 64 + 64, j * 128 : j * 128 + 128] = tile.astype(BF)

        arrived(rai.at[t, c], a_recv.at[2 * t + 1, c])
        gather(0)
        gather(1)
        summed[...] = dot(lines[:, 0:256], tab["bx"][0:256, :])
        arrived(rui.at[t, c], u_recv.at[2 * t + 1, c])
        gather(2)
        gather(3)
        values = (summed[...] + dot(lines[:, 256:512], tab["bx"][256:512, :])).astype(BF).reshape(8, 64, 512)
        if t == 0:
            values = (values.astype(F32) * mask[...].astype(F32)).astype(BF)
        field[c] = values

    def y_forward(t, i):
        arrived(ra.at[t, i], a_recv.at[2 * t, i])
        sides = [ra[t, i, :, side].reshape(512, 128) for side in range(2)]
        sb[i] = dot(tab["ty"][...], jnp.concatenate(sides, axis=1)).astype(BF)
        send_b(sb, rb, 2 * t, t, i)

    def y_inverse(t, i):
        arrived(rbi.at[t, i], b_recv.at[2 * t + 1, i])
        out = dot(tab["tyi"][...], rbi[t, i]).astype(BF)
        for side in range(2):
            sai[i, :, side] = out[:, side * 128 : side * 128 + 128].reshape(2, 256, 128)
        send_ai(t, i)

    def z_forward(t, i):
        arrived(rb.at[t, i], b_recv.at[2 * t, i])
        for half in range(2):
            lanes = slice(half * 128, half * 128 + 128)

            def source(e_from, ri):
                return rb[t, i, e_from * 32 + ri * 16 : e_from * 32 + ri * 16 + 16, lanes].astype(F32)

            for low in range(4):
                out = radix4([(source(low + 4 * j, 0), source(low + 4 * j, 1)) for j in range(4)], 1)
                for k, value in enumerate(out):
                    mid[low, k, 0, :, lanes], mid[low, k, 1, :, lanes] = turned_by(value, low * k, 1)
            for k in range(4):
                out = radix4([(mid[low, k, 0, :, lanes], mid[low, k, 1, :, lanes]) for low in range(4)], 1)
                for high, (re, im) in enumerate(out):
                    k1 = k + 4 * high
                    wc, ws = tab["tw"][0, k1 : k1 + 1, lanes], tab["tw"][1, k1 : k1 + 1, lanes]
                    big[k1 * 16 : k1 * 16 + 16, lanes] = (re * wc + im * ws).astype(BF)
                    big[256 + k1 * 16 : 256 + k1 * 16 + 16, lanes] = (im * wc - re * ws).astype(BF)
        both = dot(big[...], tab["cs"][...])
        spec[i, 0] = both[:256, :256] + both[256:, 256:]
        spec[i, 1] = both[256:, :256] - both[:256, 256:]

    def z_inverse(source, t, i):
        both = dot(source[i].reshape(512, 256), tab["csi"][...])
        for half in range(2):
            lanes = slice(half * 128, half * 128 + 128)
            other = slice(256 + half * 128, 256 + half * 128 + 128)

            def value(k1):
                upper, lower = slice(k1 * 16, k1 * 16 + 16), slice(256 + k1 * 16, 256 + k1 * 16 + 16)
                re = both[upper, lanes] - both[lower, other]
                im = both[lower, lanes] + both[upper, other]
                wc, ws = tab["tw"][0, k1 : k1 + 1, lanes], tab["tw"][1, k1 : k1 + 1, lanes]
                return re * wc - im * ws, im * wc + re * ws

            for low in range(4):
                out = radix4([value(low + 4 * j) for j in range(4)], -1)
                for k, turned in enumerate(out):
                    mid[low, k, 0, :, lanes], mid[low, k, 1, :, lanes] = turned_by(turned, low * k, -1)
            for k in range(4):
                out = radix4([(mid[low, k, 0, :, lanes], mid[low, k, 1, :, lanes]) for low in range(4)], -1)
                for high, (re, im) in enumerate(out):
                    to = (k + 4 * high) * 32
                    sbi[i, to : to + 16, lanes] = re.astype(BF)
                    sbi[i, to + 16 : to + 32, lanes] = im.astype(BF)
        send_b(sbi, rbi, 2 * t + 1, t, i)

    def v_forward(t, c):
        arrived(ru.at[t, c], u_recv.at[2 * t, c])

        def some(n, carry):
            rows = pl.ds(pl.multiple_of(n * 16, 16), 16)
            out = packed_dft16([ru[t, c, j, rows].astype(F32) for j in range(16)], 1)
            for k1, value in enumerate(out):
                wc, ws = tab["utw"][0, k1 : k1 + 1], tab["utw"][1, k1 : k1 + 1]
                sv[c, k1, rows] = (value * wc + times_minus_i(value) * ws).astype(BF)
            return carry

        lax.fori_loop(0, 4, some, 0)
        send_v(t, c)

    def v_inverse(t, c):
        arrived(rvi.at[t, c], v_recv.at[2 * t + 1, c])

        def some(n, carry):
            rows = pl.ds(pl.multiple_of(n * 16, 16), 16)
            values = []
            for k1 in range(16):
                value = rvi[t, c, k1, rows].astype(F32)
                wc, ws = tab["utw"][0, k1 : k1 + 1], tab["utw"][1, k1 : k1 + 1]
                values.append(value * wc - times_minus_i(value) * ws)
            for j, value in enumerate(packed_dft16(values, -1)):
                sui[c, j, rows] = value.astype(BF)
            return carry

        lax.fori_loop(0, 4, some, 0)
        send_u(sui, rui, 2 * t + 1, t, c)

    def y_product(table, values, wide):
        for half in range(2):
            lanes = slice(half * 128, half * 128 + 128)
            stacked[256:512, lanes] = times_minus_i(wide[:, lanes]).astype(BF)
        stacked[0:256, :] = values
        return dot(table, stacked[...]).astype(BF)

    def first_faces(t):
        for q in range(4):
            send_z(0, near if t else far, q)
        send_y(0, t)

    def w_forward(t, c, last=False):
        arrived(rv.at[t, c], v_recv.at[2 * t, c])
        if last:
            first_faces(t)
        for k1 in range(2):
            values = jnp.concatenate([rv[t, c, k1, 0], rv[t, c, k1, 1]], axis=1)
            big1[k1 * 256 : k1 * 256 + 256, :] = y_product(tab["uy"][...], values, values.astype(F32))
        spec1[c] = dot(big1[...], tab["uz"][...])

    def w_inverse(source, t, c):
        wide = dot(source[c], tab["uzi"][...])
        for k1 in range(2):
            part = wide[k1 * 256 : k1 * 256 + 256]
            out = y_product(tab["uyi"][...], part.astype(BF), part)
            for side in range(2):
                svi[c, k1, side] = out[:, side * 128 : side * 128 + 128]
        send_vi(t, c)

    lane = lax.broadcasted_iota(jnp.int32, (16, 256), 1)
    unit_long, unit = np.float32(TWO_PI / 512), np.float32(TWO_PI / 256)
    index_y = e * 16 + lax.broadcasted_iota(jnp.int32, (16, 256), 0)
    wave_y = jnp.where(index_y < 128, index_y, index_y - 256).astype(F32) * unit

    wave_x = (d * 32 + (lane & 15)).astype(F32) * unit_long
    wave_x1 = ((e // 2) * 32 + 16 + (e & 1) * 8 + (lane & 7)).astype(F32) * unit_long

    def along_z(k1):
        index_z = k1 + 16 * (lane // 16)
        return index_z, jnp.where(index_z < 128, index_z, index_z - 256).astype(F32) * unit

    def at_rows(n):
        return pl.ds(pl.multiple_of(n * 16, 16), 16)

    def along_y1(n):
        index = (n & 15) * 16 + lax.broadcasted_iota(jnp.int32, (16, 256), 0)
        return index, jnp.where(index < 128, index, index - 256).astype(F32) * unit

    def scales(kx, ky, kz, edge):
        ksq = kx * kx + ky * ky + kz * kz
        return (
            jnp.where(edge, 0.0, 1.0 / (0.05 * ksq + 0.5)),
            jnp.where(ksq > 0.0, 1.0 / jnp.where(ksq > 0.0, ksq, 1.0), 0.0),
        )

    def factors(n, carry):
        index_z, wave_z = along_z(n)
        gain[at_rows(n)], inv[at_rows(n)] = scales(wave_x, wave_y, wave_z, (index_y == 128) | (index_z == 128))
        return carry

    def factors1(n, carry):
        index_z, wave_z = along_z(2 * d + n // 16)
        index, wave = along_y1(n)
        gain1[at_rows(n)], inv1[at_rows(n)] = scales(wave_x1, wave, wave_z, (index == 128) | (index_z == 128))
        return carry

    def parts():
        def one(n, carry):
            rows = at_rows(n)
            for ri in range(2):
                dots[ri, rows] = wave_x * spec[0, ri, rows] + wave_y * spec[1, ri, rows]
            return carry

        lax.fori_loop(0, 16, one, 0)

    def keep(t, kept, result, at, value):
        if t == 0:
            kept[at] = value.astype(BF)
        else:
            result[at] = (kept[at].astype(F32) - value).astype(BF)

    def project_x(t):
        def one(n, carry):
            rows = at_rows(n)
            wave_z = along_z(n)[1]
            for ri in range(2):
                along = (dots[ri, rows] + wave_z * spec[2, ri, rows]) * inv[rows]
                dots[ri, rows] = along
                keep(t, first, second, (0, ri, rows), gain[rows] * (spec[0, ri, rows] - wave_x * along))
            return carry

        lax.fori_loop(0, 16, one, 0)

    def project_yz(t):
        def one(n, carry):
            rows = at_rows(n)
            waves = (wave_x, wave_y, along_z(n)[1])
            for ri in range(2):
                along = dots[ri, rows]
                for c in (1, 2):
                    keep(t, first, second, (c, ri, rows), gain[rows] * (spec[c, ri, rows] - waves[c] * along))
            return carry

        lax.fori_loop(0, 16, one, 0)

    def parts1():
        def one(n, carry):
            rows = at_rows(n)
            dots1[rows] = wave_x1 * spec1[0, rows] + along_y1(n)[1] * spec1[1, rows]
            return carry

        lax.fori_loop(0, 32, one, 0)

    def project1_x(t):
        def one(n, carry):
            rows = at_rows(n)
            along = (dots1[rows] + along_z(2 * d + n // 16)[1] * spec1[2, rows]) * inv1[rows]
            dots1[rows] = along
            keep(t, first1, second1, (0, rows), gain1[rows] * (spec1[0, rows] - wave_x1 * along))
            return carry

        lax.fori_loop(0, 32, one, 0)

    def project1_yz(t):
        def one(n, carry):
            rows = at_rows(n)
            waves = (wave_x1, along_y1(n)[1], along_z(2 * d + n // 16)[1])
            along = dots1[rows]
            for c in (1, 2):
                keep(t, first1, second1, (c, rows), gain1[rows] * (spec1[c, rows] - waves[c] * along))
            return carry

        lax.fori_loop(0, 32, one, 0)

    def each(count, step):
        def body(i, _):
            step(i)
            return _

        lax.fori_loop(0, count, body, 0)

    def spectral(t, source, source1):
        def out(c):
            y_forward(t, c)
            v_forward(t, c)

        def inner(c):
            w_forward(t, c)
            z_forward(t, c)

        def outer(c):
            w_inverse(source1, t, c + 1)
            z_inverse(source, t, c + 1)

        def back(c):
            v_inverse(t, c)
            y_inverse(t, c)

        each(3, out)
        each(2, inner)
        parts1()
        parts()
        w_forward(t, 2, True)
        project1_x(t)
        w_inverse(source1, t, 0)
        z_forward(t, 2)
        project_x(t)
        z_inverse(source, t, 0)
        project1_yz(t)
        project_yz(t)
        each(2, outer)
        each(3, back)

    def start(c):
        @pl.when(c > 0)
        def _():
            arrived(field.at[c], in_sem.at[c])

        x_forward(0, c)
        x_forward1(0, c)

    arrived(tab["fx"], tab_sem.at[0])
    arrived(field.at[0], in_sem.at[0])
    load_rest()
    each(3, start)
    lax.fori_loop(0, 16, factors, 0)
    lax.fori_loop(0, 32, factors1, 0)
    loads["scalar"].wait()
    for z in range(8):
        state[0, z + 1, pl.ds(8, 64), :] = scalar[z].astype(F32)
    zsend[0, 0] = scalar[0]
    zsend[0, 1] = scalar[7]
    for side in range(2):
        for z in range(8):
            edge[pl.ds(z, 1), :] = state[0, z + 1, pl.ds(8 + 63 * side, 1), :]
        pack_edge(0, side)
    for name in TABLES[1:]:
        loads[name].wait()
    loads["mask"].wait()
    spectral(0, first, first1)

    def sent(t, c):
        for k in (2 * t, 2 * t + 1):
            sent_a(k, c)
            sent_b(k, c)
            sent_u(k, c)
            sent_v(k, c)

    def middle(c):
        x_inverse(0, c)
        sent(0, c)
        x_forward(1, c)
        x_forward1(1, c)

    each(3, middle)
    spectral(1, second, second1)

    def coefficients(z, c):
        fluid = 0.25 * (1.0 - mask[z].astype(F32))
        u = field[c, z].astype(F32)
        below = fluid * (0.25 + jnp.maximum(u, 0.0))
        above = fluid * (0.25 - jnp.minimum(u, 0.0))
        coef[2 * c, z] = below
        coef[2 * c + 1, z] = above
        start = jnp.where(c == 0, jnp.ones_like(u), coef[6, z])
        coef[6, z] = start - (below + above)
        return c

    def last(c):
        x_inverse(1, c)
        pltpu.make_async_copy(field.at[c], velocity_h.at[c], out_sem.at[c]).start()

        @pl.when(c < 2)
        def _():
            lax.fori_loop(0, 8, coefficients, c)

    each(3, last)

    def block(s, z, q):
        now, later = s & 1, (s + 1) & 1
        at = 8 + 16 * q
        rows, cells = pl.ds(at, 16), pl.ds(16 * q, 16)
        center = state[now, z, rows]
        new = coef[6, z - 1, cells] * center
        new = new + coef[0, z - 1, cells] * pltpu.roll(center, 1, 1)
        new = new + coef[1, z - 1, cells] * pltpu.roll(center, 511, 1)
        new = new + coef[2, z - 1, cells] * state[now, z, pl.ds(at - 1, 16)]
        new = new + coef[3, z - 1, cells] * state[now, z, pl.ds(at + 1, 16)]
        new = new + coef[4, z - 1, cells] * state[now, z - 1, rows]
        new = new + coef[5, z - 1, cells] * state[now, z + 1, rows]
        state[later, z, rows] = new
        return new

    def outer_block(s, side, q):
        cells = pl.ds(16 * q, 16)
        arrived(zrecv.at[s, side, cells], z_rsem.at[s, side, q])
        state[s & 1, 9 * side, pl.ds(8 + 16 * q, 16)] = zrecv[s, side, cells].astype(F32)
        face = block(s, 1 + 7 * side, q)

        @pl.when(s < SECTIONS - 1)
        def _():
            zsend[s + 1, side, cells] = face.astype(BF)
            send_z(s + 1, side, q)

    def y_halo(s):
        for side in range(2):
            arrived(yrecv.at[s, side], y_rsem.at[s, side])
            halo = yrecv[s, side].astype(F32)
            for half in range(2):
                lanes = slice(half * 256, half * 256 + 256)
                state[s & 1, 1:9, 7 + 65 * side, lanes] = halo[8 * half : 8 * half + 8]

    def store_planes(z, count):
        planes = pl.ds(z, count)
        return pltpu.make_async_copy(conc.at[planes], conc_h.at[planes], out_sem.at[3 + (0, 1, 0, 0, 0, 0, 0, 2)[z]])

    def section(s, carry):
        @pl.when(s == SECTIONS - 1)
        def _():
            y_halo(s)

        for q in (0, 3, 1, 2):
            outer_block(s, near, q)
            for z in range(2, 8):
                block(s, z, q)
            if q in (0, 3):
                side = q // 3

                @pl.when(s < SECTIONS - 1)
                def _():
                    edge[...] = state[(s + 1) & 1, 1:9, 8 + 63 * side, :]
                    pack_edge(s + 1, side)
                    send_y(s + 1, side)

        @pl.when(s == SECTIONS - 1)
        def _():
            conc[pl.ds(1, 6)] = state[SECTIONS % 2, pl.ds(2, 6), pl.ds(8, 64), :].astype(BF)
            store_planes(1, 6).start()

        following = jnp.minimum(s + 1, SECTIONS - 1)

        @pl.when(s != SECTIONS - 2)
        def _():
            for q in (1, 2):
                outer_block(following, far, q)

        @pl.when(s < SECTIONS - 2)
        def _():
            y_halo(s + 1)

        @pl.when(s != SECTIONS - 2)
        def _():
            for q in (0, 3):
                outer_block(following, far, q)

        return carry

    y_halo(0)
    coefficients(7 * far, 2)
    for q in (1, 2, 0, 3):
        outer_block(0, far, q)
    lax.fori_loop(0, 7, lambda n, carry: coefficients(n + near, carry), 2)
    lax.fori_loop(0, SECTIONS, section, 0)
    for z in (0, 7):
        conc[z] = state[SECTIONS % 2, z + 1, pl.ds(8, 64), :].astype(BF)
        store_planes(z, 1).start()

    each(3, lambda c: sent(1, c))
    for s in range(SECTIONS):
        for i in range(2):
            arrived(zsend.at[s, i], z_ssem.at[s, i])
            arrived(ysend.at[s, i], y_ssem.at[s, i])
    for c in range(3):
        pltpu.make_async_copy(field.at[c], velocity_h.at[c], out_sem.at[c]).wait()
    for z, count in ((0, 1), (1, 6), (7, 1)):
        store_planes(z, count).wait()


def place_kernel(velocity_in, conc_in, velocity, conc, held, in_sem, out_sem):
    pairs = []
    for half in range(2):
        planes = pl.ds(4 * half, 4)
        pairs += [(velocity_in.at[c, planes], held.at[c, planes], velocity.at[c, planes]) for c in range(3)]
        pairs.append((conc_in.at[planes], held.at[3, planes], conc.at[planes]))
    loads = [pltpu.make_async_copy(a, b, in_sem.at[i]) for i, (a, b, _) in enumerate(pairs)]
    stores = [pltpu.make_async_copy(b, c, out_sem.at[i]) for i, (_, b, c) in enumerate(pairs)]
    for copy in loads:
        copy.start()
    for load, store in zip(loads, stores):
        load.wait()
        store.start()
    for copy in stores:
        copy.wait()


def local(force, mask, scalar):
    tables = numpy_tables()
    vm = pltpu.VMEM
    dma = pltpu.SemaphoreType.DMA
    scratch = [vm((3, 8, 64, 512), BF), vm((8, 64, 512), jnp.int32), vm((8, 64, 512), BF)]
    for name in TABLES:
        value = tables[name]
        shape = value.shape[1:] if name in VARIED else value.shape
        scratch.append(vm(shape, value.dtype))
    scratch += [
        vm((256, 256), F32), vm((256, 256), F32),
        vm((3, 8, 2, 64, 128), BF), vm((2, 3, 2, 2, 256, 128), BF),
        vm((3, 512, 256), BF), vm((2, 3, 512, 256), BF),
        vm((3, 512, 256), BF), vm((2, 3, 512, 256), BF),
        vm((3, 2, 2, 256, 128), BF), vm((2, 3, 8, 2, 64, 128), BF),
        vm((3, 2, 256, 256), F32), vm((3, 2, 256, 256), BF), vm((3, 2, 256, 256), BF),
        vm((512, 512), BF), vm((512, 256), BF), vm((4, 4, 2, 16, 256), F32),
        vm((512, 256), F32), vm((512, 256), F32),
        vm((3, 16, 64, 128), BF), vm((2, 3, 16, 64, 128), BF),
        vm((3, 16, 64, 128), BF), vm((2, 3, 2, 2, 256, 128), BF),
        vm((3, 2, 2, 256, 128), BF), vm((2, 3, 16, 64, 128), BF),
        vm((3, 16, 64, 128), BF), vm((2, 3, 16, 64, 128), BF),
        vm((3, 512, 256), F32), vm((3, 512, 256), BF), vm((3, 512, 256), BF),
        vm((512, 256), BF), vm((2, 256, 256), F32), vm((512, 256), F32),
        vm((512, 512), F32), vm((512, 256), BF),
        dma((4, 3)), dma((4, 3)), dma((4, 3)), dma((4, 3)),
        vm((SECTIONS, 2, 64, 512), BF), vm((SECTIONS, 2, 64, 512), BF),
        vm((SECTIONS, 2, 16, 256), BF), vm((SECTIONS, 2, 16, 256), BF), vm((8, 512), F32),
        vm((7, 8, 64, 512), F32), vm((2, 10, 80, 512), F32), vm((8, 64, 512), BF),
        dma((5,)), dma((len(TABLES),)),
        dma((4, 3)), dma((4, 3)), dma((4, 3)), dma((4, 3)),
        dma((SECTIONS, 2)), dma((SECTIONS, 2, 4)), dma((SECTIONS, 2)), dma((SECTIONS, 2)),
        dma((6,)),
    ]
    any_spec = pl.BlockSpec(memory_space=pl.ANY)
    velocity, conc = pl.pallas_call(
        mixer_kernel,
        out_shape=(
            jax.ShapeDtypeStruct((3, 8, 64, 512), BF),
            jax.ShapeDtypeStruct((8, 64, 512), BF),
        ),
        in_specs=[any_spec] * (3 + len(TABLES)),
        out_specs=(any_spec, any_spec),
        scratch_shapes=scratch,
        compiler_params=pltpu.CompilerParams(
            collective_id=0, has_side_effects=True, vmem_limit_bytes=62 * 1024 * 1024
        ),
        name="mixer",
    )(
        force,
        mask,
        scalar,
        *[jnp.asarray(tables[name]) for name in TABLES],
    )
    return pl.pallas_call(
        place_kernel,
        out_shape=(
            jax.ShapeDtypeStruct((3, 8, 64, 512), BF),
            jax.ShapeDtypeStruct((8, 64, 512), BF),
        ),
        in_specs=[any_spec] * 2,
        out_specs=(any_spec, any_spec),
        scratch_shapes=[vm((4, 8, 64, 512), BF), dma((8,)), dma((8,))],
        name="place",
    )(velocity, conc)


def solution(mesh):
    placed = (P(None, "col", "row", None), P("col", "row", None), P("col", "row", None))
    return jax.shard_map(
        local,
        mesh=mesh,
        in_specs=placed,
        out_specs=(P(None, "col", "row", None), P("col", "row", None)),
        check_vma=False,
    )
```
